32 devices in a mesh: groups: 2 (over y), ang: 4 (over z), tm: 4 (over x, core).
Axes of the slice: x: 2, y: 2, z: 4, core: 2. Of those that a mesh axis runs over, the one named last changes fastest.
Arguments:
- field: bfloat16 [4, 256, 512, 512], P('groups', 'ang', None, 'tm'), parts along dimension 0, may hold values from -6 to 6
- radial_tables: bfloat16 [16, 8, 64, 64], replicated, may hold values from -0.75 to 0.75
- weights: float32 [512], replicated, may hold values from 0.3 to 3
- order_map: int32 [256], P('ang'), may hold values from 0 to 15
- curvature: float32 [256, 512], P('ang'), may hold values from 0.05 to 0.5
- walk_off: float32 [256, 512], P('ang'), may hold values from -0.5 to 0.5
Outputs:
- stepped: bfloat16 [4, 256, 512, 512], P('groups', 'ang', None, 'tm'), parts along dimension 0
The draws below stay inside these ranges and needn't reach their ends.
There are 2 independent parts, one for each index of `groups`. The reference program is written for one: setup_inputs(seed, part) draws one part's arguments, and reference() takes and returns one part's arrays. A program takes and returns all parts, laid end to end along the dimension named above; an argument that names none is the same for every part. Nothing has to cross between parts.
All inputs are finite; a program needn't handle non-finite values.
Results may differ from the reference program's by a relative error of at most 0.008.
Values may be sent and summed in bfloat16 or wider, within the bound.
No kernel may reach another device: no remote copies, remote signals or barrier semaphores. Data moves between devices by JAX's collectives and lax.ppermute only.
A program may use at most 448 MiB of HBM per device.

```python
import math
import jax
import jax.numpy as jnp
from jax import lax

ORDERS = 256
RADIAL = 512
BLOCK = 64
NBLOCKS = 8
TABLES = 16
TIME_DEV = 128
TIME = 512
N_TM = 4


def set_ends(values, key, smallest, largest):
    extent = values.shape
    index_at = [jax.random.randint(jax.random.fold_in(key, axis), (), 0, extent[axis]) for axis in range(len(extent))]
    values = values.at[tuple(index_at)].set(smallest)
    longest = extent.index(max(extent))
    index_at[longest] = (index_at[longest] + 1) % extent[longest]
    return values.at[tuple(index_at)].set(largest)


def levels(key, dims, cuts, low, high):
    gain, own = 1.0, jax.random.fold_in(key, 6)
    for axis_at, parts in cuts:
        draws = jnp.exp(jax.random.uniform(jax.random.fold_in(own, axis_at), (parts,), jnp.float32, low / len(cuts), high / len(cuts)))
        gain = gain * jnp.repeat(draws, dims[axis_at] // parts).reshape([-1 if axis == axis_at else 1 for axis in range(len(dims))])
    return gain


def bell_draw(stream_key, extent, scale, limit, shards=(), kind=jnp.bfloat16):
    entries = scale * jax.random.normal(stream_key, extent, jnp.float32)
    if shards:
        entries = entries * levels(stream_key, extent, shards, -0.22, 0.18)
    return jnp.clip(entries, -limit, limit).astype(kind)


def setup_inputs(seed: int = 0, part: int = 0) -> dict:
    arg_keys = jax.random.split(jax.random.key(seed), 7)
    part_splits = jax.random.split(jax.random.fold_in(arg_keys[6], part), 7)
    return {
        "field": bell_draw(part_splits[0], (2, ORDERS, RADIAL, TIME), 1.0, 6.0, ((1, 4), (3, 4))),
        "radial_tables": bell_draw(arg_keys[1], (TABLES, NBLOCKS, BLOCK, BLOCK), BLOCK ** -0.5, 0.75),
        "weights": jnp.clip(jnp.exp(jax.random.uniform(arg_keys[2], (RADIAL,), jnp.float32, math.log(0.3), math.log(3.0))), 0.3, 3.0),
        "order_map": set_ends(jax.random.randint(arg_keys[3], (ORDERS,), 0, TABLES), jax.random.fold_in(arg_keys[3], 1), 0, TABLES - 1).astype(jnp.int32),
        "curvature": jnp.clip(jnp.exp(math.log(0.5) - 2.3025851 * jax.random.uniform(arg_keys[4], (ORDERS, RADIAL), jnp.float32) ** levels(arg_keys[4], (ORDERS, RADIAL), ((0, 4),), -0.2, 0.2)), 0.05, 0.5),
        "walk_off": jnp.clip(jax.random.uniform(arg_keys[5], (ORDERS, RADIAL), jnp.float32, -0.5, 0.5) * levels(arg_keys[5], (ORDERS, RADIAL), ((0, 4),), -0.4, 0.0), -0.5, 0.5),
    }


kerr_gamma = 0.00390625


def angle_tables(count):
    index = jnp.arange(count, dtype=jnp.int32)
    phase = ((index[:, None] * index[None, :]) % count).astype(jnp.float32) * (2.0 * math.pi / count)
    cosine = jnp.cos(phase)
    sine = jnp.sin(phase)
    forward = jnp.concatenate([jnp.concatenate([cosine, -sine], 1), jnp.concatenate([sine, cosine], 1)], 0)
    backward = jnp.concatenate([jnp.concatenate([cosine, sine], 1), jnp.concatenate([-sine, cosine], 1)], 0)
    return forward.astype(jnp.bfloat16), backward.astype(jnp.bfloat16)


def reference(field, radial_tables, weights, order_map, curvature, walk_off):
    whole = field.astype(jnp.float32)
    right = jnp.roll(whole, -1, axis=3)
    left = jnp.roll(whole, 1, axis=3)
    second = right - 2.0 * whole + left
    first = 0.5 * (right - left)
    beta = curvature[:, :, None]
    delta = walk_off[:, :, None]
    real = whole[0] - beta * second[1] + delta * first[0]
    imag = whole[1] + beta * second[0] + delta * first[1]
    moved = jnp.stack([real, imag])
    moved_low = lax.optimization_barrier(moved.astype(jnp.bfloat16)).astype(jnp.float32)
    tables = radial_tables.astype(jnp.float32)[order_map]
    scaled = radial_tables.astype(jnp.float32) * weights.reshape(NBLOCKS, BLOCK)[None, :, :, None]
    analysis = lax.optimization_barrier(scaled.astype(jnp.bfloat16)).astype(jnp.float32)[order_map]
    forward, backward = angle_tables(ORDERS)
    forward = forward.astype(jnp.float32)
    backward = backward.astype(jnp.float32)

    def one_block(start):
        slab = lax.dynamic_slice_in_dim(moved_low, start, TIME_DEV, 3)
        slab = slab.reshape(2, ORDERS, NBLOCKS, BLOCK, TIME_DEV)
        points = jnp.einsum("mbqn,cmbnt->cmbqt", tables, slab)
        points = lax.optimization_barrier(points.astype(jnp.bfloat16)).astype(jnp.float32)
        flat = points.reshape(2 * ORDERS, RADIAL * TIME_DEV)
        angular = jnp.dot(forward, flat)
        power = angular[:ORDERS] ** 2 + angular[ORDERS:] ** 2
        kerr = jnp.concatenate([-kerr_gamma * power * angular[ORDERS:], kerr_gamma * power * angular[:ORDERS]], 0)
        kerr = lax.optimization_barrier(kerr.astype(jnp.bfloat16)).astype(jnp.float32)
        back = jnp.dot(backward, kerr) * (1.0 / ORDERS)
        back = lax.optimization_barrier(back.astype(jnp.bfloat16)).astype(jnp.float32)
        back = back.reshape(2, ORDERS, NBLOCKS, BLOCK, TIME_DEV)
        return jnp.einsum("mbqn,cmbqt->cmbnt", analysis, back).reshape(2, ORDERS, RADIAL, TIME_DEV)

    starts = jnp.arange(N_TM, dtype=jnp.int32) * TIME_DEV
    pieces = lax.map(one_block, starts)
    increment = jnp.moveaxis(pieces, 0, 3).reshape(2, ORDERS, RADIAL, TIME)
    return (moved + increment).astype(jnp.bfloat16)
```

```python
import functools
import math

import jax
import jax.numpy as jnp
import numpy as np
from jax import lax
from jax.experimental import pallas as pl
from jax.experimental.pallas import tpu as pltpu
from jax.sharding import PartitionSpec as P

ORDERS = 256
LANES = 128
ROWS = 16

kerr_gamma = 0.00390625


def angle_matrices(count):
    index = np.arange(count, dtype=np.int32)
    phase = (index[:, None] * index[None, :] % count).astype(np.float32) * np.float32(
        2.0 * math.pi / count
    )
    cosine, sine = np.cos(phase), np.sin(phase)
    forward = np.block([[cosine, -sine], [sine, cosine]])
    backward = np.block([[cosine, sine], [-sine, cosine]])
    return forward.astype(jnp.bfloat16), backward.astype(jnp.bfloat16)


def ring(axis, shift):
    count = lax.axis_size(axis)
    return [(i, (i + shift) % count) for i in range(count)]


def lane_index(rows):
    return lax.broadcasted_iota(jnp.int32, (rows, LANES), 1)


def roll(x, shift):
    return pltpu.roll(x, shift, 1)


def params():
    return pltpu.CompilerParams(vmem_limit_bytes=40 * 1024 * 1024)


def cost(flops, size):
    return pl.CostEstimate(flops=flops, bytes_accessed=size, transcendentals=0)


def anywhere(count):
    return [pl.BlockSpec(memory_space=pl.ANY)] * count


def edges(field, first, count, block, deps=()):
    parts, orders = field.shape[:2]
    groups = orders // ROWS

    def kernel(x_ref, *refs):
        o_ref, acc = refs[-2:]
        g = pl.program_id(1)
        slot = ((lane_index(block) + 1) >> 1) & (LANES // 2 - 1)
        for c in range(parts):
            kept = acc[c]
            for i in range(ROWS):
                m = g * ROWS + i
                row = roll(x_ref[c, i].astype(jnp.float32), 2 * m)
                kept = jnp.where(slot == m, row, kept)
            acc[c] = kept

        @pl.when(g == groups - 1)
        def _():
            o_ref[...] = acc[...].astype(o_ref.dtype)

    return pl.pallas_call(
        kernel,
        out_shape=jax.ShapeDtypeStruct((parts, count * block, LANES), field.dtype),
        grid=(count, groups),
        in_specs=[pl.BlockSpec((parts, ROWS, block, LANES), lambda j, g: (0, g, j + first, 0))]
        + anywhere(len(deps)),
        out_specs=pl.BlockSpec((parts, block, LANES), lambda j, g: (0, j, 0)),
        scratch_shapes=[pltpu.VMEM((parts, block, LANES), jnp.float32)],
        compiler_params=params(),
        cost_estimate=cost(0, parts * orders * count * block * LANES * 2),
        name="edges",
    )(field, *deps)


def join_halo(low, high):
    lane = lane_index(low.shape[0])
    low, high = low.astype(jnp.float32), high.astype(jnp.float32)
    return jnp.where((lane & 1) == 0, roll(low, 1), roll(high, LANES - 1))


def columns(ref, start, block):
    base = start // LANES * LANES
    turned = jnp.transpose(ref[:, base : base + LANES])
    return turned[start - base : start - base + block]


def move(x, halo, beta, delta, m):
    lane = lane_index(beta.shape[0])
    second, first = [], []
    for c in range(2):
        ends = roll(halo[c], (LANES - 2 * m) & (LANES - 1))
        left = jnp.where(lane == 0, ends, roll(x[c], 1))
        right = jnp.where(lane == LANES - 1, ends, roll(x[c], LANES - 1))
        second.append(right - 2.0 * x[c] + left)
        first.append(0.5 * (right - left))
    real = x[0] - beta * second[1] + delta * first[0]
    imag = x[1] + beta * second[0] + delta * first[1]
    return real, imag


def synthesize(field, low, high, halo_at, tables, curvature, walk_off, order_map, me, b, count, deps):
    parts, orders, radial, steps = field.shape
    kinds, _, block, _ = tables.shape
    share = block // count
    groups = orders // ROWS

    def kernel(map_ref, me_ref, x_ref, low_ref, high_ref, tab_ref, beta_ref, delta_ref, *refs):
        outs, acc = refs[len(deps) : -1], refs[-1]
        g = pl.program_id(0)
        beta = columns(beta_ref, b * block, block)
        delta = columns(delta_ref, b * block, block)
        halo = [join_halo(low_ref[c], high_ref[c]) for c in range(parts)]
        for i in range(ROWS):
            m = g * ROWS + i
            x = [x_ref[c, i].astype(jnp.float32) for c in range(parts)]
            moved = move(x, halo, beta[:, i : i + 1], delta[:, i : i + 1], m)
            moved = jnp.concatenate(moved, 1).astype(jnp.bfloat16)
            points = jnp.dot(
                tab_ref[map_ref[m], 0], moved, preferred_element_type=jnp.float32
            )
            for c in range(parts):
                acc[c, pl.ds(i, block, stride=ROWS), :] = points[:, c * LANES : (c + 1) * LANES]
        for s in range(count):
            owner = lax.rem(me_ref[0] + s, count)
            for q in range(share):
                row = pl.multiple_of((owner * share + q) * ROWS, ROWS)
                for c in range(parts):
                    outs[s][q, c] = acc[c, pl.ds(row, ROWS), :].astype(jnp.bfloat16)

    piece = jax.ShapeDtypeStruct((share, parts, orders, LANES), jnp.bfloat16)
    size = parts * orders * block * LANES * 2
    return pl.pallas_call(
        kernel,
        out_shape=[piece] * count,
        grid_spec=pltpu.PrefetchScalarGridSpec(
            num_scalar_prefetch=2,
            grid=(groups,),
            in_specs=[
                pl.BlockSpec((parts, ROWS, block, LANES), lambda g, *_: (0, g, b, 0)),
                pl.BlockSpec((parts, block, LANES), lambda g, *_: (0, halo_at, 0)),
                pl.BlockSpec((parts, block, LANES), lambda g, *_: (0, halo_at, 0)),
                pl.BlockSpec((kinds, 1, block, block), lambda g, *_: (0, b, 0, 0)),
                pl.BlockSpec((ROWS, radial), lambda g, *_: (g, 0)),
                pl.BlockSpec((ROWS, radial), lambda g, *_: (g, 0)),
            ]
            + anywhere(len(deps)),
            out_specs=[
                pl.BlockSpec((share, parts, ROWS, LANES), lambda g, *_: (0, 0, g, 0))
            ]
            * count,
            scratch_shapes=[pltpu.VMEM((parts, block * ROWS, LANES), jnp.float32)],
        ),
        compiler_params=params(),
        cost_estimate=cost(2 * size * block, 2 * size),
        name="synthesize",
    )(order_map, me, field, low, high, tables, curvature, walk_off, *deps)


def kerr_step(pieces, forward, backward, me, deps):
    count = len(pieces)
    share, parts, orders, _ = pieces[0].shape
    every = count * orders
    width = 2

    def kernel(me_ref, f_ref, b_ref, *refs):
        ins = refs[:count]
        outs, flat, back = refs[count + len(deps) : -2], refs[-2], refs[-1]
        for s in range(count):
            source = lax.rem(me_ref[0] + count - s, count)
            for c in range(parts):
                row = pl.multiple_of(c * every + source * orders, orders)
                for q in range(width):
                    flat[pl.ds(row, orders), q * LANES : (q + 1) * LANES] = ins[s][q, c]
        angular = jnp.dot(f_ref[...], flat[...], preferred_element_type=jnp.float32)
        real, imag = angular[:every], angular[every:]
        power = kerr_gamma * (real * real + imag * imag)
        kerr = jnp.concatenate([-power * imag, power * real], 0).astype(jnp.bfloat16)
        back[...] = (
            jnp.dot(b_ref[...], kerr, preferred_element_type=jnp.float32) * (1.0 / every)
        ).astype(jnp.bfloat16)
        for s in range(count):
            owner = lax.rem(me_ref[0] + s, count)
            for c in range(parts):
                row = pl.multiple_of(c * every + owner * orders, orders)
                for q in range(width):
                    outs[s][q, c] = back[pl.ds(row, orders), q * LANES : (q + 1) * LANES]

    block = pl.BlockSpec((width, parts, orders, LANES), lambda q, *_: (q, 0, 0, 0))
    whole = pl.BlockSpec((parts * every, parts * every), lambda q, *_: (0, 0))
    lanes = share * LANES
    return pl.pallas_call(
        kernel,
        out_shape=[jax.ShapeDtypeStruct(pieces[0].shape, jnp.bfloat16)] * count,
        grid_spec=pltpu.PrefetchScalarGridSpec(
            num_scalar_prefetch=1,
            grid=(share // width,),
            in_specs=[whole, whole] + [block] * count + anywhere(len(deps)),
            out_specs=[block] * count,
            scratch_shapes=[
                pltpu.VMEM((parts * every, width * LANES), jnp.bfloat16),
                pltpu.VMEM((parts * every, width * LANES), jnp.bfloat16),
            ],
        ),
        compiler_params=params(),
        cost_estimate=cost(4 * (parts * every) ** 2 * lanes, 4 * parts * every * lanes),
        name="kerr",
    )(me, forward, backward, *pieces, *deps)


def analyze(
    pieces, field, low, high, halo_at, tables, curvature, walk_off, order_map, me, b, out, deps
):
    count = len(pieces)
    parts, orders, radial, steps = field.shape
    kinds, _, block, _ = tables.shape
    share = block // count
    groups = orders // ROWS
    held = () if out is None else (out,)

    def kernel(map_ref, me_ref, *refs):
        ins = refs[:count]
        x_ref, low_ref, high_ref, tab_ref, beta_ref, delta_ref = refs[count : count + 6]
        o_ref, acc = refs[-2:]
        g = pl.program_id(0)
        for s in range(count):
            source = lax.rem(me_ref[0] + count - s, count)
            for q in range(share):
                row = pl.multiple_of((source * share + q) * ROWS, ROWS)
                for c in range(parts):
                    acc[c, pl.ds(row, ROWS), :] = ins[s][q, c].astype(jnp.float32)
        beta = columns(beta_ref, b * block, block)
        delta = columns(delta_ref, b * block, block)
        halo = [join_halo(low_ref[c], high_ref[c]) for c in range(parts)]
        for i in range(ROWS):
            m = g * ROWS + i
            x = [x_ref[c, i].astype(jnp.float32) for c in range(parts)]
            moved = move(x, halo, beta[:, i : i + 1], delta[:, i : i + 1], m)
            back = [acc[c, pl.ds(i, block, stride=ROWS), :] for c in range(parts)]
            back = jnp.concatenate(back, 1).astype(jnp.bfloat16)
            increment = jnp.dot(
                tab_ref[map_ref[m], 0], back, preferred_element_type=jnp.float32
            )
            for c in range(parts):
                total = moved[c] + increment[:, c * LANES : (c + 1) * LANES]
                o_ref[c, i] = total.astype(jnp.bfloat16)

    size = parts * orders * block * LANES * 2
    return pl.pallas_call(
        kernel,
        out_shape=jax.ShapeDtypeStruct(field.shape, field.dtype),
        grid_spec=pltpu.PrefetchScalarGridSpec(
            num_scalar_prefetch=2,
            grid=(groups,),
            in_specs=[
                pl.BlockSpec((share, parts, ROWS, LANES), lambda g, *_: (0, 0, g, 0))
            ]
            * count
            + [
                pl.BlockSpec((parts, ROWS, block, LANES), lambda g, *_: (0, g, b, 0)),
                pl.BlockSpec((parts, block, LANES), lambda g, *_: (0, halo_at, 0)),
                pl.BlockSpec((parts, block, LANES), lambda g, *_: (0, halo_at, 0)),
                pl.BlockSpec((kinds, 1, block, block), lambda g, *_: (0, b, 0, 0)),
                pl.BlockSpec((ROWS, radial), lambda g, *_: (g, 0)),
                pl.BlockSpec((ROWS, radial), lambda g, *_: (g, 0)),
            ]
            + anywhere(len(held) + len(deps)),
            out_specs=pl.BlockSpec((parts, ROWS, block, LANES), lambda g, *_: (0, g, b, 0)),
            scratch_shapes=[pltpu.VMEM((parts, block * ROWS, LANES), jnp.float32)],
        ),
        input_output_aliases={2 + count + 6: 0} if held else {},
        compiler_params=params(),
        cost_estimate=cost(2 * size * block, 3 * size),
        name="analyze",
    )(
        order_map, me, *pieces, field, low, high, tables, curvature, walk_off, *held, *deps
    )


def exchange(pieces):
    return [pieces[0]] + [
        lax.ppermute(pieces[s], "ang", ring("ang", s)) for s in range(1, len(pieces))
    ]


def pipelined(field, radial_tables, weights, order_map, curvature, walk_off):
    count = lax.axis_size("ang")
    nblocks, block = radial_tables.shape[1:3]
    me = lax.axis_index("ang").astype(jnp.int32).reshape(1)
    forward, backward = (jnp.asarray(table) for table in angle_matrices(ORDERS))
    scaled = radial_tables.astype(jnp.float32) * weights.reshape(nblocks, block)[None, :, :, None]
    analysis = scaled.astype(jnp.bfloat16).transpose(0, 1, 3, 2)
    halos = []

    def halo(first, some, deps=()):
        ends = edges(field, first, some, block, deps)
        low = lax.ppermute(ends, "tm", ring("tm", 1))
        high = lax.ppermute(ends, "tm", ring("tm", -1))
        for j in range(some):
            halos.append((low, high, j))

    def points(b, deps=()):
        low, high, at = halos[b]
        return synthesize(
            field, low, high, at, radial_tables, curvature, walk_off, order_map, me, b, count, deps
        )

    sent, returned = {}, {}
    halo(0, 1)
    own = points(0)
    sent[0] = exchange(own)
    halo(1, nblocks - 1, own[:1])
    own = points(1, own[:1])
    sent[1] = exchange(own)
    out, last = None, own
    for b in range(nblocks):
        back = kerr_step(sent.pop(b), forward, backward, me, last[:1])
        returned[b] = exchange(back)
        last = back
        if b >= 1:
            low, high, at = halos[b - 1]
            out = analyze(
                returned.pop(b - 1), field, low, high, at, analysis, curvature, walk_off,
                order_map, me, b - 1, out, last[:1],
            )
        if b + 2 < nblocks:
            own = points(b + 2, last[:1])
            sent[b + 2] = exchange(own)
            last = own
    low, high, at = halos[nblocks - 1]
    return analyze(
        returned.pop(nblocks - 1), field, low, high, at, analysis, curvature, walk_off,
        order_map, me, nblocks - 1, out, (),
    )


def with_halo(block, axis, dim):
    low = lax.ppermute(
        lax.slice_in_dim(block, block.shape[dim] - 1, None, axis=dim), axis, ring(axis, 1)
    )
    high = lax.ppermute(lax.slice_in_dim(block, 0, 1, axis=dim), axis, ring(axis, -1))
    return jnp.concatenate([low, block, high], axis=dim)


def local_kerr(pieces, forward, backward):
    orders = pieces.shape[1]
    flat = pieces.reshape(2 * orders, -1)
    angular = jnp.dot(forward, flat, preferred_element_type=jnp.float32)
    power = angular[:orders] ** 2 + angular[orders:] ** 2
    kerr = jnp.concatenate(
        [-kerr_gamma * power * angular[orders:], kerr_gamma * power * angular[:orders]], 0
    )
    kerr = kerr.astype(jnp.bfloat16)
    back = jnp.dot(backward, kerr, preferred_element_type=jnp.float32) * (1.0 / orders)
    return back.astype(jnp.bfloat16).reshape(pieces.shape)


def whole_arrays(field, radial_tables, weights, order_map, curvature, walk_off):
    local_orders, radial, steps_dev = field.shape[1:]
    nblocks, block = radial_tables.shape[1:3]
    padded = with_halo(field, "tm", 3).astype(jnp.float32)
    middle = padded[..., 1:-1]
    right = padded[..., 2:]
    left = padded[..., :-2]
    second = right - 2.0 * middle + left
    first = 0.5 * (right - left)
    beta = curvature[:, :, None]
    delta = walk_off[:, :, None]
    real = middle[0] - beta * second[1] + delta * first[0]
    imag = middle[1] + beta * second[0] + delta * first[1]
    moved = jnp.stack([real, imag])
    moved_low = moved.astype(jnp.bfloat16).reshape(2, local_orders, nblocks, block, steps_dev)
    tables = jnp.take(radial_tables, order_map, axis=0)
    scaled = radial_tables.astype(jnp.float32) * weights.reshape(nblocks, block)[None, :, :, None]
    analysis = jnp.take(scaled.astype(jnp.bfloat16), order_map, axis=0)
    points = jnp.einsum("mbqn,cmbnt->cmbqt", tables, moved_low, preferred_element_type=jnp.float32)
    points = points.reshape(2, local_orders, radial, steps_dev).astype(jnp.bfloat16)
    forward, backward = (jnp.asarray(table) for table in angle_matrices(ORDERS))
    back = local_kerr(
        lax.all_to_all(points, "ang", split_axis=2, concat_axis=1, tiled=True), forward, backward
    )
    returned = lax.all_to_all(back, "ang", split_axis=1, concat_axis=2, tiled=True)
    returned = returned.reshape(2, local_orders, nblocks, block, steps_dev)
    increment = jnp.einsum(
        "mbqn,cmbqt->cmbnt", analysis, returned, preferred_element_type=jnp.float32
    )
    increment = increment.reshape(2, local_orders, radial, steps_dev)
    return (moved + increment).astype(jnp.bfloat16)


def per_device(field, radial_tables, weights, order_map, curvature, walk_off):
    parts, orders, radial, steps = field.shape
    nblocks, block = radial_tables.shape[1:3]
    count = lax.axis_size("ang")
    fits = (
        steps == LANES
        and orders % ROWS == 0
        and 2 * orders <= LANES
        and block % (2 * count) == 0
        and radial % LANES == 0
        and LANES % block == 0
        and nblocks >= 2
    )
    plan = pipelined if fits else whole_arrays
    return plan(field, radial_tables, weights, order_map, curvature, walk_off)


def solution(mesh):
    in_specs = (P("groups", "ang", None, "tm"), P(), P(), P("ang"), P("ang", None), P("ang", None))
    out_specs = P("groups", "ang", None, "tm")
    return jax.shard_map(
        per_device, mesh=mesh, in_specs=in_specs, out_specs=out_specs, check_vma=False
    )
```

```python
import functools
import math

import jax
import jax.numpy as jnp
import numpy as np
from jax import lax
from jax.experimental import pallas as pl
from jax.experimental.pallas import tpu as pltpu
from jax.sharding import PartitionSpec as P

ORDERS = 256
LANES = 128
ROWS = 16

kerr_gamma = 0.00390625


def angle_matrices(count):
    index = np.arange(count, dtype=np.int32)
    phase = (index[:, None] * index[None, :] % count).astype(np.float32) * np.float32(
        2.0 * math.pi / count
    )
    cosine, sine = np.cos(phase), np.sin(phase)
    forward = np.block([[cosine, -sine], [sine, cosine]])
    backward = np.block([[cosine, sine], [-sine, cosine]])
    return forward.astype(jnp.bfloat16), backward.astype(jnp.bfloat16)


def ring(axis, shift):
    count = lax.axis_size(axis)
    return [(i, (i + shift) % count) for i in range(count)]


def lane_index(rows):
    return lax.broadcasted_iota(jnp.int32, (rows, LANES), 1)


def roll(x, shift):
    return pltpu.roll(x, shift, 1)


def params():
    return pltpu.CompilerParams(vmem_limit_bytes=40 * 1024 * 1024)


def cost(flops, size):
    return pl.CostEstimate(flops=flops, bytes_accessed=size, transcendentals=0)


def anywhere(count):
    return [pl.BlockSpec(memory_space=pl.ANY)] * count


def token():
    return jax.ShapeDtypeStruct((8, LANES), jnp.float32)


def edges(field, first, count, block, span, after):
    parts = field.shape[0]
    base, groups = span[0] // ROWS, span[1] // ROWS

    def kernel(x_ref, *refs):
        o_ref, _, acc = refs[-3:]
        g = pl.program_id(1)
        slot = ((lane_index(block) + 1) >> 1) & (LANES // 2 - 1)
        for c in range(parts):
            kept = acc[c]
            for i in range(ROWS):
                m = (g + base) * ROWS + i
                row = roll(x_ref[c, i].astype(jnp.float32), 2 * m)
                kept = jnp.where(slot == m, row, kept)
            acc[c] = kept

        @pl.when(g == groups - 1)
        def _():
            o_ref[...] = acc[...].astype(o_ref.dtype)

    return pl.pallas_call(
        kernel,
        out_shape=[
            jax.ShapeDtypeStruct((parts, count * block, LANES), field.dtype),
            token(),
        ],
        grid=(count, groups),
        in_specs=[
            pl.BlockSpec((parts, ROWS, block, LANES), lambda j, g: (0, g + base, j + first, 0))
        ]
        + anywhere(len(after)),
        out_specs=[pl.BlockSpec((parts, block, LANES), lambda j, g: (0, j, 0))] + anywhere(1),
        scratch_shapes=[pltpu.VMEM((parts, block, LANES), jnp.float32)],
        compiler_params=params(),
        cost_estimate=cost(0, parts * span[1] * count * block * LANES * 2),
        name="edges",
    )(field, *after)


def join_halo(low, high):
    lane = lane_index(low.shape[0])
    low, high = low.astype(jnp.float32), high.astype(jnp.float32)
    return jnp.where((lane & 1) == 0, roll(low, 1), roll(high, LANES - 1))


def columns(ref, start, block):
    base = start // LANES * LANES
    turned = jnp.transpose(ref[:, base : base + LANES])
    return turned[start - base : start - base + block]


def move(x, halo, beta, delta, m):
    lane = lane_index(beta.shape[0])
    second, first = [], []
    for c in range(2):
        ends = roll(halo[c], (LANES - 2 * m) & (LANES - 1))
        left = jnp.where(lane == 0, ends, roll(x[c], 1))
        right = jnp.where(lane == LANES - 1, ends, roll(x[c], LANES - 1))
        second.append(right - 2.0 * x[c] + left)
        first.append(0.5 * (right - left))
    real = x[0] - beta * second[1] + delta * first[0]
    imag = x[1] + beta * second[0] + delta * first[1]
    return real, imag


def radial_specs(parts, kinds, block, radial, b, halo_at, base):
    return [
        pl.BlockSpec((parts, ROWS, block, LANES), lambda g, *_: (0, g + base, b, 0)),
        pl.BlockSpec((parts, block, LANES), lambda g, *_: (0, halo_at, 0)),
        pl.BlockSpec((parts, block, LANES), lambda g, *_: (0, halo_at, 0)),
        pl.BlockSpec((kinds, 1, block, block), lambda g, *_: (0, b, 0, 0)),
        pl.BlockSpec((ROWS, radial), lambda g, *_: (g + base, 0)),
        pl.BlockSpec((ROWS, radial), lambda g, *_: (g + base, 0)),
    ]


def synthesize(field, halo, tables, curvature, walk_off, order_map, me, b, count, span, after):
    low, high, halo_at = halo
    parts, _, radial, _ = field.shape
    kinds, _, block, _ = tables.shape
    share = block // count
    base, groups = span[0] // ROWS, span[1] // ROWS

    def kernel(map_ref, me_ref, x_ref, low_ref, high_ref, tab_ref, beta_ref, delta_ref, *refs):
        outs, acc = refs[len(after) : len(after) + count], refs[-1]
        g = pl.program_id(0)
        beta = columns(beta_ref, b * block, block)
        delta = columns(delta_ref, b * block, block)
        ends = [join_halo(low_ref[c], high_ref[c]) for c in range(parts)]
        for i in range(ROWS):
            m = (g + base) * ROWS + i
            x = [x_ref[c, i].astype(jnp.float32) for c in range(parts)]
            moved = move(x, ends, beta[:, i : i + 1], delta[:, i : i + 1], m)
            moved = jnp.concatenate(moved, 1).astype(jnp.bfloat16)
            points = jnp.dot(
                tab_ref[map_ref[m], 0], moved, preferred_element_type=jnp.float32
            )
            for c in range(parts):
                acc[c, pl.ds(i, block, stride=ROWS), :] = points[:, c * LANES : (c + 1) * LANES]
        for s in range(count):
            owner = lax.rem(me_ref[0] + s, count)
            for q in range(share):
                row = pl.multiple_of((owner * share + q) * ROWS, ROWS)
                for c in range(parts):
                    outs[s][q, c] = acc[c, pl.ds(row, ROWS), :].astype(jnp.bfloat16)

    piece = jax.ShapeDtypeStruct((share, parts, span[1], LANES), jnp.bfloat16)
    size = parts * span[1] * block * LANES * 2
    *pieces, done = pl.pallas_call(
        kernel,
        out_shape=[piece] * count + [token()],
        grid_spec=pltpu.PrefetchScalarGridSpec(
            num_scalar_prefetch=2,
            grid=(groups,),
            in_specs=radial_specs(parts, kinds, block, radial, b, halo_at, base)
            + anywhere(len(after)),
            out_specs=[
                pl.BlockSpec((share, parts, ROWS, LANES), lambda g, *_: (0, 0, g, 0))
            ]
            * count
            + anywhere(1),
            scratch_shapes=[pltpu.VMEM((parts, block * ROWS, LANES), jnp.float32)],
        ),
        compiler_params=params(),
        cost_estimate=cost(2 * size * block, 2 * size),
        name="synthesize",
    )(order_map, me, field, low, high, tables, curvature, walk_off, *after)
    return pieces, done


def kerr_step(pieces, spans, out_spans, forward, backward, me, after):
    count = len(pieces[0])
    share, parts = pieces[0][0].shape[:2]
    orders = sum(size for _, size in spans)
    every = count * orders
    width = 2
    ins_count, outs_count = count * len(spans), count * len(out_spans)

    def kernel(me_ref, f_ref, b_ref, *refs):
        ins = refs[:ins_count]
        outs = refs[ins_count + len(after) : ins_count + len(after) + outs_count]
        flat, back = refs[-2:]
        for k, (start, size) in enumerate(spans):
            for s in range(count):
                source = lax.rem(me_ref[0] + count - s, count)
                for c in range(parts):
                    row = pl.multiple_of(c * every + source * orders + start, ROWS)
                    for q in range(width):
                        flat[pl.ds(row, size), q * LANES : (q + 1) * LANES] = ins[
                            k * count + s
                        ][q, c]
        angular = jnp.dot(f_ref[...], flat[...], preferred_element_type=jnp.float32)
        real, imag = angular[:every], angular[every:]
        power = kerr_gamma * (real * real + imag * imag)
        kerr = jnp.concatenate([-power * imag, power * real], 0).astype(jnp.bfloat16)
        back[...] = (
            jnp.dot(b_ref[...], kerr, preferred_element_type=jnp.float32) * (1.0 / every)
        ).astype(jnp.bfloat16)
        for k, (start, size) in enumerate(out_spans):
            for s in range(count):
                owner = lax.rem(me_ref[0] + s, count)
                for c in range(parts):
                    row = pl.multiple_of(c * every + owner * orders + start, ROWS)
                    for q in range(width):
                        outs[k * count + s][q, c] = back[
                            pl.ds(row, size), q * LANES : (q + 1) * LANES
                        ]

    def blocks(some):
        return [
            pl.BlockSpec((width, parts, size, LANES), lambda q, *_: (q, 0, 0, 0))
            for _, size in some
            for _ in range(count)
        ]

    whole = pl.BlockSpec((parts * every, parts * every), lambda q, *_: (0, 0))
    lanes = share * LANES
    *back, done = pl.pallas_call(
        kernel,
        out_shape=[
            jax.ShapeDtypeStruct((share, parts, size, LANES), jnp.bfloat16)
            for _, size in out_spans
            for _ in range(count)
        ]
        + [token()],
        grid_spec=pltpu.PrefetchScalarGridSpec(
            num_scalar_prefetch=1,
            grid=(share // width,),
            in_specs=[whole, whole] + blocks(spans) + anywhere(len(after)),
            out_specs=blocks(out_spans) + anywhere(1),
            scratch_shapes=[
                pltpu.VMEM((parts * every, width * LANES), jnp.bfloat16),
                pltpu.VMEM((parts * every, width * LANES), jnp.bfloat16),
            ],
        ),
        compiler_params=params(),
        cost_estimate=cost(4 * (parts * every) ** 2 * lanes, 4 * parts * every * lanes),
        name="kerr",
    )(me, forward, backward, *(piece for group in pieces for piece in group), *after)
    return [back[k * count : (k + 1) * count] for k in range(len(out_spans))], done


def analyze(
    pieces, field, halo, tables, curvature, walk_off, order_map, me, b, span, out, after
):
    low, high, halo_at = halo
    count = len(pieces)
    parts, _, radial, _ = field.shape
    kinds, _, block, _ = tables.shape
    share = block // count
    base, groups = span[0] // ROWS, span[1] // ROWS
    held = () if out is None else (out,)

    def kernel(map_ref, me_ref, *refs):
        ins = refs[:count]
        x_ref, low_ref, high_ref, tab_ref, beta_ref, delta_ref = refs[count : count + 6]
        o_ref, _, acc = refs[-3:]
        g = pl.program_id(0)
        for s in range(count):
            source = lax.rem(me_ref[0] + count - s, count)
            for q in range(share):
                row = pl.multiple_of((source * share + q) * ROWS, ROWS)
                for c in range(parts):
                    acc[c, pl.ds(row, ROWS), :] = ins[s][q, c].astype(jnp.float32)
        beta = columns(beta_ref, b * block, block)
        delta = columns(delta_ref, b * block, block)
        ends = [join_halo(low_ref[c], high_ref[c]) for c in range(parts)]
        for i in range(ROWS):
            m = (g + base) * ROWS + i
            x = [x_ref[c, i].astype(jnp.float32) for c in range(parts)]
            moved = move(x, ends, beta[:, i : i + 1], delta[:, i : i + 1], m)
            back = [acc[c, pl.ds(i, block, stride=ROWS), :] for c in range(parts)]
            back = jnp.concatenate(back, 1).astype(jnp.bfloat16)
            increment = jnp.dot(
                tab_ref[map_ref[m], 0], back, preferred_element_type=jnp.float32
            )
            for c in range(parts):
                total = moved[c] + increment[:, c * LANES : (c + 1) * LANES]
                o_ref[c, i] = total.astype(jnp.bfloat16)

    size = parts * span[1] * block * LANES * 2
    return pl.pallas_call(
        kernel,
        out_shape=[jax.ShapeDtypeStruct(field.shape, field.dtype), token()],
        grid_spec=pltpu.PrefetchScalarGridSpec(
            num_scalar_prefetch=2,
            grid=(groups,),
            in_specs=[
                pl.BlockSpec((share, parts, ROWS, LANES), lambda g, *_: (0, 0, g, 0))
            ]
            * count
            + radial_specs(parts, kinds, block, radial, b, halo_at, base)
            + anywhere(len(held) + len(after)),
            out_specs=[
                pl.BlockSpec((parts, ROWS, block, LANES), lambda g, *_: (0, g + base, b, 0))
            ]
            + anywhere(1),
            scratch_shapes=[pltpu.VMEM((parts, block * ROWS, LANES), jnp.float32)],
        ),
        input_output_aliases={2 + count + 6: 0} if held else {},
        compiler_params=params(),
        cost_estimate=cost(2 * size * block, 3 * size),
        name="analyze",
    )(
        order_map, me, *pieces, field, low, high, tables, curvature, walk_off, *held, *after
    )


def exchange(pieces):
    return [pieces[0]] + [
        lax.ppermute(pieces[s], "ang", ring("ang", s)) for s in range(1, len(pieces))
    ]


def spans_of(sizes):
    starts = [sum(sizes[:k]) for k in range(len(sizes))]
    return list(zip(starts, sizes, strict=True))


def pipelined(field, radial_tables, weights, order_map, curvature, walk_off):
    count = lax.axis_size("ang")
    orders = field.shape[1]
    nblocks, block = radial_tables.shape[1:3]
    me = lax.axis_index("ang").astype(jnp.int32).reshape(1)
    forward, backward = (jnp.asarray(table) for table in angle_matrices(ORDERS))
    scaled = radial_tables.astype(jnp.float32) * weights.reshape(nblocks, block)[None, :, :, None]
    analysis = scaled.astype(jnp.bfloat16).transpose(0, 1, 3, 2)
    whole = spans_of([orders])
    head = spans_of([ROWS, orders - ROWS]) if orders > ROWS else whole
    tail = spans_of([orders // 2, orders // 4, orders // 4]) if orders % (4 * ROWS) == 0 else whole
    spans = {0: head}
    out_spans = {nblocks - 1: tail}
    after = ()
    halos, sent, returned = {}, {}, {}
    out = None

    def halo(first, some, span, after):
        ends, done = edges(field, first, some, block, span, after)
        low = lax.ppermute(ends, "tm", ring("tm", 1))
        high = lax.ppermute(ends, "tm", ring("tm", -1))
        return [(low, high, j) for j in range(some)], (done,)

    def points(b, span, ends, after):
        own, done = synthesize(
            field, ends, radial_tables, curvature, walk_off, order_map, me, b, count, span, after
        )
        sent.setdefault(b, []).append(exchange(own))
        return (done,)

    def turn(b, after):
        back, done = kerr_step(
            sent.pop(b), spans.get(b, whole), out_spans.get(b, whole), forward, backward, me, after
        )
        returned[b] = [exchange(group) for group in back]
        return (done,)

    def finish(b, out, after):
        for span, group in zip(out_spans.get(b, whole), returned.pop(b), strict=True):
            out, done = analyze(
                group, field, halos[b], analysis, curvature, walk_off, order_map, me, b, span,
                out, after,
            )
            after = (done,)
        return out, after

    early, after = halo(0, 1, head[0], after)
    (halos[0],), after = halo(0, 1, whole[0], after)
    for k, span in enumerate(head):
        after = points(0, span, early[0] if k == 0 else halos[0], after)
    (halos[1],), after = halo(1, 1, whole[0], after)
    after = points(1, whole[0], halos[1], after)
    if nblocks > 2:
        rest, after = halo(2, nblocks - 2, whole[0], after)
        halos.update(zip(range(2, nblocks), rest, strict=True))
    for b in range(nblocks):
        after = turn(b, after)
        if b >= 1:
            out, after = finish(b - 1, out, after)
        if b + 2 < nblocks:
            after = points(b + 2, whole[0], halos[b + 2], after)
    out, after = finish(nblocks - 1, out, after)
    return out


def with_halo(block, axis, dim):
    low = lax.ppermute(
        lax.slice_in_dim(block, block.shape[dim] - 1, None, axis=dim), axis, ring(axis, 1)
    )
    high = lax.ppermute(lax.slice_in_dim(block, 0, 1, axis=dim), axis, ring(axis, -1))
    return jnp.concatenate([low, block, high], axis=dim)


def local_kerr(pieces, forward, backward):
    orders = pieces.shape[1]
    flat = pieces.reshape(2 * orders, -1)
    angular = jnp.dot(forward, flat, preferred_element_type=jnp.float32)
    power = angular[:orders] ** 2 + angular[orders:] ** 2
    kerr = jnp.concatenate(
        [-kerr_gamma * power * angular[orders:], kerr_gamma * power * angular[:orders]], 0
    )
    kerr = kerr.astype(jnp.bfloat16)
    back = jnp.dot(backward, kerr, preferred_element_type=jnp.float32) * (1.0 / orders)
    return back.astype(jnp.bfloat16).reshape(pieces.shape)


def whole_arrays(field, radial_tables, weights, order_map, curvature, walk_off):
    local_orders, radial, steps_dev = field.shape[1:]
    nblocks, block = radial_tables.shape[1:3]
    padded = with_halo(field, "tm", 3).astype(jnp.float32)
    middle = padded[..., 1:-1]
    right = padded[..., 2:]
    left = padded[..., :-2]
    second = right - 2.0 * middle + left
    first = 0.5 * (right - left)
    beta = curvature[:, :, None]
    delta = walk_off[:, :, None]
    real = middle[0] - beta * second[1] + delta * first[0]
    imag = middle[1] + beta * second[0] + delta * first[1]
    moved = jnp.stack([real, imag])
    moved_low = moved.astype(jnp.bfloat16).reshape(2, local_orders, nblocks, block, steps_dev)
    tables = jnp.take(radial_tables, order_map, axis=0)
    scaled = radial_tables.astype(jnp.float32) * weights.reshape(nblocks, block)[None, :, :, None]
    analysis = jnp.take(scaled.astype(jnp.bfloat16), order_map, axis=0)
    points = jnp.einsum("mbqn,cmbnt->cmbqt", tables, moved_low, preferred_element_type=jnp.float32)
    points = points.reshape(2, local_orders, radial, steps_dev).astype(jnp.bfloat16)
    forward, backward = (jnp.asarray(table) for table in angle_matrices(ORDERS))
    back = local_kerr(
        lax.all_to_all(points, "ang", split_axis=2, concat_axis=1, tiled=True), forward, backward
    )
    returned = lax.all_to_all(back, "ang", split_axis=1, concat_axis=2, tiled=True)
    returned = returned.reshape(2, local_orders, nblocks, block, steps_dev)
    increment = jnp.einsum(
        "mbqn,cmbqt->cmbnt", analysis, returned, preferred_element_type=jnp.float32
    )
    increment = increment.reshape(2, local_orders, radial, steps_dev)
    return (moved + increment).astype(jnp.bfloat16)


def per_device(field, radial_tables, weights, order_map, curvature, walk_off):
    parts, orders, radial, steps = field.shape
    nblocks, block = radial_tables.shape[1:3]
    count = lax.axis_size("ang")
    fits = (
        steps == LANES
        and orders % ROWS == 0
        and 2 * orders <= LANES
        and block % (2 * count) == 0
        and radial % LANES == 0
        and LANES % block == 0
        and nblocks >= 2
    )
    plan = pipelined if fits else whole_arrays
    return plan(field, radial_tables, weights, order_map, curvature, walk_off)


def solution(mesh):
    in_specs = (P("groups", "ang", None, "tm"), P(), P(), P("ang"), P("ang", None), P("ang", None))
    out_specs = P("groups", "ang", None, "tm")
    return jax.shard_map(
        per_device, mesh=mesh, in_specs=in_specs, out_specs=out_specs, check_vma=False
    )
```

```python
import functools
import math

import jax
import jax.numpy as jnp
import numpy as np
from jax import lax
from jax.experimental import pallas as pl
from jax.experimental.pallas import tpu as pltpu
from jax.sharding import PartitionSpec as P

ORDERS = 256
LANES = 128
ROWS = 16

kerr_gamma = 0.00390625


def angle_matrices(count):
    index = np.arange(count, dtype=np.int32)
    phase = (index[:, None] * index[None, :] % count).astype(np.float32) * np.float32(
        2.0 * math.pi / count
    )
    cosine, sine = np.cos(phase), np.sin(phase)
    forward = np.block([[cosine, -sine], [sine, cosine]])
    backward = np.block([[cosine, sine], [-sine, cosine]])
    return forward.astype(jnp.bfloat16), backward.astype(jnp.bfloat16)


def ring(axis, shift):
    count = lax.axis_size(axis)
    return [(i, (i + shift) % count) for i in range(count)]


def lane_index(rows):
    return lax.broadcasted_iota(jnp.int32, (rows, LANES), 1)


def roll(x, shift):
    return pltpu.roll(x, shift, 1)


def params():
    return pltpu.CompilerParams(vmem_limit_bytes=40 * 1024 * 1024)


def cost(flops, size):
    return pl.CostEstimate(flops=flops, bytes_accessed=size, transcendentals=0)


def anywhere(count):
    return [pl.BlockSpec(memory_space=pl.ANY)] * count


def token():
    return jax.ShapeDtypeStruct((8, LANES), jnp.float32)


def edges(field, first, count, block, span, after):
    parts = field.shape[0]
    base, groups = span[0] // ROWS, span[1] // ROWS

    def kernel(x_ref, *refs):
        o_ref, _, acc = refs[-3:]
        g = pl.program_id(1)
        slot = ((lane_index(block) + 1) >> 1) & (LANES // 2 - 1)
        for c in range(parts):
            kept = acc[c]
            for i in range(ROWS):
                m = (g + base) * ROWS + i
                row = roll(x_ref[c, i].astype(jnp.float32), 2 * m)
                kept = jnp.where(slot == m, row, kept)
            acc[c] = kept

        @pl.when(g == groups - 1)
        def _():
            o_ref[...] = acc[...].astype(o_ref.dtype)

    return pl.pallas_call(
        kernel,
        out_shape=[
            jax.ShapeDtypeStruct((parts, count * block, LANES), field.dtype),
            token(),
        ],
        grid=(count, groups),
        in_specs=[
            pl.BlockSpec((parts, ROWS, block, LANES), lambda j, g: (0, g + base, j + first, 0))
        ]
        + anywhere(len(after)),
        out_specs=[pl.BlockSpec((parts, block, LANES), lambda j, g: (0, j, 0))] + anywhere(1),
        scratch_shapes=[pltpu.VMEM((parts, block, LANES), jnp.float32)],
        compiler_params=params(),
        cost_estimate=cost(0, parts * span[1] * count * block * LANES * 2),
        name="edges",
    )(field, *after)


def join_halo(low, high):
    lane = lane_index(low.shape[0])
    low, high = low.astype(jnp.float32), high.astype(jnp.float32)
    return jnp.where((lane & 1) == 0, roll(low, 1), roll(high, LANES - 1))


def columns(ref, start, block):
    base = start // LANES * LANES
    turned = jnp.transpose(ref[:, base : base + LANES])
    return turned[start - base : start - base + block]


def move(x, halo, beta, delta, m):
    lane = lane_index(beta.shape[0])
    second, first = [], []
    for c in range(2):
        ends = roll(halo[c], (LANES - 2 * m) & (LANES - 1))
        left = jnp.where(lane == 0, ends, roll(x[c], 1))
        right = jnp.where(lane == LANES - 1, ends, roll(x[c], LANES - 1))
        second.append(right - 2.0 * x[c] + left)
        first.append(0.5 * (right - left))
    real = x[0] - beta * second[1] + delta * first[0]
    imag = x[1] + beta * second[0] + delta * first[1]
    return real, imag


def radial_specs(parts, kinds, block, radial, b, halo_at, base):
    return [
        pl.BlockSpec((parts, ROWS, block, LANES), lambda g, *_: (0, g + base, b, 0)),
        pl.BlockSpec((parts, block, LANES), lambda g, *_: (0, halo_at, 0)),
        pl.BlockSpec((parts, block, LANES), lambda g, *_: (0, halo_at, 0)),
        pl.BlockSpec((kinds, 1, block, block), lambda g, *_: (0, b, 0, 0)),
        pl.BlockSpec((ROWS, radial), lambda g, *_: (g + base, 0)),
        pl.BlockSpec((ROWS, radial), lambda g, *_: (g + base, 0)),
    ]


def synthesize(field, halo, tables, curvature, walk_off, order_map, b, count, span, after):
    low, high, halo_at = halo
    parts, _, radial, _ = field.shape
    kinds, _, block, _ = tables.shape
    share = block // count
    base, groups = span[0] // ROWS, span[1] // ROWS

    def kernel(map_ref, x_ref, low_ref, high_ref, tab_ref, beta_ref, delta_ref, *refs):
        o_ref, _, acc = refs[-3:]
        g = pl.program_id(0)
        beta = columns(beta_ref, b * block, block)
        delta = columns(delta_ref, b * block, block)
        ends = [join_halo(low_ref[c], high_ref[c]) for c in range(parts)]
        for i in range(ROWS):
            m = (g + base) * ROWS + i
            x = [x_ref[c, i].astype(jnp.float32) for c in range(parts)]
            moved = move(x, ends, beta[:, i : i + 1], delta[:, i : i + 1], m)
            moved = jnp.concatenate(moved, 1).astype(jnp.bfloat16)
            points = jnp.dot(
                tab_ref[map_ref[m], 0], moved, preferred_element_type=jnp.float32
            )
            for c in range(parts):
                acc[c, pl.ds(i, block, stride=ROWS), :] = points[:, c * LANES : (c + 1) * LANES]
        for d in range(count):
            for q in range(share):
                row = (d * share + q) * ROWS
                for c in range(parts):
                    o_ref[d, q, c] = acc[c, row : row + ROWS, :].astype(jnp.bfloat16)

    size = parts * span[1] * block * LANES * 2
    return pl.pallas_call(
        kernel,
        out_shape=[
            jax.ShapeDtypeStruct((count, share, parts, span[1], LANES), jnp.bfloat16),
            token(),
        ],
        grid_spec=pltpu.PrefetchScalarGridSpec(
            num_scalar_prefetch=1,
            grid=(groups,),
            in_specs=radial_specs(parts, kinds, block, radial, b, halo_at, base)
            + anywhere(len(after)),
            out_specs=[
                pl.BlockSpec((count, share, parts, ROWS, LANES), lambda g, *_: (0, 0, 0, g, 0))
            ]
            + anywhere(1),
            scratch_shapes=[pltpu.VMEM((parts, block * ROWS, LANES), jnp.float32)],
        ),
        compiler_params=params(),
        cost_estimate=cost(2 * size * block, 2 * size),
        name="synthesize",
    )(order_map, field, low, high, tables, curvature, walk_off, *after)


def kerr_step(pieces, spans, out_spans, forward, backward, after):
    count, share, parts = pieces[0].shape[:3]
    orders = sum(size for _, size in spans)
    every = count * orders
    width = 2

    def kernel(f_ref, b_ref, *refs):
        ins, flat, back = refs[: len(spans)], refs[-2], refs[-1]
        outs = refs[len(spans) + len(after) : -3]
        for k, (start, size) in enumerate(spans):
            for d in range(count):
                for c in range(parts):
                    row = c * every + d * orders + start
                    for q in range(width):
                        flat[row : row + size, q * LANES : (q + 1) * LANES] = ins[k][d, q, c]
        angular = jnp.dot(f_ref[...], flat[...], preferred_element_type=jnp.float32)
        real, imag = angular[:every], angular[every:]
        power = kerr_gamma * (real * real + imag * imag)
        kerr = jnp.concatenate([-power * imag, power * real], 0).astype(jnp.bfloat16)
        back[...] = (
            jnp.dot(b_ref[...], kerr, preferred_element_type=jnp.float32) * (1.0 / every)
        ).astype(jnp.bfloat16)
        for k, (start, size) in enumerate(out_spans):
            for d in range(count):
                for c in range(parts):
                    row = c * every + d * orders + start
                    for q in range(width):
                        outs[k][d, q, c] = back[row : row + size, q * LANES : (q + 1) * LANES]

    def blocks(some):
        return [
            pl.BlockSpec((count, width, parts, size, LANES), lambda q: (0, q, 0, 0, 0))
            for _, size in some
        ]

    whole = pl.BlockSpec((parts * every, parts * every), lambda q: (0, 0))
    lanes = share * LANES
    *back, done = pl.pallas_call(
        kernel,
        out_shape=[
            jax.ShapeDtypeStruct((count, share, parts, size, LANES), jnp.bfloat16)
            for _, size in out_spans
        ]
        + [token()],
        grid=(share // width,),
        in_specs=[whole, whole] + blocks(spans) + anywhere(len(after)),
        out_specs=blocks(out_spans) + anywhere(1),
        scratch_shapes=[
            pltpu.VMEM((parts * every, width * LANES), jnp.bfloat16),
            pltpu.VMEM((parts * every, width * LANES), jnp.bfloat16),
        ],
        compiler_params=params(),
        cost_estimate=cost(4 * (parts * every) ** 2 * lanes, 4 * parts * every * lanes),
        name="kerr",
    )(forward, backward, *pieces, *after)
    return back, done


def analyze(piece, field, halo, tables, curvature, walk_off, order_map, b, span, out, after):
    low, high, halo_at = halo
    count = piece.shape[0]
    parts, _, radial, _ = field.shape
    kinds, _, block, _ = tables.shape
    share = block // count
    base, groups = span[0] // ROWS, span[1] // ROWS
    held = () if out is None else (out,)

    def kernel(
        map_ref, p_ref, x_ref, low_ref, high_ref, tab_ref, beta_ref, delta_ref, *refs
    ):
        o_ref, _, acc = refs[-3:]
        g = pl.program_id(0)
        for d in range(count):
            for q in range(share):
                row = (d * share + q) * ROWS
                for c in range(parts):
                    acc[c, row : row + ROWS, :] = p_ref[d, q, c].astype(jnp.float32)
        beta = columns(beta_ref, b * block, block)
        delta = columns(delta_ref, b * block, block)
        ends = [join_halo(low_ref[c], high_ref[c]) for c in range(parts)]
        for i in range(ROWS):
            m = (g + base) * ROWS + i
            x = [x_ref[c, i].astype(jnp.float32) for c in range(parts)]
            moved = move(x, ends, beta[:, i : i + 1], delta[:, i : i + 1], m)
            back = [acc[c, pl.ds(i, block, stride=ROWS), :] for c in range(parts)]
            back = jnp.concatenate(back, 1).astype(jnp.bfloat16)
            increment = jnp.dot(
                tab_ref[map_ref[m], 0], back, preferred_element_type=jnp.float32
            )
            for c in range(parts):
                total = moved[c] + increment[:, c * LANES : (c + 1) * LANES]
                o_ref[c, i] = total.astype(jnp.bfloat16)

    size = parts * span[1] * block * LANES * 2
    return pl.pallas_call(
        kernel,
        out_shape=[jax.ShapeDtypeStruct(field.shape, field.dtype), token()],
        grid_spec=pltpu.PrefetchScalarGridSpec(
            num_scalar_prefetch=1,
            grid=(groups,),
            in_specs=[
                pl.BlockSpec((count, share, parts, ROWS, LANES), lambda g, *_: (0, 0, 0, g, 0))
            ]
            + radial_specs(parts, kinds, block, radial, b, halo_at, base)
            + anywhere(len(held) + len(after)),
            out_specs=[
                pl.BlockSpec((parts, ROWS, block, LANES), lambda g, *_: (0, g + base, b, 0))
            ]
            + anywhere(1),
            scratch_shapes=[pltpu.VMEM((parts, block * ROWS, LANES), jnp.float32)],
        ),
        input_output_aliases={8: 0} if held else {},
        compiler_params=params(),
        cost_estimate=cost(2 * size * block, 3 * size),
        name="analyze",
    )(order_map, piece, field, low, high, tables, curvature, walk_off, *held, *after)


def exchange(pieces):
    return lax.all_to_all(pieces, "ang", split_axis=0, concat_axis=0, tiled=True)


def spans_of(sizes):
    starts = [sum(sizes[:k]) for k in range(len(sizes))]
    return list(zip(starts, sizes, strict=True))


def pipelined(field, radial_tables, weights, order_map, curvature, walk_off):
    count = lax.axis_size("ang")
    orders = field.shape[1]
    nblocks, block = radial_tables.shape[1:3]
    forward, backward = (jnp.asarray(table) for table in angle_matrices(ORDERS))
    scaled = radial_tables.astype(jnp.float32) * weights.reshape(nblocks, block)[None, :, :, None]
    analysis = scaled.astype(jnp.bfloat16).transpose(0, 1, 3, 2)
    whole = spans_of([orders])
    head = spans_of([ROWS, orders - ROWS]) if orders > ROWS else whole
    tail = spans_of([orders // 2, orders // 4, orders // 4]) if orders % (4 * ROWS) == 0 else whole
    spans = {0: head}
    out_spans = {nblocks - 1: tail}
    after = ()
    halos, sent, returned = {}, {}, {}
    out = None

    def halo(first, some, span, after):
        ends, done = edges(field, first, some, block, span, after)
        low = lax.ppermute(ends, "tm", ring("tm", 1))
        high = lax.ppermute(ends, "tm", ring("tm", -1))
        return [(low, high, j) for j in range(some)], (done,)

    def points(b, span, ends, after):
        own, done = synthesize(
            field, ends, radial_tables, curvature, walk_off, order_map, b, count, span, after
        )
        sent.setdefault(b, []).append(exchange(own))
        return (done,)

    def turn(b, after):
        back, done = kerr_step(
            sent.pop(b), spans.get(b, whole), out_spans.get(b, whole), forward, backward, after
        )
        returned[b] = [exchange(group) for group in back]
        return (done,)

    def finish(b, out, after):
        for span, group in zip(out_spans.get(b, whole), returned.pop(b), strict=True):
            out, done = analyze(
                group, field, halos[b], analysis, curvature, walk_off, order_map, b, span,
                out, after,
            )
            after = (done,)
        return out, after

    early, after = halo(0, 1, head[0], after)
    (halos[0],), after = halo(0, 1, whole[0], after)
    for k, span in enumerate(head):
        after = points(0, span, early[0] if k == 0 else halos[0], after)
    (halos[1],), after = halo(1, 1, whole[0], after)
    after = points(1, whole[0], halos[1], after)
    if nblocks > 2:
        rest, after = halo(2, nblocks - 2, whole[0], after)
        halos.update(zip(range(2, nblocks), rest, strict=True))
    for b in range(nblocks):
        after = turn(b, after)
        if b >= 1:
            out, after = finish(b - 1, out, after)
        if b + 2 < nblocks:
            after = points(b + 2, whole[0], halos[b + 2], after)
    out, after = finish(nblocks - 1, out, after)
    return out


def with_halo(block, axis, dim):
    low = lax.ppermute(
        lax.slice_in_dim(block, block.shape[dim] - 1, None, axis=dim), axis, ring(axis, 1)
    )
    high = lax.ppermute(lax.slice_in_dim(block, 0, 1, axis=dim), axis, ring(axis, -1))
    return jnp.concatenate([low, block, high], axis=dim)


def local_kerr(pieces, forward, backward):
    orders = pieces.shape[1]
    flat = pieces.reshape(2 * orders, -1)
    angular = jnp.dot(forward, flat, preferred_element_type=jnp.float32)
    power = angular[:orders] ** 2 + angular[orders:] ** 2
    kerr = jnp.concatenate(
        [-kerr_gamma * power * angular[orders:], kerr_gamma * power * angular[:orders]], 0
    )
    kerr = kerr.astype(jnp.bfloat16)
    back = jnp.dot(backward, kerr, preferred_element_type=jnp.float32) * (1.0 / orders)
    return back.astype(jnp.bfloat16).reshape(pieces.shape)


def whole_arrays(field, radial_tables, weights, order_map, curvature, walk_off):
    local_orders, radial, steps_dev = field.shape[1:]
    nblocks, block = radial_tables.shape[1:3]
    padded = with_halo(field, "tm", 3).astype(jnp.float32)
    middle = padded[..., 1:-1]
    right = padded[..., 2:]
    left = padded[..., :-2]
    second = right - 2.0 * middle + left
    first = 0.5 * (right - left)
    beta = curvature[:, :, None]
    delta = walk_off[:, :, None]
    real = middle[0] - beta * second[1] + delta * first[0]
    imag = middle[1] + beta * second[0] + delta * first[1]
    moved = jnp.stack([real, imag])
    moved_low = moved.astype(jnp.bfloat16).reshape(2, local_orders, nblocks, block, steps_dev)
    tables = jnp.take(radial_tables, order_map, axis=0)
    scaled = radial_tables.astype(jnp.float32) * weights.reshape(nblocks, block)[None, :, :, None]
    analysis = jnp.take(scaled.astype(jnp.bfloat16), order_map, axis=0)
    points = jnp.einsum("mbqn,cmbnt->cmbqt", tables, moved_low, preferred_element_type=jnp.float32)
    points = points.reshape(2, local_orders, radial, steps_dev).astype(jnp.bfloat16)
    forward, backward = (jnp.asarray(table) for table in angle_matrices(ORDERS))
    back = local_kerr(
        lax.all_to_all(points, "ang", split_axis=2, concat_axis=1, tiled=True), forward, backward
    )
    returned = lax.all_to_all(back, "ang", split_axis=1, concat_axis=2, tiled=True)
    returned = returned.reshape(2, local_orders, nblocks, block, steps_dev)
    increment = jnp.einsum(
        "mbqn,cmbqt->cmbnt", analysis, returned, preferred_element_type=jnp.float32
    )
    increment = increment.reshape(2, local_orders, radial, steps_dev)
    return (moved + increment).astype(jnp.bfloat16)


def per_device(field, radial_tables, weights, order_map, curvature, walk_off):
    parts, orders, radial, steps = field.shape
    nblocks, block = radial_tables.shape[1:3]
    count = lax.axis_size("ang")
    fits = (
        steps == LANES
        and orders % ROWS == 0
        and 2 * orders <= LANES
        and block % (2 * count) == 0
        and radial % LANES == 0
        and LANES % block == 0
        and nblocks >= 2
    )
    plan = pipelined if fits else whole_arrays
    return plan(field, radial_tables, weights, order_map, curvature, walk_off)


def solution(mesh):
    in_specs = (P("groups", "ang", None, "tm"), P(), P(), P("ang"), P("ang", None), P("ang", None))
    out_specs = P("groups", "ang", None, "tm")
    return jax.shard_map(
        per_device, mesh=mesh, in_specs=in_specs, out_specs=out_specs, check_vma=False
    )
```

```python
import functools
import math

import jax
import jax.numpy as jnp
import numpy as np
from jax import lax
from jax.experimental import pallas as pl
from jax.experimental.pallas import tpu as pltpu
from jax.sharding import PartitionSpec as P

ORDERS = 256
LANES = 128
ROWS = 16

kerr_gamma = 0.00390625


def angle_matrices(count):
    index = np.arange(count, dtype=np.int32)
    phase = (index[:, None] * index[None, :] % count).astype(np.float32) * np.float32(
        2.0 * math.pi / count
    )
    cosine, sine = np.cos(phase), np.sin(phase)
    forward = np.block([[cosine, -sine], [sine, cosine]])
    backward = np.block([[cosine, sine], [-sine, cosine]])
    return forward.astype(jnp.bfloat16), backward.astype(jnp.bfloat16)


def ring(axis, shift):
    count = lax.axis_size(axis)
    return [(i, (i + shift) % count) for i in range(count)]


def lane_index(rows):
    return lax.broadcasted_iota(jnp.int32, (rows, LANES), 1)


def roll(x, shift):
    return pltpu.roll(x, shift, 1)


def params():
    return pltpu.CompilerParams(vmem_limit_bytes=40 * 1024 * 1024)


def cost(flops, size):
    return pl.CostEstimate(flops=flops, bytes_accessed=size, transcendentals=0)


def anywhere(count):
    return [pl.BlockSpec(memory_space=pl.ANY)] * count


def token():
    return jax.ShapeDtypeStruct((8, LANES), jnp.float32)


def edges(field, first, count, block, span, after):
    parts = field.shape[0]
    base, groups = span[0] // ROWS, span[1] // ROWS

    def kernel(x_ref, *refs):
        o_ref, _, acc = refs[-3:]
        g = pl.program_id(1)
        slot = ((lane_index(block) + 1) >> 1) & (LANES // 2 - 1)
        for c in range(parts):
            kept = acc[c]
            for i in range(ROWS):
                m = (g + base) * ROWS + i
                row = roll(x_ref[c, i].astype(jnp.float32), 2 * m)
                kept = jnp.where(slot == m, row, kept)
            acc[c] = kept

        @pl.when(g == groups - 1)
        def _():
            o_ref[...] = acc[...].astype(o_ref.dtype)

    return pl.pallas_call(
        kernel,
        out_shape=[
            jax.ShapeDtypeStruct((parts, count * block, LANES), field.dtype),
            token(),
        ],
        grid=(count, groups),
        in_specs=[
            pl.BlockSpec((parts, ROWS, block, LANES), lambda j, g: (0, g + base, j + first, 0))
        ]
        + anywhere(len(after)),
        out_specs=[pl.BlockSpec((parts, block, LANES), lambda j, g: (0, j, 0))] + anywhere(1),
        scratch_shapes=[pltpu.VMEM((parts, block, LANES), jnp.float32)],
        compiler_params=params(),
        cost_estimate=cost(0, parts * span[1] * count * block * LANES * 2),
        name="edges",
    )(field, *after)


def join_halo(low, high):
    lane = lane_index(low.shape[0])
    low, high = low.astype(jnp.float32), high.astype(jnp.float32)
    return jnp.where((lane & 1) == 0, roll(low, 1), roll(high, LANES - 1))


def columns(ref, start, block):
    base = start // LANES * LANES
    turned = jnp.transpose(ref[:, base : base + LANES])
    return turned[start - base : start - base + block]


def move(x, halo, beta, delta, m):
    lane = lane_index(beta.shape[0])
    second, first = [], []
    for c in range(2):
        ends = roll(halo[c], (LANES - 2 * m) & (LANES - 1))
        left = jnp.where(lane == 0, ends, roll(x[c], 1))
        right = jnp.where(lane == LANES - 1, ends, roll(x[c], LANES - 1))
        second.append(right - 2.0 * x[c] + left)
        first.append(0.5 * (right - left))
    real = x[0] - beta * second[1] + delta * first[0]
    imag = x[1] + beta * second[0] + delta * first[1]
    return real, imag


def radial_specs(parts, kinds, block, radial, b, halo_at, base):
    return [
        pl.BlockSpec((parts, ROWS, block, LANES), lambda g, *_: (0, g + base, b, 0)),
        pl.BlockSpec((parts, block, LANES), lambda g, *_: (0, halo_at, 0)),
        pl.BlockSpec((parts, block, LANES), lambda g, *_: (0, halo_at, 0)),
        pl.BlockSpec((kinds, 1, block, block), lambda g, *_: (0, b, 0, 0)),
        pl.BlockSpec((ROWS, radial), lambda g, *_: (g + base, 0)),
        pl.BlockSpec((ROWS, radial), lambda g, *_: (g + base, 0)),
    ]


def synthesize(field, halo, tables, curvature, walk_off, order_map, me, b, count, span, after):
    low, high, halo_at = halo
    parts, _, radial, _ = field.shape
    kinds, _, block, _ = tables.shape
    share = block // count
    base, groups = span[0] // ROWS, span[1] // ROWS

    def kernel(map_ref, me_ref, x_ref, low_ref, high_ref, tab_ref, beta_ref, delta_ref, *refs):
        outs, acc = refs[len(after) : len(after) + count], refs[-1]
        g = pl.program_id(0)
        beta = columns(beta_ref, b * block, block)
        delta = columns(delta_ref, b * block, block)
        ends = [join_halo(low_ref[c], high_ref[c]) for c in range(parts)]
        for i in range(ROWS):
            m = (g + base) * ROWS + i
            x = [x_ref[c, i].astype(jnp.float32) for c in range(parts)]
            moved = move(x, ends, beta[:, i : i + 1], delta[:, i : i + 1], m)
            moved = jnp.concatenate(moved, 1).astype(jnp.bfloat16)
            points = jnp.dot(
                tab_ref[map_ref[m], 0], moved, preferred_element_type=jnp.float32
            )
            for c in range(parts):
                acc[c, pl.ds(i, block, stride=ROWS), :] = points[:, c * LANES : (c + 1) * LANES]
        for s in range(count):
            owner = lax.rem(me_ref[0] + s, count)
            for q in range(share):
                row = pl.multiple_of((owner * share + q) * ROWS, ROWS)
                for c in range(parts):
                    outs[s][q, c] = acc[c, pl.ds(row, ROWS), :].astype(jnp.bfloat16)

    piece = jax.ShapeDtypeStruct((share, parts, span[1], LANES), jnp.bfloat16)
    size = parts * span[1] * block * LANES * 2
    *pieces, done = pl.pallas_call(
        kernel,
        out_shape=[piece] * count + [token()],
        grid_spec=pltpu.PrefetchScalarGridSpec(
            num_scalar_prefetch=2,
            grid=(groups,),
            in_specs=radial_specs(parts, kinds, block, radial, b, halo_at, base)
            + anywhere(len(after)),
            out_specs=[
                pl.BlockSpec((share, parts, ROWS, LANES), lambda g, *_: (0, 0, g, 0))
            ]
            * count
            + anywhere(1),
            scratch_shapes=[pltpu.VMEM((parts, block * ROWS, LANES), jnp.float32)],
        ),
        compiler_params=params(),
        cost_estimate=cost(2 * size * block, 2 * size),
        name="synthesize",
    )(order_map, me, field, low, high, tables, curvature, walk_off, *after)
    return pieces, done


def kerr_step(pieces, spans, out_spans, forward, backward, me, after):
    count = len(pieces[0])
    share, parts = pieces[0][0].shape[:2]
    orders = sum(size for _, size in spans)
    every = count * orders
    width = 2
    ins_count, outs_count = count * len(spans), count * len(out_spans)

    def kernel(me_ref, f_ref, b_ref, *refs):
        ins = refs[:ins_count]
        outs = refs[ins_count + len(after) : ins_count + len(after) + outs_count]
        flat, back = refs[-2:]
        for k, (start, size) in enumerate(spans):
            for s in range(count):
                source = lax.rem(me_ref[0] + count - s, count)
                for c in range(parts):
                    row = pl.multiple_of(c * every + source * orders + start, ROWS)
                    for q in range(width):
                        flat[pl.ds(row, size), q * LANES : (q + 1) * LANES] = ins[
                            k * count + s
                        ][q, c]
        angular = jnp.dot(f_ref[...], flat[...], preferred_element_type=jnp.float32)
        real, imag = angular[:every], angular[every:]
        power = kerr_gamma * (real * real + imag * imag)
        kerr = jnp.concatenate([-power * imag, power * real], 0).astype(jnp.bfloat16)
        back[...] = (
            jnp.dot(b_ref[...], kerr, preferred_element_type=jnp.float32) * (1.0 / every)
        ).astype(jnp.bfloat16)
        for k, (start, size) in enumerate(out_spans):
            for s in range(count):
                owner = lax.rem(me_ref[0] + s, count)
                for c in range(parts):
                    row = pl.multiple_of(c * every + owner * orders + start, ROWS)
                    for q in range(width):
                        outs[k * count + s][q, c] = back[
                            pl.ds(row, size), q * LANES : (q + 1) * LANES
                        ]

    def blocks(some):
        return [
            pl.BlockSpec((width, parts, size, LANES), lambda q, *_: (q, 0, 0, 0))
            for _, size in some
            for _ in range(count)
        ]

    whole = pl.BlockSpec((parts * every, parts * every), lambda q, *_: (0, 0))
    lanes = share * LANES
    *back, done = pl.pallas_call(
        kernel,
        out_shape=[
            jax.ShapeDtypeStruct((share, parts, size, LANES), jnp.bfloat16)
            for _, size in out_spans
            for _ in range(count)
        ]
        + [token()],
        grid_spec=pltpu.PrefetchScalarGridSpec(
            num_scalar_prefetch=1,
            grid=(share // width,),
            in_specs=[whole, whole] + blocks(spans) + anywhere(len(after)),
            out_specs=blocks(out_spans) + anywhere(1),
            scratch_shapes=[
                pltpu.VMEM((parts * every, width * LANES), jnp.bfloat16),
                pltpu.VMEM((parts * every, width * LANES), jnp.bfloat16),
            ],
        ),
        compiler_params=params(),
        cost_estimate=cost(4 * (parts * every) ** 2 * lanes, 4 * parts * every * lanes),
        name="kerr",
    )(me, forward, backward, *(piece for group in pieces for piece in group), *after)
    return [back[k * count : (k + 1) * count] for k in range(len(out_spans))], done


def analyze(
    pieces, field, halo, tables, curvature, walk_off, order_map, me, b, span, out, after
):
    low, high, halo_at = halo
    count = len(pieces)
    parts, _, radial, _ = field.shape
    kinds, _, block, _ = tables.shape
    share = block // count
    base, groups = span[0] // ROWS, span[1] // ROWS
    held = () if out is None else (out,)

    def kernel(map_ref, me_ref, *refs):
        ins = refs[:count]
        x_ref, low_ref, high_ref, tab_ref, beta_ref, delta_ref = refs[count : count + 6]
        o_ref, _, acc = refs[-3:]
        g = pl.program_id(0)
        for s in range(count):
            source = lax.rem(me_ref[0] + count - s, count)
            for q in range(share):
                row = pl.multiple_of((source * share + q) * ROWS, ROWS)
                for c in range(parts):
                    acc[c, pl.ds(row, ROWS), :] = ins[s][q, c].astype(jnp.float32)
        beta = columns(beta_ref, b * block, block)
        delta = columns(delta_ref, b * block, block)
        ends = [join_halo(low_ref[c], high_ref[c]) for c in range(parts)]
        for i in range(ROWS):
            m = (g + base) * ROWS + i
            x = [x_ref[c, i].astype(jnp.float32) for c in range(parts)]
            moved = move(x, ends, beta[:, i : i + 1], delta[:, i : i + 1], m)
            back = [acc[c, pl.ds(i, block, stride=ROWS), :] for c in range(parts)]
            back = jnp.concatenate(back, 1).astype(jnp.bfloat16)
            increment = jnp.dot(
                tab_ref[map_ref[m], 0], back, preferred_element_type=jnp.float32
            )
            for c in range(parts):
                total = moved[c] + increment[:, c * LANES : (c + 1) * LANES]
                o_ref[c, i] = total.astype(jnp.bfloat16)

    size = parts * span[1] * block * LANES * 2
    return pl.pallas_call(
        kernel,
        out_shape=[jax.ShapeDtypeStruct(field.shape, field.dtype), token()],
        grid_spec=pltpu.PrefetchScalarGridSpec(
            num_scalar_prefetch=2,
            grid=(groups,),
            in_specs=[
                pl.BlockSpec((share, parts, ROWS, LANES), lambda g, *_: (0, 0, g, 0))
            ]
            * count
            + radial_specs(parts, kinds, block, radial, b, halo_at, base)
            + anywhere(len(held) + len(after)),
            out_specs=[
                pl.BlockSpec((parts, ROWS, block, LANES), lambda g, *_: (0, g + base, b, 0))
            ]
            + anywhere(1),
            scratch_shapes=[pltpu.VMEM((parts, block * ROWS, LANES), jnp.float32)],
        ),
        input_output_aliases={2 + count + 6: 0} if held else {},
        compiler_params=params(),
        cost_estimate=cost(2 * size * block, 3 * size),
        name="analyze",
    )(
        order_map, me, *pieces, field, low, high, tables, curvature, walk_off, *held, *after
    )


def exchange(pieces):
    return [pieces[0]] + [
        lax.ppermute(pieces[s], "ang", ring("ang", s)) for s in range(1, len(pieces))
    ]


def spans_of(sizes):
    starts = [sum(sizes[:k]) for k in range(len(sizes))]
    return list(zip(starts, sizes, strict=True))


def pipelined(field, radial_tables, weights, order_map, curvature, walk_off):
    count = lax.axis_size("ang")
    orders = field.shape[1]
    nblocks, block = radial_tables.shape[1:3]
    me = lax.axis_index("ang").astype(jnp.int32).reshape(1)
    forward, backward = (jnp.asarray(table) for table in angle_matrices(ORDERS))
    scaled = radial_tables.astype(jnp.float32) * weights.reshape(nblocks, block)[None, :, :, None]
    analysis = scaled.astype(jnp.bfloat16).transpose(0, 1, 3, 2)
    whole = spans_of([orders])
    tail = spans_of([orders - ROWS, ROWS]) if orders > ROWS else whole
    spans = {}
    out_spans = {nblocks - 1: tail}
    after = ()
    halos, sent, returned = {}, {}, {}
    out = None

    def halo(first, some, span, after):
        ends, done = edges(field, first, some, block, span, after)
        low = lax.ppermute(ends, "tm", ring("tm", 1))
        high = lax.ppermute(ends, "tm", ring("tm", -1))
        return [(low, high, j) for j in range(some)], (done,)

    def points(b, span, ends, after):
        own, done = synthesize(
            field, ends, radial_tables, curvature, walk_off, order_map, me, b, count, span, after
        )
        sent.setdefault(b, []).append(exchange(own))
        return (done,)

    def turn(b, after):
        back, done = kerr_step(
            sent.pop(b), spans.get(b, whole), out_spans.get(b, whole), forward, backward, me, after
        )
        returned[b] = [exchange(group) for group in back]
        return (done,)

    def finish(b, out, after):
        for span, group in zip(out_spans.get(b, whole), returned.pop(b), strict=True):
            out, done = analyze(
                group, field, halos[b], analysis, curvature, walk_off, order_map, me, b, span,
                out, after,
            )
            after = (done,)
        return out, after

    (halos[0],), after = halo(0, 1, whole[0], after)
    after = points(0, whole[0], halos[0], after)
    (halos[1],), after = halo(1, 1, whole[0], after)
    after = points(1, whole[0], halos[1], after)
    if nblocks > 2:
        rest, after = halo(2, nblocks - 2, whole[0], after)
        halos.update(zip(range(2, nblocks), rest, strict=True))
    for b in range(nblocks):
        if b >= nblocks - 1:
            after = after + tuple(returned[b - 1][0][1:2])
        after = turn(b, after)
        if b >= 1:
            out, after = finish(b - 1, out, after)
        if b + 2 < nblocks:
            after = points(b + 2, whole[0], halos[b + 2], after)
    out, after = finish(nblocks - 1, out, after)
    return out


def with_halo(block, axis, dim):
    low = lax.ppermute(
        lax.slice_in_dim(block, block.shape[dim] - 1, None, axis=dim), axis, ring(axis, 1)
    )
    high = lax.ppermute(lax.slice_in_dim(block, 0, 1, axis=dim), axis, ring(axis, -1))
    return jnp.concatenate([low, block, high], axis=dim)


def local_kerr(pieces, forward, backward):
    orders = pieces.shape[1]
    flat = pieces.reshape(2 * orders, -1)
    angular = jnp.dot(forward, flat, preferred_element_type=jnp.float32)
    power = angular[:orders] ** 2 + angular[orders:] ** 2
    kerr = jnp.concatenate(
        [-kerr_gamma * power * angular[orders:], kerr_gamma * power * angular[:orders]], 0
    )
    kerr = kerr.astype(jnp.bfloat16)
    back = jnp.dot(backward, kerr, preferred_element_type=jnp.float32) * (1.0 / orders)
    return back.astype(jnp.bfloat16).reshape(pieces.shape)


def whole_arrays(field, radial_tables, weights, order_map, curvature, walk_off):
    local_orders, radial, steps_dev = field.shape[1:]
    nblocks, block = radial_tables.shape[1:3]
    padded = with_halo(field, "tm", 3).astype(jnp.float32)
    middle = padded[..., 1:-1]
    right = padded[..., 2:]
    left = padded[..., :-2]
    second = right - 2.0 * middle + left
    first = 0.5 * (right - left)
    beta = curvature[:, :, None]
    delta = walk_off[:, :, None]
    real = middle[0] - beta * second[1] + delta * first[0]
    imag = middle[1] + beta * second[0] + delta * first[1]
    moved = jnp.stack([real, imag])
    moved_low = moved.astype(jnp.bfloat16).reshape(2, local_orders, nblocks, block, steps_dev)
    tables = jnp.take(radial_tables, order_map, axis=0)
    scaled = radial_tables.astype(jnp.float32) * weights.reshape(nblocks, block)[None, :, :, None]
    analysis = jnp.take(scaled.astype(jnp.bfloat16), order_map, axis=0)
    points = jnp.einsum("mbqn,cmbnt->cmbqt", tables, moved_low, preferred_element_type=jnp.float32)
    points = points.reshape(2, local_orders, radial, steps_dev).astype(jnp.bfloat16)
    forward, backward = (jnp.asarray(table) for table in angle_matrices(ORDERS))
    back = local_kerr(
        lax.all_to_all(points, "ang", split_axis=2, concat_axis=1, tiled=True), forward, backward
    )
    returned = lax.all_to_all(back, "ang", split_axis=1, concat_axis=2, tiled=True)
    returned = returned.reshape(2, local_orders, nblocks, block, steps_dev)
    increment = jnp.einsum(
        "mbqn,cmbqt->cmbnt", analysis, returned, preferred_element_type=jnp.float32
    )
    increment = increment.reshape(2, local_orders, radial, steps_dev)
    return (moved + increment).astype(jnp.bfloat16)


def per_device(field, radial_tables, weights, order_map, curvature, walk_off):
    parts, orders, radial, steps = field.shape
    nblocks, block = radial_tables.shape[1:3]
    count = lax.axis_size("ang")
    fits = (
        steps == LANES
        and orders % ROWS == 0
        and 2 * orders <= LANES
        and block % (2 * count) == 0
        and radial % LANES == 0
        and LANES % block == 0
        and nblocks >= 2
    )
    plan = pipelined if fits else whole_arrays
    return plan(field, radial_tables, weights, order_map, curvature, walk_off)


def solution(mesh):
    in_specs = (P("groups", "ang", None, "tm"), P(), P(), P("ang"), P("ang", None), P("ang", None))
    out_specs = P("groups", "ang", None, "tm")
    return jax.shard_map(
        per_device, mesh=mesh, in_specs=in_specs, out_specs=out_specs, check_vma=False
    )
```

```python
import functools
import math

import jax
import jax.numpy as jnp
import numpy as np
from jax import lax
from jax.experimental import pallas as pl
from jax.experimental.pallas import tpu as pltpu
from jax.sharding import PartitionSpec as P

ORDERS = 256
LANES = 128
ROWS = 16

kerr_gamma = 0.00390625


def angle_matrices(count):
    index = np.arange(count, dtype=np.int32)
    phase = (index[:, None] * index[None, :] % count).astype(np.float32) * np.float32(
        2.0 * math.pi / count
    )
    cosine, sine = np.cos(phase), np.sin(phase)
    forward = np.block([[cosine, -sine], [sine, cosine]])
    backward = np.block([[cosine, sine], [-sine, cosine]])
    return forward.astype(jnp.bfloat16), backward.astype(jnp.bfloat16)


def ring(axis, shift):
    count = lax.axis_size(axis)
    return [(i, (i + shift) % count) for i in range(count)]


def lane_index(rows):
    return lax.broadcasted_iota(jnp.int32, (rows, LANES), 1)


def roll(x, shift):
    return pltpu.roll(x, shift, 1)


def params():
    return pltpu.CompilerParams(vmem_limit_bytes=40 * 1024 * 1024)


def cost(flops, size):
    return pl.CostEstimate(flops=flops, bytes_accessed=size, transcendentals=0)


def anywhere(count):
    return [pl.BlockSpec(memory_space=pl.ANY)] * count


def token():
    return jax.ShapeDtypeStruct((8, LANES), jnp.float32)


def edges(field, first, count, block, span, after):
    parts = field.shape[0]
    base, groups = span[0] // ROWS, span[1] // ROWS

    def kernel(x_ref, *refs):
        o_ref, _, acc = refs[-3:]
        g = pl.program_id(1)
        slot = ((lane_index(block) + 1) >> 1) & (LANES // 2 - 1)
        for c in range(parts):
            kept = acc[c]
            for i in range(ROWS):
                m = (g + base) * ROWS + i
                row = roll(x_ref[c, i].astype(jnp.float32), 2 * m)
                kept = jnp.where(slot == m, row, kept)
            acc[c] = kept

        @pl.when(g == groups - 1)
        def _():
            o_ref[...] = acc[...].astype(o_ref.dtype)

    return pl.pallas_call(
        kernel,
        out_shape=[
            jax.ShapeDtypeStruct((parts, count * block, LANES), field.dtype),
            token(),
        ],
        grid=(count, groups),
        in_specs=[
            pl.BlockSpec((parts, ROWS, block, LANES), lambda j, g: (0, g + base, j + first, 0))
        ]
        + anywhere(len(after)),
        out_specs=[pl.BlockSpec((parts, block, LANES), lambda j, g: (0, j, 0))] + anywhere(1),
        scratch_shapes=[pltpu.VMEM((parts, block, LANES), jnp.float32)],
        compiler_params=params(),
        cost_estimate=cost(0, parts * span[1] * count * block * LANES * 2),
        name="edges",
    )(field, *after)


def join_halo(low, high):
    lane = lane_index(low.shape[0])
    low, high = low.astype(jnp.float32), high.astype(jnp.float32)
    return jnp.where((lane & 1) == 0, roll(low, 1), roll(high, LANES - 1))


def columns(ref, start, block):
    base = start // LANES * LANES
    turned = jnp.transpose(ref[:, base : base + LANES])
    return turned[start - base : start - base + block]


def move(x, halo, beta, delta, m):
    lane = lane_index(beta.shape[0])
    second, first = [], []
    for c in range(2):
        ends = roll(halo[c], (LANES - 2 * m) & (LANES - 1))
        left = jnp.where(lane == 0, ends, roll(x[c], 1))
        right = jnp.where(lane == LANES - 1, ends, roll(x[c], LANES - 1))
        second.append(right - 2.0 * x[c] + left)
        first.append(0.5 * (right - left))
    real = x[0] - beta * second[1] + delta * first[0]
    imag = x[1] + beta * second[0] + delta * first[1]
    return real, imag


def radial_specs(parts, kinds, block, radial, b, halo_at, base):
    return [
        pl.BlockSpec((parts, ROWS, block, LANES), lambda g, *_: (0, g + base, b, 0)),
        pl.BlockSpec((parts, block, LANES), lambda g, *_: (0, halo_at, 0)),
        pl.BlockSpec((parts, block, LANES), lambda g, *_: (0, halo_at, 0)),
        pl.BlockSpec((kinds, 1, block, block), lambda g, *_: (0, b, 0, 0)),
        pl.BlockSpec((ROWS, radial), lambda g, *_: (g + base, 0)),
        pl.BlockSpec((ROWS, radial), lambda g, *_: (g + base, 0)),
    ]


def synthesize(
    field, halo, tables, curvature, walk_off, order_map, me, b, count, span, after,
    apart=(), held=(),
):
    low, high, halo_at = halo
    parts, orders, radial, _ = field.shape
    kinds, _, block, _ = tables.shape
    share = block // count
    base, groups = span[0] // ROWS, span[1] // ROWS

    def kernel(map_ref, me_ref, x_ref, low_ref, high_ref, tab_ref, beta_ref, delta_ref, *refs):
        outs, acc = refs[-count - 2 : -2], refs[-1]
        g = pl.program_id(0)
        beta = columns(beta_ref, b * block, block)
        delta = columns(delta_ref, b * block, block)
        ends = [join_halo(low_ref[c], high_ref[c]) for c in range(parts)]
        for i in range(ROWS):
            m = (g + base) * ROWS + i
            x = [x_ref[c, i].astype(jnp.float32) for c in range(parts)]
            moved = move(x, ends, beta[:, i : i + 1], delta[:, i : i + 1], m)
            moved = jnp.concatenate(moved, 1).astype(jnp.bfloat16)
            points = jnp.dot(
                tab_ref[map_ref[m], 0], moved, preferred_element_type=jnp.float32
            )
            for c in range(parts):
                acc[c, pl.ds(i, block, stride=ROWS), :] = points[:, c * LANES : (c + 1) * LANES]
        for s in range(count):
            owner = lax.rem(me_ref[0] + s, count)
            for q in range(share):
                row = pl.multiple_of((owner * share + q) * ROWS, ROWS)
                for c in range(parts):
                    outs[s][q, c] = acc[c, pl.ds(row, ROWS), :].astype(jnp.bfloat16)

    def piece(s):
        room = span[1] if s in apart else orders
        return jax.ShapeDtypeStruct((share, parts, room, LANES), jnp.bfloat16)

    def place(s):
        first = 0 if s in apart else base
        return pl.BlockSpec((share, parts, ROWS, LANES), lambda g, *_: (0, 0, g + first, 0))

    joined = [s for s in range(count) if s not in apart]
    size = parts * span[1] * block * LANES * 2
    return pl.pallas_call(
        kernel,
        out_shape=[piece(s) for s in range(count)] + [token()],
        grid_spec=pltpu.PrefetchScalarGridSpec(
            num_scalar_prefetch=2,
            grid=(groups,),
            in_specs=radial_specs(parts, kinds, block, radial, b, halo_at, base)
            + anywhere(len(held) + len(after)),
            out_specs=[place(s) for s in range(count)] + anywhere(1),
            scratch_shapes=[pltpu.VMEM((parts, block * ROWS, LANES), jnp.float32)],
        ),
        input_output_aliases={8 + k: s for k, s in enumerate(joined)} if held else {},
        compiler_params=params(),
        cost_estimate=cost(2 * size * block, 2 * size),
        name="synthesize",
    )(order_map, me, field, low, high, tables, curvature, walk_off, *held, *after)


def kerr_step(pieces, out_spans, forward, backward, me, count, after):
    share, parts = pieces[0][0].shape[:2]
    orders = sum(size for _, size in out_spans)
    every = count * orders
    width = 2
    outs_count = count * len(out_spans)

    def kernel(me_ref, f_ref, b_ref, *refs):
        ins, outs = refs[: len(pieces)], refs[-outs_count - 3 : -3]
        flat, back = refs[-2:]
        for piece, (_, s, (start, size)) in zip(ins, pieces, strict=True):
            source = lax.rem(me_ref[0] + count - s, count)
            for c in range(parts):
                row = pl.multiple_of(c * every + source * orders + start, ROWS)
                for q in range(width):
                    flat[pl.ds(row, size), q * LANES : (q + 1) * LANES] = piece[q, c]
        angular = jnp.dot(f_ref[...], flat[...], preferred_element_type=jnp.float32)
        real, imag = angular[:every], angular[every:]
        power = kerr_gamma * (real * real + imag * imag)
        kerr = jnp.concatenate([-power * imag, power * real], 0).astype(jnp.bfloat16)
        back[...] = (
            jnp.dot(b_ref[...], kerr, preferred_element_type=jnp.float32) * (1.0 / every)
        ).astype(jnp.bfloat16)
        for k, (start, size) in enumerate(out_spans):
            for s in range(count):
                owner = lax.rem(me_ref[0] + s, count)
                for c in range(parts):
                    row = pl.multiple_of(c * every + owner * orders + start, ROWS)
                    for q in range(width):
                        outs[k * count + s][q, c] = back[
                            pl.ds(row, size), q * LANES : (q + 1) * LANES
                        ]

    def rows(size):
        return pl.BlockSpec((width, parts, size, LANES), lambda q, *_: (q, 0, 0, 0))

    whole = pl.BlockSpec((parts * every, parts * every), lambda q, *_: (0, 0))
    lanes = share * LANES
    *back, done = pl.pallas_call(
        kernel,
        out_shape=[
            jax.ShapeDtypeStruct((share, parts, size, LANES), jnp.bfloat16)
            for _, size in out_spans
            for _ in range(count)
        ]
        + [token()],
        grid_spec=pltpu.PrefetchScalarGridSpec(
            num_scalar_prefetch=1,
            grid=(share // width,),
            in_specs=[whole, whole]
            + [rows(size) for _, _, (_, size) in pieces]
            + anywhere(len(after)),
            out_specs=[rows(size) for _, size in out_spans for _ in range(count)] + anywhere(1),
            scratch_shapes=[
                pltpu.VMEM((parts * every, width * LANES), jnp.bfloat16),
                pltpu.VMEM((parts * every, width * LANES), jnp.bfloat16),
            ],
        ),
        compiler_params=params(),
        cost_estimate=cost(4 * (parts * every) ** 2 * lanes, 4 * parts * every * lanes),
        name="kerr",
    )(me, forward, backward, *(piece for piece, _, _ in pieces), *after)
    return [back[k * count : (k + 1) * count] for k in range(len(out_spans))], done


def analyze(
    pieces, field, halo, tables, curvature, walk_off, order_map, me, b, span, out, after
):
    low, high, halo_at = halo
    count = len(pieces)
    parts, _, radial, _ = field.shape
    kinds, _, block, _ = tables.shape
    share = block // count
    base, groups = span[0] // ROWS, span[1] // ROWS
    held = () if out is None else (out,)

    def kernel(map_ref, me_ref, *refs):
        ins = refs[:count]
        x_ref, low_ref, high_ref, tab_ref, beta_ref, delta_ref = refs[count : count + 6]
        o_ref, _, acc = refs[-3:]
        g = pl.program_id(0)
        for s in range(count):
            source = lax.rem(me_ref[0] + count - s, count)
            for q in range(share):
                row = pl.multiple_of((source * share + q) * ROWS, ROWS)
                for c in range(parts):
                    acc[c, pl.ds(row, ROWS), :] = ins[s][q, c].astype(jnp.float32)
        beta = columns(beta_ref, b * block, block)
        delta = columns(delta_ref, b * block, block)
        ends = [join_halo(low_ref[c], high_ref[c]) for c in range(parts)]
        for i in range(ROWS):
            m = (g + base) * ROWS + i
            x = [x_ref[c, i].astype(jnp.float32) for c in range(parts)]
            moved = move(x, ends, beta[:, i : i + 1], delta[:, i : i + 1], m)
            back = [acc[c, pl.ds(i, block, stride=ROWS), :] for c in range(parts)]
            back = jnp.concatenate(back, 1).astype(jnp.bfloat16)
            increment = jnp.dot(
                tab_ref[map_ref[m], 0], back, preferred_element_type=jnp.float32
            )
            for c in range(parts):
                total = moved[c] + increment[:, c * LANES : (c + 1) * LANES]
                o_ref[c, i] = total.astype(jnp.bfloat16)

    size = parts * span[1] * block * LANES * 2
    return pl.pallas_call(
        kernel,
        out_shape=[jax.ShapeDtypeStruct(field.shape, field.dtype), token()],
        grid_spec=pltpu.PrefetchScalarGridSpec(
            num_scalar_prefetch=2,
            grid=(groups,),
            in_specs=[
                pl.BlockSpec((share, parts, ROWS, LANES), lambda g, *_: (0, 0, g, 0))
            ]
            * count
            + radial_specs(parts, kinds, block, radial, b, halo_at, base)
            + anywhere(len(held) + len(after)),
            out_specs=[
                pl.BlockSpec((parts, ROWS, block, LANES), lambda g, *_: (0, g + base, b, 0))
            ]
            + anywhere(1),
            scratch_shapes=[pltpu.VMEM((parts, block * ROWS, LANES), jnp.float32)],
        ),
        input_output_aliases={2 + count + 6: 0} if held else {},
        compiler_params=params(),
        cost_estimate=cost(2 * size * block, 3 * size),
        name="analyze",
    )(
        order_map, me, *pieces, field, low, high, tables, curvature, walk_off, *held, *after
    )


def gate(arrays, before):
    def kernel(*refs):
        pass

    return pl.pallas_call(
        kernel,
        out_shape=[jax.ShapeDtypeStruct(x.shape, x.dtype) for x in arrays] + [token()],
        in_specs=anywhere(len(arrays) + len(before)),
        out_specs=anywhere(len(arrays) + 1),
        input_output_aliases={k: k for k in range(len(arrays))},
        compiler_params=params(),
        name="gate",
    )(*arrays, *before)


def step(piece, s):
    return lax.ppermute(piece, "ang", ring("ang", s)) if s else piece


def exchange(pieces):
    return [step(piece, s) for s, piece in enumerate(pieces)]


def spans_of(sizes):
    starts = [sum(sizes[:k]) for k in range(len(sizes))]
    return list(zip(starts, sizes, strict=True))


def pipelined(field, radial_tables, weights, order_map, curvature, walk_off):
    count = lax.axis_size("ang")
    orders = field.shape[1]
    nblocks, block = radial_tables.shape[1:3]
    me = lax.axis_index("ang").astype(jnp.int32).reshape(1)
    forward, backward = (jnp.asarray(table) for table in angle_matrices(ORDERS))
    scaled = radial_tables.astype(jnp.float32) * weights.reshape(nblocks, block)[None, :, :, None]
    analysis = scaled.astype(jnp.bfloat16).transpose(0, 1, 3, 2)
    whole = spans_of([orders])
    tail = spans_of([orders - ROWS, ROWS])
    out_spans = {nblocks - 1: tail}
    after = ()
    halos, sent, returned = {}, {}, {}
    out = None

    def halo(first, some, span, after):
        ends, done = edges(field, first, some, block, span, after)
        low = lax.ppermute(ends, "tm", ring("tm", 1))
        high = lax.ppermute(ends, "tm", ring("tm", -1))
        return [(low, high, j) for j in range(some)], (done,)

    def radial_points(b, span, ends, after, **how):
        *own, done = synthesize(
            field, ends, radial_tables, curvature, walk_off, order_map, me, b, count, span, after,
            **how,
        )
        return own, (done,)

    def points(b, after):
        own, after = radial_points(b, whole[0], halos[b], after)
        sent[b] = [(piece, s, whole[0]) for s, piece in enumerate(exchange(own))]
        return after

    def first_points(after):
        early, late = (0, ROWS), (ROWS, orders - ROWS)
        far = count // 2
        (ends,), after = halo(0, 1, early, after)
        (halos[0],), after = halo(0, 1, whole[0], after)
        own, after = radial_points(0, early, ends, after, apart=(far,))
        ahead = step(own.pop(far), far)
        own, after = radial_points(0, late, halos[0], after, apart=(far,), held=tuple(own))
        *own, done = gate(own, (ahead,) + after)
        after = (done,)
        sent[0] = [
            (piece, s, late if s == far else whole[0]) for s, piece in enumerate(exchange(own))
        ]
        sent[0].append((ahead, far, early))
        return after

    def turn(b, after):
        back, done = kerr_step(
            sent.pop(b), out_spans.get(b, whole), forward, backward, me, count, after
        )
        returned[b] = [exchange(group) for group in back]
        return (done,)

    def finish(b, out, after):
        for span, group in zip(out_spans.get(b, whole), returned.pop(b), strict=True):
            out, done = analyze(
                group, field, halos[b], analysis, curvature, walk_off, order_map, me, b, span,
                out, after,
            )
            after = (done,)
        return out, after

    after = first_points(after)
    (halos[1],), after = halo(1, 1, whole[0], after)
    after = points(1, after)
    if nblocks > 2:
        rest, after = halo(2, nblocks - 2, whole[0], after)
        halos.update(zip(range(2, nblocks), rest, strict=True))
    for b in range(nblocks):
        if b >= nblocks - 1:
            after = after + tuple(returned[b - 1][0][1:2])
        after = turn(b, after)
        if b >= 1:
            out, after = finish(b - 1, out, after)
        if b + 2 < nblocks:
            after = points(b + 2, after)
    out, after = finish(nblocks - 1, out, after)
    return out


def with_halo(block, axis, dim):
    low = lax.ppermute(
        lax.slice_in_dim(block, block.shape[dim] - 1, None, axis=dim), axis, ring(axis, 1)
    )
    high = lax.ppermute(lax.slice_in_dim(block, 0, 1, axis=dim), axis, ring(axis, -1))
    return jnp.concatenate([low, block, high], axis=dim)


def local_kerr(pieces, forward, backward):
    orders = pieces.shape[1]
    flat = pieces.reshape(2 * orders, -1)
    angular = jnp.dot(forward, flat, preferred_element_type=jnp.float32)
    power = angular[:orders] ** 2 + angular[orders:] ** 2
    kerr = jnp.concatenate(
        [-kerr_gamma * power * angular[orders:], kerr_gamma * power * angular[:orders]], 0
    )
    kerr = kerr.astype(jnp.bfloat16)
    back = jnp.dot(backward, kerr, preferred_element_type=jnp.float32) * (1.0 / orders)
    return back.astype(jnp.bfloat16).reshape(pieces.shape)


def whole_arrays(field, radial_tables, weights, order_map, curvature, walk_off):
    local_orders, radial, steps_dev = field.shape[1:]
    nblocks, block = radial_tables.shape[1:3]
    padded = with_halo(field, "tm", 3).astype(jnp.float32)
    middle = padded[..., 1:-1]
    right = padded[..., 2:]
    left = padded[..., :-2]
    second = right - 2.0 * middle + left
    first = 0.5 * (right - left)
    beta = curvature[:, :, None]
    delta = walk_off[:, :, None]
    real = middle[0] - beta * second[1] + delta * first[0]
    imag = middle[1] + beta * second[0] + delta * first[1]
    moved = jnp.stack([real, imag])
    moved_low = moved.astype(jnp.bfloat16).reshape(2, local_orders, nblocks, block, steps_dev)
    tables = jnp.take(radial_tables, order_map, axis=0)
    scaled = radial_tables.astype(jnp.float32) * weights.reshape(nblocks, block)[None, :, :, None]
    analysis = jnp.take(scaled.astype(jnp.bfloat16), order_map, axis=0)
    points = jnp.einsum("mbqn,cmbnt->cmbqt", tables, moved_low, preferred_element_type=jnp.float32)
    points = points.reshape(2, local_orders, radial, steps_dev).astype(jnp.bfloat16)
    forward, backward = (jnp.asarray(table) for table in angle_matrices(ORDERS))
    back = local_kerr(
        lax.all_to_all(points, "ang", split_axis=2, concat_axis=1, tiled=True), forward, backward
    )
    returned = lax.all_to_all(back, "ang", split_axis=1, concat_axis=2, tiled=True)
    returned = returned.reshape(2, local_orders, nblocks, block, steps_dev)
    increment = jnp.einsum(
        "mbqn,cmbqt->cmbnt", analysis, returned, preferred_element_type=jnp.float32
    )
    increment = increment.reshape(2, local_orders, radial, steps_dev)
    return (moved + increment).astype(jnp.bfloat16)


def per_device(field, radial_tables, weights, order_map, curvature, walk_off):
    parts, orders, radial, steps = field.shape
    nblocks, block = radial_tables.shape[1:3]
    count = lax.axis_size("ang")
    fits = (
        steps == LANES
        and orders % ROWS == 0
        and ROWS < orders <= LANES // 2
        and block % (2 * count) == 0
        and count > 1
        and radial % LANES == 0
        and LANES % block == 0
        and nblocks >= 2
    )
    plan = pipelined if fits else whole_arrays
    return plan(field, radial_tables, weights, order_map, curvature, walk_off)


def solution(mesh):
    in_specs = (P("groups", "ang", None, "tm"), P(), P(), P("ang"), P("ang", None), P("ang", None))
    out_specs = P("groups", "ang", None, "tm")
    return jax.shard_map(
        per_device, mesh=mesh, in_specs=in_specs, out_specs=out_specs, check_vma=False
    )
```

```python
import functools
import math

import jax
import jax.numpy as jnp
import numpy as np
from jax import lax
from jax.experimental import pallas as pl
from jax.experimental.pallas import tpu as pltpu
from jax.sharding import PartitionSpec as P

ORDERS = 256
LANES = 128
ROWS = 16

kerr_gamma = 0.00390625


def angle_matrices(count):
    index = np.arange(count, dtype=np.int32)
    phase = (index[:, None] * index[None, :] % count).astype(np.float32) * np.float32(
        2.0 * math.pi / count
    )
    cosine, sine = np.cos(phase), np.sin(phase)
    forward = np.block([[cosine, -sine], [sine, cosine]])
    backward = np.block([[cosine, sine], [-sine, cosine]])
    return forward.astype(jnp.bfloat16), backward.astype(jnp.bfloat16)


def ring(axis, shift):
    count = lax.axis_size(axis)
    return [(i, (i + shift) % count) for i in range(count)]


def lane_index(rows):
    return lax.broadcasted_iota(jnp.int32, (rows, LANES), 1)


def roll(x, shift):
    return pltpu.roll(x, shift, 1)


def params():
    return pltpu.CompilerParams(vmem_limit_bytes=40 * 1024 * 1024)


def cost(flops, size):
    return pl.CostEstimate(flops=flops, bytes_accessed=size, transcendentals=0)


def anywhere(count):
    return [pl.BlockSpec(memory_space=pl.ANY)] * count


def token():
    return jax.ShapeDtypeStruct((8, LANES), jnp.float32)


def indices(shape):
    return [lax.broadcasted_iota(jnp.int32, shape, axis) for axis in range(2)]


def ones_where(mask):
    return jnp.where(mask, 1.0, 0.0).astype(jnp.bfloat16)


def fill_packer(ref):
    ref[...] = jnp.zeros_like(ref)
    row, lane = indices((ROWS, LANES))
    for i in range(ROWS):
        at = i * LANES
        ref[at : at + ROWS, :] = ones_where((row == 0) & (lane == 2 * i))
        at += LANES - ROWS
        last = (2 * i - 1) % LANES
        ref[at : at + ROWS, :] = ones_where((row == ROWS - 1) & (lane == last))


def fill_picker(ref):
    ref[...] = jnp.zeros_like(ref)
    row, lane = indices((ROWS, LANES))
    for i in range(ROWS):
        first, last = 2 * i, (2 * i - 1) % LANES
        for tile in {first // ROWS, last // ROWS}:
            mask = ((lane == 0) & (row == first - tile * ROWS)) | (
                (lane == LANES - 1) & (row == last - tile * ROWS)
            )
            ref[tile * ROWS : (tile + 1) * ROWS, i * LANES : (i + 1) * LANES] = ones_where(mask)


def fill_stencil(ref):
    row, lane = indices((LANES, LANES))
    apart = row - lane
    near = jnp.where((apart == 1) | (apart == -1), 1.0, 0.0)
    side = jnp.where(apart == 1, 0.5, 0.0) - jnp.where(apart == -1, 0.5, 0.0)
    low = (row == 0) & (lane == 0)
    high = (row == LANES - 1) & (lane == LANES - 1)
    ref[:LANES, :LANES] = (near - jnp.where(apart == 0, 2.0, 0.0)).astype(jnp.bfloat16)
    ref[:LANES, LANES:] = side.astype(jnp.bfloat16)
    ref[LANES:, :LANES] = ones_where(low | high)
    ref[LANES:, LANES:] = (jnp.where(high, 0.5, 0.0) - jnp.where(low, 0.5, 0.0)).astype(
        jnp.bfloat16
    )


def edges(field, first, count, block, span, after):
    parts = field.shape[0]
    base, groups = span[0] // ROWS, span[1] // ROWS

    def kernel(x_ref, *refs):
        o_ref, _, acc, packer = refs[-4:]
        g = pl.program_id(1)

        @pl.when((pl.program_id(0) == 0) & (g == 0))
        def _():
            fill_packer(packer)

        rows = [
            jnp.concatenate([x_ref[c, i] for i in range(ROWS)], 1) for c in range(parts)
        ]
        packed = jnp.dot(
            jnp.concatenate(rows, 0), packer[...], preferred_element_type=jnp.float32
        )
        packed = roll(packed, 2 * ROWS * (g + base))

        @pl.when(g == 0)
        def _():
            acc[...] = packed

        @pl.when(g > 0)
        def _():
            acc[...] += packed

        @pl.when(g == groups - 1)
        def _():
            for c in range(parts):
                o_ref[c] = acc[c * block : (c + 1) * block, :].astype(o_ref.dtype)

    return pl.pallas_call(
        kernel,
        out_shape=[
            jax.ShapeDtypeStruct((parts, count * block, LANES), field.dtype),
            token(),
        ],
        grid=(count, groups),
        in_specs=[
            pl.BlockSpec((parts, ROWS, block, LANES), lambda j, g: (0, g + base, j + first, 0))
        ]
        + anywhere(len(after)),
        out_specs=[pl.BlockSpec((parts, block, LANES), lambda j, g: (0, j, 0))] + anywhere(1),
        scratch_shapes=[
            pltpu.VMEM((parts * block, LANES), jnp.float32),
            pltpu.VMEM((ROWS * LANES, LANES), jnp.bfloat16),
        ],
        compiler_params=params(),
        cost_estimate=cost(0, parts * span[1] * count * block * LANES * 2),
        name="edges",
    )(field, *after)


def join_halo(low, high):
    lane = lane_index(low.shape[0])
    low, high = low.astype(jnp.float32), high.astype(jnp.float32)
    return jnp.where((lane & 1) == 0, roll(low, 1), roll(high, LANES - 1))


def parts_of(x):
    found = []
    for _ in range(3):
        found.append(x.astype(jnp.bfloat16).astype(jnp.float32))
        x = x - found[-1]
    return jnp.concatenate(found, 0)


def columns(ref, start, block):
    base = start // LANES * LANES
    turned = jnp.transpose(parts_of(ref[:, base : base + LANES]))
    return turned[start - base : start - base + block].astype(jnp.bfloat16)


def moving_scratch(parts, block):
    return [
        pltpu.VMEM((2 * LANES, 2 * LANES), jnp.bfloat16),
        pltpu.VMEM((LANES, ROWS * LANES), jnp.bfloat16),
        pltpu.VMEM((ROWS * parts * block, 2 * LANES), jnp.bfloat16),
        pltpu.VMEM((ROWS * parts * block, 2 * LANES), jnp.float32),
        pltpu.VMEM((2 * block, ROWS * LANES), jnp.float32),
    ]


def moving(x_ref, low_ref, high_ref, beta_ref, delta_ref, scratch, group, start):
    parts, _, block, _ = x_ref.shape
    stencil, picker, wide, change, rates = scratch

    @pl.when(pl.program_id(0) == 0)
    def _():
        fill_stencil(stencil)
        fill_picker(picker)

    shift = (LANES - 2 * ROWS * group) & (LANES - 1)
    halo = [roll(join_halo(low_ref[c], high_ref[c]), shift) for c in range(parts)]
    halo = jnp.concatenate(halo, 0).astype(jnp.bfloat16)
    ends = jnp.dot(halo, picker[...], preferred_element_type=jnp.float32).astype(jnp.bfloat16)
    for i in range(ROWS):
        for c in range(parts):
            at = (i * parts + c) * block
            wide[at : at + block, :LANES] = x_ref[c, i]
            wide[at : at + block, LANES:] = ends[
                c * block : (c + 1) * block, i * LANES : (i + 1) * LANES
            ]
    change[...] = jnp.dot(wide[...], stencil[...], preferred_element_type=jnp.float32)
    factors = jnp.concatenate(
        [columns(beta_ref, start, block), columns(delta_ref, start, block)], 0
    )
    row, lane = indices((3 * ROWS, ROWS * LANES))
    spread = ones_where(row % ROWS == lane // LANES)
    rates[...] = jnp.dot(factors, spread, preferred_element_type=jnp.float32)

    def order(i):
        lanes = slice(i * LANES, (i + 1) * LANES)
        beta, delta = rates[:block, lanes], rates[block:, lanes]
        at = [(i * parts + c) * block for c in range(parts)]
        second = [change[a : a + block, :LANES] for a in at]
        first = [change[a : a + block, LANES:] for a in at]
        real = x_ref[0, i].astype(jnp.float32) - beta * second[1] + delta * first[0]
        imag = x_ref[1, i].astype(jnp.float32) + beta * second[0] + delta * first[1]
        return real, imag

    return order


def radial_specs(parts, kinds, block, radial, b, halo_at, base):
    return [
        pl.BlockSpec((parts, ROWS, block, LANES), lambda g, *_: (0, g + base, b, 0)),
        pl.BlockSpec((parts, block, LANES), lambda g, *_: (0, halo_at, 0)),
        pl.BlockSpec((parts, block, LANES), lambda g, *_: (0, halo_at, 0)),
        pl.BlockSpec((kinds, 1, block, block), lambda g, *_: (0, b, 0, 0)),
        pl.BlockSpec((ROWS, radial), lambda g, *_: (g + base, 0)),
        pl.BlockSpec((ROWS, radial), lambda g, *_: (g + base, 0)),
    ]


def synthesize(field, halo, tables, curvature, walk_off, order_map, me, b, count, span, after):
    low, high, halo_at = halo
    parts, _, radial, _ = field.shape
    kinds, _, block, _ = tables.shape
    share = block // count
    base, groups = span[0] // ROWS, span[1] // ROWS

    def kernel(map_ref, me_ref, x_ref, low_ref, high_ref, tab_ref, beta_ref, delta_ref, *refs):
        outs, acc, scratch = refs[len(after) : len(after) + count], refs[-6], refs[-5:]
        g = pl.program_id(0)
        order = moving(
            x_ref, low_ref, high_ref, beta_ref, delta_ref, scratch, g + base, b * block
        )
        for i in range(ROWS):
            m = (g + base) * ROWS + i
            moved = jnp.concatenate(order(i), 1).astype(jnp.bfloat16)
            points = jnp.dot(
                tab_ref[map_ref[m], 0], moved, preferred_element_type=jnp.float32
            )
            for c in range(parts):
                acc[c, pl.ds(i, block, stride=ROWS), :] = points[:, c * LANES : (c + 1) * LANES]
        for s in range(count):
            owner = lax.rem(me_ref[0] + s, count)
            for q in range(share):
                row = pl.multiple_of((owner * share + q) * ROWS, ROWS)
                for c in range(parts):
                    outs[s][q, c] = acc[c, pl.ds(row, ROWS), :].astype(jnp.bfloat16)

    piece = jax.ShapeDtypeStruct((share, parts, span[1], LANES), jnp.bfloat16)
    size = parts * span[1] * block * LANES * 2
    *pieces, done = pl.pallas_call(
        kernel,
        out_shape=[piece] * count + [token()],
        grid_spec=pltpu.PrefetchScalarGridSpec(
            num_scalar_prefetch=2,
            grid=(groups,),
            in_specs=radial_specs(parts, kinds, block, radial, b, halo_at, base)
            + anywhere(len(after)),
            out_specs=[
                pl.BlockSpec((share, parts, ROWS, LANES), lambda g, *_: (0, 0, g, 0))
            ]
            * count
            + anywhere(1),
            scratch_shapes=[pltpu.VMEM((parts, block * ROWS, LANES), jnp.float32)]
            + moving_scratch(parts, block),
        ),
        compiler_params=params(),
        cost_estimate=cost(2 * size * block, 2 * size),
        name="synthesize",
    )(order_map, me, field, low, high, tables, curvature, walk_off, *after)
    return pieces, done


def kerr_step(pieces, spans, out_spans, forward, backward, me, after):
    count = len(pieces[0])
    share, parts = pieces[0][0].shape[:2]
    orders = sum(size for _, size in spans)
    every = count * orders
    width = 2
    ins_count, outs_count = count * len(spans), count * len(out_spans)

    def kernel(me_ref, f_ref, b_ref, *refs):
        ins = refs[:ins_count]
        outs = refs[ins_count + len(after) : ins_count + len(after) + outs_count]
        flat, back = refs[-2:]
        for k, (start, size) in enumerate(spans):
            for s in range(count):
                source = lax.rem(me_ref[0] + count - s, count)
                for c in range(parts):
                    row = pl.multiple_of(c * every + source * orders + start, ROWS)
                    for q in range(width):
                        flat[pl.ds(row, size), q * LANES : (q + 1) * LANES] = ins[
                            k * count + s
                        ][q, c]
        angular = jnp.dot(f_ref[...], flat[...], preferred_element_type=jnp.float32)
        real, imag = angular[:every], angular[every:]
        power = kerr_gamma * (real * real + imag * imag)
        kerr = jnp.concatenate([-power * imag, power * real], 0).astype(jnp.bfloat16)
        back[...] = (
            jnp.dot(b_ref[...], kerr, preferred_element_type=jnp.float32) * (1.0 / every)
        ).astype(jnp.bfloat16)
        for k, (start, size) in enumerate(out_spans):
            for s in range(count):
                owner = lax.rem(me_ref[0] + s, count)
                for c in range(parts):
                    row = pl.multiple_of(c * every + owner * orders + start, ROWS)
                    for q in range(width):
                        outs[k * count + s][q, c] = back[
                            pl.ds(row, size), q * LANES : (q + 1) * LANES
                        ]

    def blocks(some):
        return [
            pl.BlockSpec((width, parts, size, LANES), lambda q, *_: (q, 0, 0, 0))
            for _, size in some
            for _ in range(count)
        ]

    whole = pl.BlockSpec((parts * every, parts * every), lambda q, *_: (0, 0))
    lanes = share * LANES
    *back, done = pl.pallas_call(
        kernel,
        out_shape=[
            jax.ShapeDtypeStruct((share, parts, size, LANES), jnp.bfloat16)
            for _, size in out_spans
            for _ in range(count)
        ]
        + [token()],
        grid_spec=pltpu.PrefetchScalarGridSpec(
            num_scalar_prefetch=1,
            grid=(share // width,),
            in_specs=[whole, whole] + blocks(spans) + anywhere(len(after)),
            out_specs=blocks(out_spans) + anywhere(1),
            scratch_shapes=[
                pltpu.VMEM((parts * every, width * LANES), jnp.bfloat16),
                pltpu.VMEM((parts * every, width * LANES), jnp.bfloat16),
            ],
        ),
        compiler_params=params(),
        cost_estimate=cost(4 * (parts * every) ** 2 * lanes, 4 * parts * every * lanes),
        name="kerr",
    )(me, forward, backward, *(piece for group in pieces for piece in group), *after)
    return [back[k * count : (k + 1) * count] for k in range(len(out_spans))], done


def analyze(
    pieces, field, halo, tables, curvature, walk_off, order_map, me, b, span, out, after
):
    low, high, halo_at = halo
    count = len(pieces)
    parts, _, radial, _ = field.shape
    kinds, _, block, _ = tables.shape
    share = block // count
    base, groups = span[0] // ROWS, span[1] // ROWS
    held = () if out is None else (out,)

    def kernel(map_ref, me_ref, *refs):
        ins = refs[:count]
        x_ref, low_ref, high_ref, tab_ref, beta_ref, delta_ref = refs[count : count + 6]
        o_ref, _, acc = refs[-8:-5]
        scratch = refs[-5:]
        g = pl.program_id(0)
        for s in range(count):
            source = lax.rem(me_ref[0] + count - s, count)
            for q in range(share):
                row = pl.multiple_of((source * share + q) * ROWS, ROWS)
                for c in range(parts):
                    acc[c, pl.ds(row, ROWS), :] = ins[s][q, c].astype(jnp.float32)
        order = moving(
            x_ref, low_ref, high_ref, beta_ref, delta_ref, scratch, g + base, b * block
        )
        for i in range(ROWS):
            m = (g + base) * ROWS + i
            moved = order(i)
            back = [acc[c, pl.ds(i, block, stride=ROWS), :] for c in range(parts)]
            back = jnp.concatenate(back, 1).astype(jnp.bfloat16)
            increment = jnp.dot(
                tab_ref[map_ref[m], 0], back, preferred_element_type=jnp.float32
            )
            for c in range(parts):
                total = moved[c] + increment[:, c * LANES : (c + 1) * LANES]
                o_ref[c, i] = total.astype(jnp.bfloat16)

    size = parts * span[1] * block * LANES * 2
    return pl.pallas_call(
        kernel,
        out_shape=[jax.ShapeDtypeStruct(field.shape, field.dtype), token()],
        grid_spec=pltpu.PrefetchScalarGridSpec(
            num_scalar_prefetch=2,
            grid=(groups,),
            in_specs=[
                pl.BlockSpec((share, parts, ROWS, LANES), lambda g, *_: (0, 0, g, 0))
            ]
            * count
            + radial_specs(parts, kinds, block, radial, b, halo_at, base)
            + anywhere(len(held) + len(after)),
            out_specs=[
                pl.BlockSpec((parts, ROWS, block, LANES), lambda g, *_: (0, g + base, b, 0))
            ]
            + anywhere(1),
            scratch_shapes=[pltpu.VMEM((parts, block * ROWS, LANES), jnp.float32)]
            + moving_scratch(parts, block),
        ),
        input_output_aliases={2 + count + 6: 0} if held else {},
        compiler_params=params(),
        cost_estimate=cost(2 * size * block, 3 * size),
        name="analyze",
    )(
        order_map, me, *pieces, field, low, high, tables, curvature, walk_off, *held, *after
    )


def exchange(pieces):
    return [pieces[0]] + [
        lax.ppermute(pieces[s], "ang", ring("ang", s)) for s in range(1, len(pieces))
    ]


def spans_of(sizes):
    starts = [sum(sizes[:k]) for k in range(len(sizes))]
    return list(zip(starts, sizes, strict=True))


def pipelined(field, radial_tables, weights, order_map, curvature, walk_off):
    count = lax.axis_size("ang")
    orders = field.shape[1]
    nblocks, block = radial_tables.shape[1:3]
    me = lax.axis_index("ang").astype(jnp.int32).reshape(1)
    forward, backward = (jnp.asarray(table) for table in angle_matrices(ORDERS))
    scaled = radial_tables.astype(jnp.float32) * weights.reshape(nblocks, block)[None, :, :, None]
    analysis = scaled.astype(jnp.bfloat16).transpose(0, 1, 3, 2)
    whole = spans_of([orders])
    tail = spans_of([orders - ROWS, ROWS]) if orders > ROWS else whole
    spans = {}
    out_spans = {nblocks - 1: tail}
    after = ()
    halos, sent, returned = {}, {}, {}
    out = None

    def halo(first, some, span, after):
        ends, done = edges(field, first, some, block, span, after)
        low = lax.ppermute(ends, "tm", ring("tm", 1))
        high = lax.ppermute(ends, "tm", ring("tm", -1))
        return [(low, high, j) for j in range(some)], (done,)

    def points(b, span, ends, after):
        own, done = synthesize(
            field, ends, radial_tables, curvature, walk_off, order_map, me, b, count, span, after
        )
        sent.setdefault(b, []).append(exchange(own))
        return (done,)

    def turn(b, after):
        back, done = kerr_step(
            sent.pop(b), spans.get(b, whole), out_spans.get(b, whole), forward, backward, me, after
        )
        returned[b] = [exchange(group) for group in back]
        return (done,)

    def finish(b, out, after):
        for span, group in zip(out_spans.get(b, whole), returned.pop(b), strict=True):
            out, done = analyze(
                group, field, halos[b], analysis, curvature, walk_off, order_map, me, b, span,
                out, after,
            )
            after = (done,)
        return out, after

    (halos[0],), after = halo(0, 1, whole[0], after)
    after = points(0, whole[0], halos[0], after)
    (halos[1],), after = halo(1, 1, whole[0], after)
    after = points(1, whole[0], halos[1], after)
    if nblocks > 2:
        rest, after = halo(2, nblocks - 2, whole[0], after)
        halos.update(zip(range(2, nblocks), rest, strict=True))
    for b in range(nblocks):
        if b >= nblocks - 1:
            after = after + tuple(returned[b - 1][0][1:2])
        after = turn(b, after)
        if b >= 1:
            out, after = finish(b - 1, out, after)
        if b + 2 < nblocks:
            after = points(b + 2, whole[0], halos[b + 2], after)
    out, after = finish(nblocks - 1, out, after)
    return out


def with_halo(block, axis, dim):
    low = lax.ppermute(
        lax.slice_in_dim(block, block.shape[dim] - 1, None, axis=dim), axis, ring(axis, 1)
    )
    high = lax.ppermute(lax.slice_in_dim(block, 0, 1, axis=dim), axis, ring(axis, -1))
    return jnp.concatenate([low, block, high], axis=dim)


def local_kerr(pieces, forward, backward):
    orders = pieces.shape[1]
    flat = pieces.reshape(2 * orders, -1)
    angular = jnp.dot(forward, flat, preferred_element_type=jnp.float32)
    power = angular[:orders] ** 2 + angular[orders:] ** 2
    kerr = jnp.concatenate(
        [-kerr_gamma * power * angular[orders:], kerr_gamma * power * angular[:orders]], 0
    )
    kerr = kerr.astype(jnp.bfloat16)
    back = jnp.dot(backward, kerr, preferred_element_type=jnp.float32) * (1.0 / orders)
    return back.astype(jnp.bfloat16).reshape(pieces.shape)


def whole_arrays(field, radial_tables, weights, order_map, curvature, walk_off):
    local_orders, radial, steps_dev = field.shape[1:]
    nblocks, block = radial_tables.shape[1:3]
    padded = with_halo(field, "tm", 3).astype(jnp.float32)
    middle = padded[..., 1:-1]
    right = padded[..., 2:]
    left = padded[..., :-2]
    second = right - 2.0 * middle + left
    first = 0.5 * (right - left)
    beta = curvature[:, :, None]
    delta = walk_off[:, :, None]
    real = middle[0] - beta * second[1] + delta * first[0]
    imag = middle[1] + beta * second[0] + delta * first[1]
    moved = jnp.stack([real, imag])
    moved_low = moved.astype(jnp.bfloat16).reshape(2, local_orders, nblocks, block, steps_dev)
    tables = jnp.take(radial_tables, order_map, axis=0)
    scaled = radial_tables.astype(jnp.float32) * weights.reshape(nblocks, block)[None, :, :, None]
    analysis = jnp.take(scaled.astype(jnp.bfloat16), order_map, axis=0)
    points = jnp.einsum("mbqn,cmbnt->cmbqt", tables, moved_low, preferred_element_type=jnp.float32)
    points = points.reshape(2, local_orders, radial, steps_dev).astype(jnp.bfloat16)
    forward, backward = (jnp.asarray(table) for table in angle_matrices(ORDERS))
    back = local_kerr(
        lax.all_to_all(points, "ang", split_axis=2, concat_axis=1, tiled=True), forward, backward
    )
    returned = lax.all_to_all(back, "ang", split_axis=1, concat_axis=2, tiled=True)
    returned = returned.reshape(2, local_orders, nblocks, block, steps_dev)
    increment = jnp.einsum(
        "mbqn,cmbqt->cmbnt", analysis, returned, preferred_element_type=jnp.float32
    )
    increment = increment.reshape(2, local_orders, radial, steps_dev)
    return (moved + increment).astype(jnp.bfloat16)


def per_device(field, radial_tables, weights, order_map, curvature, walk_off):
    parts, orders, radial, steps = field.shape
    nblocks, block = radial_tables.shape[1:3]
    count = lax.axis_size("ang")
    fits = (
        steps == LANES
        and orders % ROWS == 0
        and 2 * orders <= LANES
        and block % (2 * count) == 0
        and radial % LANES == 0
        and LANES % block == 0
        and nblocks >= 2
    )
    plan = pipelined if fits else whole_arrays
    return plan(field, radial_tables, weights, order_map, curvature, walk_off)


def solution(mesh):
    in_specs = (P("groups", "ang", None, "tm"), P(), P(), P("ang"), P("ang", None), P("ang", None))
    out_specs = P("groups", "ang", None, "tm")
    return jax.shard_map(
        per_device, mesh=mesh, in_specs=in_specs, out_specs=out_specs, check_vma=False
    )
```

```python
import functools
import math

import jax
import jax.numpy as jnp
import numpy as np
from jax import lax
from jax.experimental import pallas as pl
from jax.experimental.pallas import tpu as pltpu
from jax.sharding import PartitionSpec as P

ORDERS = 256
LANES = 128
ROWS = 16

kerr_gamma = 0.00390625


def angle_matrices(count):
    index = np.arange(count, dtype=np.int32)
    phase = (index[:, None] * index[None, :] % count).astype(np.float32) * np.float32(
        2.0 * math.pi / count
    )
    cosine, sine = np.cos(phase), np.sin(phase)
    forward = np.block([[cosine, -sine], [sine, cosine]])
    backward = np.block([[cosine, sine], [-sine, cosine]])
    return forward.astype(jnp.bfloat16), backward.astype(jnp.bfloat16)


def ring(axis, shift):
    count = lax.axis_size(axis)
    return [(i, (i + shift) % count) for i in range(count)]


def lane_index(rows):
    return lax.broadcasted_iota(jnp.int32, (rows, LANES), 1)


def roll(x, shift):
    return pltpu.roll(x, shift, 1)


def params():
    return pltpu.CompilerParams(vmem_limit_bytes=40 * 1024 * 1024)


def cost(flops, size):
    return pl.CostEstimate(flops=flops, bytes_accessed=size, transcendentals=0)


def anywhere(count):
    return [pl.BlockSpec(memory_space=pl.ANY)] * count


def token():
    return jax.ShapeDtypeStruct((8, LANES), jnp.float32)


def indices(shape):
    return [lax.broadcasted_iota(jnp.int32, shape, axis) for axis in range(2)]


def ones_where(mask):
    return jnp.where(mask, 1.0, 0.0).astype(jnp.bfloat16)


HALVES = 2


def field_specs(parts, block, place):
    rows = ROWS // HALVES

    def spec(c, half):
        def index(*at):
            group, b = place(*at)
            return (c, group * HALVES + half, b, 0)

        return pl.BlockSpec((1, rows, block, LANES), index)

    return [spec(c, half) for c in range(parts) for half in range(HALVES)]


def field_block(x_refs, c, i):
    rows = ROWS // HALVES
    return x_refs[c * HALVES + i // rows][0, i % rows]


def fill_stencil(ref):
    row, lane = indices((LANES, LANES))
    apart = row - lane
    near = jnp.where((apart == 1) | (apart == -1), 1.0, 0.0)
    side = jnp.where(apart == 1, 0.5, 0.0) - jnp.where(apart == -1, 0.5, 0.0)
    low = (row == 0) & (lane == 0)
    high = (row == LANES - 1) & (lane == LANES - 1)
    ref[:LANES, :LANES] = (near - jnp.where(apart == 0, 2.0, 0.0)).astype(jnp.bfloat16)
    ref[:LANES, LANES:] = side.astype(jnp.bfloat16)
    ref[LANES:, :LANES] = ones_where(low | high)
    ref[LANES:, LANES:] = (jnp.where(high, 0.5, 0.0) - jnp.where(low, 0.5, 0.0)).astype(
        jnp.bfloat16
    )


def edges(field, first, count, block, span, after):
    parts = field.shape[0]
    base, groups = span[0] // ROWS, span[1] // ROWS

    def kernel(*refs):
        x_refs, (o_ref, _, acc) = refs[: parts * HALVES], refs[-3:]
        g = pl.program_id(1)
        slot = ((lane_index(block) + 1) >> 1) & (LANES // 2 - 1)
        for c in range(parts):
            kept = jnp.where(g == 0, 0.0, acc[c])
            for i in range(ROWS):
                m = (g + base) * ROWS + i
                row = roll(field_block(x_refs, c, i).astype(jnp.float32), 2 * m)
                kept = jnp.where(slot == m, row, kept)
            acc[c] = kept

        @pl.when(g == groups - 1)
        def _():
            o_ref[...] = acc[...].astype(o_ref.dtype)

    return pl.pallas_call(
        kernel,
        out_shape=[
            jax.ShapeDtypeStruct((parts, count * block, LANES), field.dtype),
            token(),
        ],
        grid=(count, groups),
        in_specs=field_specs(parts, block, lambda j, g: (g + base, j + first))
        + anywhere(len(after)),
        out_specs=[pl.BlockSpec((parts, block, LANES), lambda j, g: (0, j, 0))] + anywhere(1),
        scratch_shapes=[pltpu.VMEM((parts, block, LANES), jnp.float32)],
        compiler_params=params(),
        cost_estimate=cost(0, parts * span[1] * count * block * LANES * 2),
        name="edges",
    )(*[field] * (parts * HALVES), *after)


def join_halo(low, high):
    lane = lane_index(low.shape[0])
    low, high = low.astype(jnp.float32), high.astype(jnp.float32)
    return jnp.where((lane & 1) == 0, roll(low, 1), roll(high, LANES - 1))


def columns(ref, start, block):
    base = start // LANES * LANES
    turned = jnp.transpose(ref[:, base : base + LANES])
    return turned[start - base : start - base + block]


def moving_scratch(parts, block):
    return [
        pltpu.VMEM((2 * LANES, 2 * LANES), jnp.bfloat16),
        pltpu.VMEM((ROWS * parts * block, 2 * LANES), jnp.bfloat16),
        pltpu.VMEM((ROWS * parts * block, 2 * LANES), jnp.float32),
    ]


def moving(x_refs, low_ref, high_ref, beta_ref, delta_ref, scratch, group, start):
    parts, block, _ = low_ref.shape
    stencil, wide, change = scratch

    @pl.when(pl.program_id(0) == 0)
    def _():
        fill_stencil(stencil)

    halo = [join_halo(low_ref[c], high_ref[c]) for c in range(parts)]
    for i in range(ROWS):
        shift = (LANES - 2 * (ROWS * group + i)) & (LANES - 1)
        for c in range(parts):
            at = (i * parts + c) * block
            wide[at : at + block, :LANES] = field_block(x_refs, c, i)
            wide[at : at + block, LANES:] = roll(halo[c], shift).astype(jnp.bfloat16)
    change[...] = jnp.dot(wide[...], stencil[...], preferred_element_type=jnp.float32)
    beta = columns(beta_ref, start, block)
    delta = columns(delta_ref, start, block)

    def order(i):
        at = [(i * parts + c) * block for c in range(parts)]
        second = [change[a : a + block, :LANES] for a in at]
        first = [change[a : a + block, LANES:] for a in at]
        x = [field_block(x_refs, c, i).astype(jnp.float32) for c in range(parts)]
        real = x[0] - beta[:, i : i + 1] * second[1] + delta[:, i : i + 1] * first[0]
        imag = x[1] + beta[:, i : i + 1] * second[0] + delta[:, i : i + 1] * first[1]
        return real, imag

    return order


def radial_specs(parts, kinds, block, radial, b, halo_at, base):
    return field_specs(parts, block, lambda g, *_: (g + base, b)) + [
        pl.BlockSpec((parts, block, LANES), lambda g, *_: (0, halo_at, 0)),
        pl.BlockSpec((parts, block, LANES), lambda g, *_: (0, halo_at, 0)),
        pl.BlockSpec((kinds, 1, block, block), lambda g, *_: (0, b, 0, 0)),
        pl.BlockSpec((ROWS, radial), lambda g, *_: (g + base, 0)),
        pl.BlockSpec((ROWS, radial), lambda g, *_: (g + base, 0)),
    ]


def synthesize(field, halo, tables, curvature, walk_off, order_map, me, b, count, span, after):
    low, high, halo_at = halo
    parts, _, radial, _ = field.shape
    kinds, _, block, _ = tables.shape
    share = block // count
    base, groups = span[0] // ROWS, span[1] // ROWS

    def kernel(map_ref, me_ref, *refs):
        x_refs, refs = refs[: parts * HALVES], refs[parts * HALVES :]
        low_ref, high_ref, tab_ref, beta_ref, delta_ref = refs[:5]
        outs, acc, scratch = refs[-count - 5 : -5], refs[-4], refs[-3:]
        g = pl.program_id(0)
        order = moving(
            x_refs, low_ref, high_ref, beta_ref, delta_ref, scratch, g + base, b * block
        )
        for i in range(ROWS):
            m = (g + base) * ROWS + i
            moved = jnp.concatenate(order(i), 1).astype(jnp.bfloat16)
            points = jnp.dot(
                tab_ref[map_ref[m], 0], moved, preferred_element_type=jnp.float32
            )
            for c in range(parts):
                acc[c, pl.ds(i, block, stride=ROWS), :] = points[:, c * LANES : (c + 1) * LANES]
        for s in range(count):
            owner = lax.rem(me_ref[0] + s, count)
            for q in range(share):
                row = pl.multiple_of((owner * share + q) * ROWS, ROWS)
                for c in range(parts):
                    outs[s][q, c] = acc[c, pl.ds(row, ROWS), :].astype(jnp.bfloat16)

    piece = jax.ShapeDtypeStruct((share, parts, span[1], LANES), jnp.bfloat16)
    size = parts * span[1] * block * LANES * 2
    *pieces, done = pl.pallas_call(
        kernel,
        out_shape=[piece] * count + [token()],
        grid_spec=pltpu.PrefetchScalarGridSpec(
            num_scalar_prefetch=2,
            grid=(groups,),
            in_specs=radial_specs(parts, kinds, block, radial, b, halo_at, base)
            + anywhere(len(after)),
            out_specs=[
                pl.BlockSpec((share, parts, ROWS, LANES), lambda g, *_: (0, 0, g, 0))
            ]
            * count
            + anywhere(1),
            scratch_shapes=[pltpu.VMEM((parts, block * ROWS, LANES), jnp.float32)]
            + moving_scratch(parts, block),
        ),
        compiler_params=params(),
        cost_estimate=cost(2 * size * block, 2 * size),
        name="synthesize",
    )(
        order_map, me, *[field] * (parts * HALVES), low, high, tables, curvature, walk_off, *after
    )
    return pieces, done


def kerr_step(pieces, spans, out_spans, forward, backward, me, after):
    count = len(pieces[0])
    share, parts = pieces[0][0].shape[:2]
    orders = sum(size for _, size in spans)
    every = count * orders
    width = 2
    ins_count, outs_count = count * len(spans), count * len(out_spans)

    def kernel(me_ref, f_ref, b_ref, *refs):
        ins = refs[:ins_count]
        outs = refs[ins_count + len(after) : ins_count + len(after) + outs_count]
        flat, back = refs[-2:]
        for k, (start, size) in enumerate(spans):
            for s in range(count):
                source = lax.rem(me_ref[0] + count - s, count)
                for c in range(parts):
                    row = pl.multiple_of(c * every + source * orders + start, ROWS)
                    for q in range(width):
                        flat[pl.ds(row, size), q * LANES : (q + 1) * LANES] = ins[
                            k * count + s
                        ][q, c]
        angular = jnp.dot(f_ref[...], flat[...], preferred_element_type=jnp.float32)
        real, imag = angular[:every], angular[every:]
        power = kerr_gamma * (real * real + imag * imag)
        kerr = jnp.concatenate([-power * imag, power * real], 0).astype(jnp.bfloat16)
        back[...] = (
            jnp.dot(b_ref[...], kerr, preferred_element_type=jnp.float32) * (1.0 / every)
        ).astype(jnp.bfloat16)
        for k, (start, size) in enumerate(out_spans):
            for s in range(count):
                owner = lax.rem(me_ref[0] + s, count)
                for c in range(parts):
                    row = pl.multiple_of(c * every + owner * orders + start, ROWS)
                    for q in range(width):
                        outs[k * count + s][q, c] = back[
                            pl.ds(row, size), q * LANES : (q + 1) * LANES
                        ]

    def blocks(some):
        return [
            pl.BlockSpec((width, parts, size, LANES), lambda q, *_: (q, 0, 0, 0))
            for _, size in some
            for _ in range(count)
        ]

    whole = pl.BlockSpec((parts * every, parts * every), lambda q, *_: (0, 0))
    lanes = share * LANES
    *back, done = pl.pallas_call(
        kernel,
        out_shape=[
            jax.ShapeDtypeStruct((share, parts, size, LANES), jnp.bfloat16)
            for _, size in out_spans
            for _ in range(count)
        ]
        + [token()],
        grid_spec=pltpu.PrefetchScalarGridSpec(
            num_scalar_prefetch=1,
            grid=(share // width,),
            in_specs=[whole, whole] + blocks(spans) + anywhere(len(after)),
            out_specs=blocks(out_spans) + anywhere(1),
            scratch_shapes=[
                pltpu.VMEM((parts * every, width * LANES), jnp.bfloat16),
                pltpu.VMEM((parts * every, width * LANES), jnp.bfloat16),
            ],
        ),
        compiler_params=params(),
        cost_estimate=cost(4 * (parts * every) ** 2 * lanes, 4 * parts * every * lanes),
        name="kerr",
    )(me, forward, backward, *(piece for group in pieces for piece in group), *after)
    return [back[k * count : (k + 1) * count] for k in range(len(out_spans))], done


def analyze(
    pieces, field, halo, tables, curvature, walk_off, order_map, me, b, span, out, after
):
    low, high, halo_at = halo
    count = len(pieces)
    parts, _, radial, _ = field.shape
    kinds, _, block, _ = tables.shape
    share = block // count
    base, groups = span[0] // ROWS, span[1] // ROWS
    held = () if out is None else (out,)

    def kernel(map_ref, me_ref, *refs):
        ins, refs = refs[:count], refs[count:]
        x_refs, refs = refs[: parts * HALVES], refs[parts * HALVES :]
        low_ref, high_ref, tab_ref, beta_ref, delta_ref = refs[:5]
        o_ref, _, acc = refs[-6:-3]
        scratch = refs[-3:]
        g = pl.program_id(0)
        for s in range(count):
            source = lax.rem(me_ref[0] + count - s, count)
            for q in range(share):
                row = pl.multiple_of((source * share + q) * ROWS, ROWS)
                for c in range(parts):
                    acc[c, pl.ds(row, ROWS), :] = ins[s][q, c].astype(jnp.float32)
        order = moving(
            x_refs, low_ref, high_ref, beta_ref, delta_ref, scratch, g + base, b * block
        )
        for i in range(ROWS):
            m = (g + base) * ROWS + i
            moved = order(i)
            back = [acc[c, pl.ds(i, block, stride=ROWS), :] for c in range(parts)]
            back = jnp.concatenate(back, 1).astype(jnp.bfloat16)
            increment = jnp.dot(
                tab_ref[map_ref[m], 0], back, preferred_element_type=jnp.float32
            )
            for c in range(parts):
                total = moved[c] + increment[:, c * LANES : (c + 1) * LANES]
                o_ref[c, i] = total.astype(jnp.bfloat16)

    size = parts * span[1] * block * LANES * 2
    return pl.pallas_call(
        kernel,
        out_shape=[jax.ShapeDtypeStruct(field.shape, field.dtype), token()],
        grid_spec=pltpu.PrefetchScalarGridSpec(
            num_scalar_prefetch=2,
            grid=(groups,),
            in_specs=[
                pl.BlockSpec((share, parts, ROWS, LANES), lambda g, *_: (0, 0, g, 0))
            ]
            * count
            + radial_specs(parts, kinds, block, radial, b, halo_at, base)
            + anywhere(len(held) + len(after)),
            out_specs=[
                pl.BlockSpec((parts, ROWS, block, LANES), lambda g, *_: (0, g + base, b, 0))
            ]
            + anywhere(1),
            scratch_shapes=[pltpu.VMEM((parts, block * ROWS, LANES), jnp.float32)]
            + moving_scratch(parts, block),
        ),
        input_output_aliases={2 + count + parts * HALVES + 5: 0} if held else {},
        compiler_params=params(),
        cost_estimate=cost(2 * size * block, 3 * size),
        name="analyze",
    )(
        order_map, me, *pieces, *[field] * (parts * HALVES), low, high, tables, curvature,
        walk_off, *held, *after,
    )


def exchange(pieces):
    return [pieces[0]] + [
        lax.ppermute(pieces[s], "ang", ring("ang", s)) for s in range(1, len(pieces))
    ]


def spans_of(sizes):
    starts = [sum(sizes[:k]) for k in range(len(sizes))]
    return list(zip(starts, sizes, strict=True))


def pipelined(field, radial_tables, weights, order_map, curvature, walk_off):
    count = lax.axis_size("ang")
    orders = field.shape[1]
    nblocks, block = radial_tables.shape[1:3]
    me = lax.axis_index("ang").astype(jnp.int32).reshape(1)
    forward, backward = (jnp.asarray(table) for table in angle_matrices(ORDERS))
    scaled = radial_tables.astype(jnp.float32) * weights.reshape(nblocks, block)[None, :, :, None]
    analysis = scaled.astype(jnp.bfloat16).transpose(0, 1, 3, 2)
    whole = spans_of([orders])
    tail = spans_of([orders - ROWS, ROWS]) if orders > ROWS else whole
    spans = {}
    out_spans = {nblocks - 1: tail}
    after = ()
    halos, sent, returned = {}, {}, {}
    out = None

    def halo(first, some, span, after):
        ends, done = edges(field, first, some, block, span, after)
        low = lax.ppermute(ends, "tm", ring("tm", 1))
        high = lax.ppermute(ends, "tm", ring("tm", -1))
        return [(low, high, j) for j in range(some)], (done,)

    def points(b, span, ends, after):
        own, done = synthesize(
            field, ends, radial_tables, curvature, walk_off, order_map, me, b, count, span, after
        )
        sent.setdefault(b, []).append(exchange(own))
        return (done,)

    def turn(b, after):
        back, done = kerr_step(
            sent.pop(b), spans.get(b, whole), out_spans.get(b, whole), forward, backward, me, after
        )
        returned[b] = [exchange(group) for group in back]
        return (done,)

    def finish(b, out, after):
        for span, group in zip(out_spans.get(b, whole), returned.pop(b), strict=True):
            out, done = analyze(
                group, field, halos[b], analysis, curvature, walk_off, order_map, me, b, span,
                out, after,
            )
            after = (done,)
        return out, after

    (halos[0],), after = halo(0, 1, whole[0], after)
    after = points(0, whole[0], halos[0], after)
    (halos[1],), after = halo(1, 1, whole[0], after)
    after = points(1, whole[0], halos[1], after)
    if nblocks > 2:
        rest, after = halo(2, nblocks - 2, whole[0], after)
        halos.update(zip(range(2, nblocks), rest, strict=True))
    for b in range(nblocks):
        if b >= nblocks - 1:
            after = after + tuple(returned[b - 1][0][1:2])
        after = turn(b, after)
        if b >= 1:
            out, after = finish(b - 1, out, after)
        if b + 2 < nblocks:
            after = points(b + 2, whole[0], halos[b + 2], after)
    out, after = finish(nblocks - 1, out, after)
    return out


def with_halo(block, axis, dim):
    low = lax.ppermute(
        lax.slice_in_dim(block, block.shape[dim] - 1, None, axis=dim), axis, ring(axis, 1)
    )
    high = lax.ppermute(lax.slice_in_dim(block, 0, 1, axis=dim), axis, ring(axis, -1))
    return jnp.concatenate([low, block, high], axis=dim)


def local_kerr(pieces, forward, backward):
    orders = pieces.shape[1]
    flat = pieces.reshape(2 * orders, -1)
    angular = jnp.dot(forward, flat, preferred_element_type=jnp.float32)
    power = angular[:orders] ** 2 + angular[orders:] ** 2
    kerr = jnp.concatenate(
        [-kerr_gamma * power * angular[orders:], kerr_gamma * power * angular[:orders]], 0
    )
    kerr = kerr.astype(jnp.bfloat16)
    back = jnp.dot(backward, kerr, preferred_element_type=jnp.float32) * (1.0 / orders)
    return back.astype(jnp.bfloat16).reshape(pieces.shape)


def whole_arrays(field, radial_tables, weights, order_map, curvature, walk_off):
    local_orders, radial, steps_dev = field.shape[1:]
    nblocks, block = radial_tables.shape[1:3]
    padded = with_halo(field, "tm", 3).astype(jnp.float32)
    middle = padded[..., 1:-1]
    right = padded[..., 2:]
    left = padded[..., :-2]
    second = right - 2.0 * middle + left
    first = 0.5 * (right - left)
    beta = curvature[:, :, None]
    delta = walk_off[:, :, None]
    real = middle[0] - beta * second[1] + delta * first[0]
    imag = middle[1] + beta * second[0] + delta * first[1]
    moved = jnp.stack([real, imag])
    moved_low = moved.astype(jnp.bfloat16).reshape(2, local_orders, nblocks, block, steps_dev)
    tables = jnp.take(radial_tables, order_map, axis=0)
    scaled = radial_tables.astype(jnp.float32) * weights.reshape(nblocks, block)[None, :, :, None]
    analysis = jnp.take(scaled.astype(jnp.bfloat16), order_map, axis=0)
    points = jnp.einsum("mbqn,cmbnt->cmbqt", tables, moved_low, preferred_element_type=jnp.float32)
    points = points.reshape(2, local_orders, radial, steps_dev).astype(jnp.bfloat16)
    forward, backward = (jnp.asarray(table) for table in angle_matrices(ORDERS))
    back = local_kerr(
        lax.all_to_all(points, "ang", split_axis=2, concat_axis=1, tiled=True), forward, backward
    )
    returned = lax.all_to_all(back, "ang", split_axis=1, concat_axis=2, tiled=True)
    returned = returned.reshape(2, local_orders, nblocks, block, steps_dev)
    increment = jnp.einsum(
        "mbqn,cmbqt->cmbnt", analysis, returned, preferred_element_type=jnp.float32
    )
    increment = increment.reshape(2, local_orders, radial, steps_dev)
    return (moved + increment).astype(jnp.bfloat16)


def per_device(field, radial_tables, weights, order_map, curvature, walk_off):
    parts, orders, radial, steps = field.shape
    nblocks, block = radial_tables.shape[1:3]
    count = lax.axis_size("ang")
    fits = (
        steps == LANES
        and orders % ROWS == 0
        and 2 * orders <= LANES
        and block % (2 * count) == 0
        and radial % LANES == 0
        and LANES % block == 0
        and nblocks >= 2
    )
    plan = pipelined if fits else whole_arrays
    return plan(field, radial_tables, weights, order_map, curvature, walk_off)


def solution(mesh):
    in_specs = (P("groups", "ang", None, "tm"), P(), P(), P("ang"), P("ang", None), P("ang", None))
    out_specs = P("groups", "ang", None, "tm")
    return jax.shard_map(
        per_device, mesh=mesh, in_specs=in_specs, out_specs=out_specs, check_vma=False
    )
```

```python
import functools
import math

import jax
import jax.numpy as jnp
import numpy as np
from jax import lax
from jax.experimental import pallas as pl
from jax.experimental.pallas import tpu as pltpu
from jax.sharding import PartitionSpec as P

ORDERS = 256
LANES = 128
ROWS = 16
STRIDE = ROWS + 1

kerr_gamma = 0.00390625


def angle_matrices(count):
    index = np.arange(count, dtype=np.int32)
    phase = (index[:, None] * index[None, :] % count).astype(np.float32) * np.float32(
        2.0 * math.pi / count
    )
    cosine, sine = np.cos(phase), np.sin(phase)
    forward = np.block([[cosine, -sine], [sine, cosine]])
    backward = np.block([[cosine, sine], [-sine, cosine]])
    return forward.astype(jnp.bfloat16), backward.astype(jnp.bfloat16)


def ring(axis, shift):
    count = lax.axis_size(axis)
    return [(i, (i + shift) % count) for i in range(count)]


def lane_index(rows):
    return lax.broadcasted_iota(jnp.int32, (rows, LANES), 1)


def roll(x, shift):
    return pltpu.roll(x, shift, 1)


def params():
    return pltpu.CompilerParams(vmem_limit_bytes=40 * 1024 * 1024)


def cost(flops, size):
    return pl.CostEstimate(flops=flops, bytes_accessed=size, transcendentals=0)


def anywhere(count):
    return [pl.BlockSpec(memory_space=pl.ANY)] * count


def token():
    return jax.ShapeDtypeStruct((8, LANES), jnp.float32)


def edges(field, first, count, block, span, after):
    parts = field.shape[0]
    base, groups = span[0] // ROWS, span[1] // ROWS

    def kernel(x_ref, *refs):
        o_ref, _, acc = refs[-3:]
        g = pl.program_id(1)
        slot = ((lane_index(block) + 1) >> 1) & (LANES // 2 - 1)
        for c in range(parts):
            kept = acc[c]
            for i in range(ROWS):
                m = (g + base) * ROWS + i
                row = roll(x_ref[c, i].astype(jnp.float32), 2 * m)
                kept = jnp.where(slot == m, row, kept)
            acc[c] = kept

        @pl.when(g == groups - 1)
        def _():
            o_ref[...] = acc[...].astype(o_ref.dtype)

    return pl.pallas_call(
        kernel,
        out_shape=[
            jax.ShapeDtypeStruct((parts, count * block, LANES), field.dtype),
            token(),
        ],
        grid=(count, groups),
        in_specs=[
            pl.BlockSpec((parts, ROWS, block, LANES), lambda j, g: (0, g + base, j + first, 0))
        ]
        + anywhere(len(after)),
        out_specs=[pl.BlockSpec((parts, block, LANES), lambda j, g: (0, j, 0))] + anywhere(1),
        scratch_shapes=[pltpu.VMEM((parts, block, LANES), jnp.float32)],
        compiler_params=params(),
        cost_estimate=cost(0, parts * span[1] * count * block * LANES * 2),
        name="edges",
    )(field, *after)


def join_halo(low, high):
    lane = lane_index(low.shape[0])
    low, high = low.astype(jnp.float32), high.astype(jnp.float32)
    return jnp.where((lane & 1) == 0, roll(low, 1), roll(high, LANES - 1))


def columns(ref, start, block):
    base = start // LANES * LANES
    turned = jnp.transpose(ref[:, base : base + LANES])
    return turned[start - base : start - base + block]


def move(x, halo, beta, delta, m):
    lane = lane_index(beta.shape[0])
    second, first = [], []
    for c in range(2):
        ends = roll(halo[c], (LANES - 2 * m) & (LANES - 1))
        left = jnp.where(lane == 0, ends, roll(x[c], 1))
        right = jnp.where(lane == LANES - 1, ends, roll(x[c], LANES - 1))
        second.append(right - 2.0 * x[c] + left)
        first.append(0.5 * (right - left))
    real = x[0] - beta * second[1] + delta * first[0]
    imag = x[1] + beta * second[0] + delta * first[1]
    return real, imag


def radial_specs(parts, kinds, block, radial, b, halo_at, base):
    return [
        pl.BlockSpec((parts, ROWS, block, LANES), lambda g, *_: (0, g + base, b, 0)),
        pl.BlockSpec((parts, block, LANES), lambda g, *_: (0, halo_at, 0)),
        pl.BlockSpec((parts, block, LANES), lambda g, *_: (0, halo_at, 0)),
        pl.BlockSpec((kinds, 1, block, block), lambda g, *_: (0, b, 0, 0)),
        pl.BlockSpec((ROWS, radial), lambda g, *_: (g + base, 0)),
        pl.BlockSpec((ROWS, radial), lambda g, *_: (g + base, 0)),
    ]


def synthesize(field, halo, tables, curvature, walk_off, order_map, me, b, count, span, after):
    low, high, halo_at = halo
    parts, _, radial, _ = field.shape
    kinds, _, block, _ = tables.shape
    share = block // count
    base, groups = span[0] // ROWS, span[1] // ROWS

    def kernel(map_ref, me_ref, x_ref, low_ref, high_ref, tab_ref, beta_ref, delta_ref, *refs):
        outs, acc = refs[len(after) : len(after) + count], refs[-1]
        g = pl.program_id(0)
        beta = columns(beta_ref, b * block, block)
        delta = columns(delta_ref, b * block, block)
        ends = [join_halo(low_ref[c], high_ref[c]) for c in range(parts)]
        for i in range(ROWS):
            m = (g + base) * ROWS + i
            x = [x_ref[c, i].astype(jnp.float32) for c in range(parts)]
            moved = move(x, ends, beta[:, i : i + 1], delta[:, i : i + 1], m)
            moved = jnp.concatenate(moved, 1).astype(jnp.bfloat16)
            points = jnp.dot(
                tab_ref[map_ref[m], 0], moved, preferred_element_type=jnp.float32
            )
            for c in range(parts):
                acc[c, pl.ds(i, block, stride=STRIDE), :] = points[:, c * LANES : (c + 1) * LANES]
        for s in range(count):
            owner = lax.rem(me_ref[0] + s, count)
            start = pl.multiple_of(owner * share * STRIDE, 8)
            for c in range(parts):
                part = acc.at[c, pl.ds(start, share * STRIDE), :]
                for q in range(share):
                    row = q * STRIDE
                    outs[s][q, c] = part[row : row + ROWS, :].astype(jnp.bfloat16)

    piece = jax.ShapeDtypeStruct((share, parts, span[1], LANES), jnp.bfloat16)
    size = parts * span[1] * block * LANES * 2
    *pieces, done = pl.pallas_call(
        kernel,
        out_shape=[piece] * count + [token()],
        grid_spec=pltpu.PrefetchScalarGridSpec(
            num_scalar_prefetch=2,
            grid=(groups,),
            in_specs=radial_specs(parts, kinds, block, radial, b, halo_at, base)
            + anywhere(len(after)),
            out_specs=[
                pl.BlockSpec((share, parts, ROWS, LANES), lambda g, *_: (0, 0, g, 0))
            ]
            * count
            + anywhere(1),
            scratch_shapes=[pltpu.VMEM((parts, (block + 8) * STRIDE, LANES), jnp.float32)],
        ),
        compiler_params=params(),
        cost_estimate=cost(2 * size * block, 2 * size),
        name="synthesize",
    )(order_map, me, field, low, high, tables, curvature, walk_off, *after)
    return pieces, done


def kerr_step(pieces, spans, out_spans, forward, backward, me, after):
    count = len(pieces[0])
    share, parts = pieces[0][0].shape[:2]
    orders = sum(size for _, size in spans)
    every = count * orders
    width = 2
    ins_count, outs_count = count * len(spans), count * len(out_spans)

    def kernel(me_ref, f_ref, b_ref, *refs):
        ins = refs[:ins_count]
        outs = refs[ins_count + len(after) : ins_count + len(after) + outs_count]
        flat, back = refs[-2:]
        for k, (start, size) in enumerate(spans):
            for s in range(count):
                source = lax.rem(me_ref[0] + count - s, count)
                for c in range(parts):
                    row = pl.multiple_of(c * every + source * orders + start, ROWS)
                    for q in range(width):
                        flat[pl.ds(row, size), q * LANES : (q + 1) * LANES] = ins[
                            k * count + s
                        ][q, c]
        angular = jnp.dot(f_ref[...], flat[...], preferred_element_type=jnp.float32)
        real, imag = angular[:every], angular[every:]
        power = kerr_gamma * (real * real + imag * imag)
        kerr = jnp.concatenate([-power * imag, power * real], 0).astype(jnp.bfloat16)
        back[...] = (
            jnp.dot(b_ref[...], kerr, preferred_element_type=jnp.float32) * (1.0 / every)
        ).astype(jnp.bfloat16)
        for k, (start, size) in enumerate(out_spans):
            for s in range(count):
                owner = lax.rem(me_ref[0] + s, count)
                for c in range(parts):
                    row = pl.multiple_of(c * every + owner * orders + start, ROWS)
                    for q in range(width):
                        outs[k * count + s][q, c] = back[
                            pl.ds(row, size), q * LANES : (q + 1) * LANES
                        ]

    def blocks(some):
        return [
            pl.BlockSpec((width, parts, size, LANES), lambda q, *_: (q, 0, 0, 0))
            for _, size in some
            for _ in range(count)
        ]

    whole = pl.BlockSpec((parts * every, parts * every), lambda q, *_: (0, 0))
    lanes = share * LANES
    *back, done = pl.pallas_call(
        kernel,
        out_shape=[
            jax.ShapeDtypeStruct((share, parts, size, LANES), jnp.bfloat16)
            for _, size in out_spans
            for _ in range(count)
        ]
        + [token()],
        grid_spec=pltpu.PrefetchScalarGridSpec(
            num_scalar_prefetch=1,
            grid=(share // width,),
            in_specs=[whole, whole] + blocks(spans) + anywhere(len(after)),
            out_specs=blocks(out_spans) + anywhere(1),
            scratch_shapes=[
                pltpu.VMEM((parts * every, width * LANES), jnp.bfloat16),
                pltpu.VMEM((parts * every, width * LANES), jnp.bfloat16),
            ],
        ),
        compiler_params=params(),
        cost_estimate=cost(4 * (parts * every) ** 2 * lanes, 4 * parts * every * lanes),
        name="kerr",
    )(me, forward, backward, *(piece for group in pieces for piece in group), *after)
    return [back[k * count : (k + 1) * count] for k in range(len(out_spans))], done


def analyze(
    pieces, field, halo, tables, curvature, walk_off, order_map, me, b, span, out, after
):
    low, high, halo_at = halo
    count = len(pieces)
    parts, _, radial, _ = field.shape
    kinds, _, block, _ = tables.shape
    share = block // count
    base, groups = span[0] // ROWS, span[1] // ROWS
    held = () if out is None else (out,)

    def kernel(map_ref, me_ref, *refs):
        ins = refs[:count]
        x_ref, low_ref, high_ref, tab_ref, beta_ref, delta_ref = refs[count : count + 6]
        o_ref, _, acc = refs[-3:]
        g = pl.program_id(0)
        for s in range(count):
            source = lax.rem(me_ref[0] + count - s, count)
            start = pl.multiple_of(source * share * STRIDE, 8)
            for c in range(parts):
                part = acc.at[c, pl.ds(start, share * STRIDE), :]
                for q in range(share):
                    row = q * STRIDE
                    part[row : row + ROWS, :] = ins[s][q, c].astype(jnp.float32)
        beta = columns(beta_ref, b * block, block)
        delta = columns(delta_ref, b * block, block)
        ends = [join_halo(low_ref[c], high_ref[c]) for c in range(parts)]
        for i in range(ROWS):
            m = (g + base) * ROWS + i
            x = [x_ref[c, i].astype(jnp.float32) for c in range(parts)]
            moved = move(x, ends, beta[:, i : i + 1], delta[:, i : i + 1], m)
            back = [acc[c, pl.ds(i, block, stride=STRIDE), :] for c in range(parts)]
            back = jnp.concatenate(back, 1).astype(jnp.bfloat16)
            increment = jnp.dot(
                tab_ref[map_ref[m], 0], back, preferred_element_type=jnp.float32
            )
            for c in range(parts):
                total = moved[c] + increment[:, c * LANES : (c + 1) * LANES]
                o_ref[c, i] = total.astype(jnp.bfloat16)

    size = parts * span[1] * block * LANES * 2
    return pl.pallas_call(
        kernel,
        out_shape=[jax.ShapeDtypeStruct(field.shape, field.dtype), token()],
        grid_spec=pltpu.PrefetchScalarGridSpec(
            num_scalar_prefetch=2,
            grid=(groups,),
            in_specs=[
                pl.BlockSpec((share, parts, ROWS, LANES), lambda g, *_: (0, 0, g, 0))
            ]
            * count
            + radial_specs(parts, kinds, block, radial, b, halo_at, base)
            + anywhere(len(held) + len(after)),
            out_specs=[
                pl.BlockSpec((parts, ROWS, block, LANES), lambda g, *_: (0, g + base, b, 0))
            ]
            + anywhere(1),
            scratch_shapes=[pltpu.VMEM((parts, (block + 8) * STRIDE, LANES), jnp.float32)],
        ),
        input_output_aliases={2 + count + 6: 0} if held else {},
        compiler_params=params(),
        cost_estimate=cost(2 * size * block, 3 * size),
        name="analyze",
    )(
        order_map, me, *pieces, field, low, high, tables, curvature, walk_off, *held, *after
    )


def exchange(pieces):
    return [pieces[0]] + [
        lax.ppermute(pieces[s], "ang", ring("ang", s)) for s in range(1, len(pieces))
    ]


def spans_of(sizes):
    starts = [sum(sizes[:k]) for k in range(len(sizes))]
    return list(zip(starts, sizes, strict=True))


def pipelined(field, radial_tables, weights, order_map, curvature, walk_off):
    count = lax.axis_size("ang")
    orders = field.shape[1]
    nblocks, block = radial_tables.shape[1:3]
    me = lax.axis_index("ang").astype(jnp.int32).reshape(1)
    forward, backward = (jnp.asarray(table) for table in angle_matrices(ORDERS))
    scaled = radial_tables.astype(jnp.float32) * weights.reshape(nblocks, block)[None, :, :, None]
    analysis = scaled.astype(jnp.bfloat16).transpose(0, 1, 3, 2)
    whole = spans_of([orders])
    tail = spans_of([orders - ROWS, ROWS]) if orders > ROWS else whole
    spans = {}
    out_spans = {nblocks - 1: tail}
    after = ()
    halos, sent, returned = {}, {}, {}
    out = None

    def halo(first, some, span, after):
        ends, done = edges(field, first, some, block, span, after)
        low = lax.ppermute(ends, "tm", ring("tm", 1))
        high = lax.ppermute(ends, "tm", ring("tm", -1))
        return [(low, high, j) for j in range(some)], (done,)

    def points(b, span, ends, after):
        own, done = synthesize(
            field, ends, radial_tables, curvature, walk_off, order_map, me, b, count, span, after
        )
        sent.setdefault(b, []).append(exchange(own))
        return (done,)

    def turn(b, after):
        back, done = kerr_step(
            sent.pop(b), spans.get(b, whole), out_spans.get(b, whole), forward, backward, me, after
        )
        returned[b] = [exchange(group) for group in back]
        return (done,)

    def finish(b, out, after):
        for span, group in zip(out_spans.get(b, whole), returned.pop(b), strict=True):
            out, done = analyze(
                group, field, halos[b], analysis, curvature, walk_off, order_map, me, b, span,
                out, after,
            )
            after = (done,)
        return out, after

    (halos[0],), after = halo(0, 1, whole[0], after)
    after = points(0, whole[0], halos[0], after)
    (halos[1],), after = halo(1, 1, whole[0], after)
    after = points(1, whole[0], halos[1], after)
    if nblocks > 2:
        rest, after = halo(2, nblocks - 2, whole[0], after)
        halos.update(zip(range(2, nblocks), rest, strict=True))
    for b in range(nblocks):
        if b >= nblocks - 1:
            after = after + tuple(returned[b - 1][0][1:2])
        after = turn(b, after)
        if b >= 1:
            out, after = finish(b - 1, out, after)
        if b + 2 < nblocks:
            after = points(b + 2, whole[0], halos[b + 2], after)
    out, after = finish(nblocks - 1, out, after)
    return out


def with_halo(block, axis, dim):
    low = lax.ppermute(
        lax.slice_in_dim(block, block.shape[dim] - 1, None, axis=dim), axis, ring(axis, 1)
    )
    high = lax.ppermute(lax.slice_in_dim(block, 0, 1, axis=dim), axis, ring(axis, -1))
    return jnp.concatenate([low, block, high], axis=dim)


def local_kerr(pieces, forward, backward):
    orders = pieces.shape[1]
    flat = pieces.reshape(2 * orders, -1)
    angular = jnp.dot(forward, flat, preferred_element_type=jnp.float32)
    power = angular[:orders] ** 2 + angular[orders:] ** 2
    kerr = jnp.concatenate(
        [-kerr_gamma * power * angular[orders:], kerr_gamma * power * angular[:orders]], 0
    )
    kerr = kerr.astype(jnp.bfloat16)
    back = jnp.dot(backward, kerr, preferred_element_type=jnp.float32) * (1.0 / orders)
    return back.astype(jnp.bfloat16).reshape(pieces.shape)


def whole_arrays(field, radial_tables, weights, order_map, curvature, walk_off):
    local_orders, radial, steps_dev = field.shape[1:]
    nblocks, block = radial_tables.shape[1:3]
    padded = with_halo(field, "tm", 3).astype(jnp.float32)
    middle = padded[..., 1:-1]
    right = padded[..., 2:]
    left = padded[..., :-2]
    second = right - 2.0 * middle + left
    first = 0.5 * (right - left)
    beta = curvature[:, :, None]
    delta = walk_off[:, :, None]
    real = middle[0] - beta * second[1] + delta * first[0]
    imag = middle[1] + beta * second[0] + delta * first[1]
    moved = jnp.stack([real, imag])
    moved_low = moved.astype(jnp.bfloat16).reshape(2, local_orders, nblocks, block, steps_dev)
    tables = jnp.take(radial_tables, order_map, axis=0)
    scaled = radial_tables.astype(jnp.float32) * weights.reshape(nblocks, block)[None, :, :, None]
    analysis = jnp.take(scaled.astype(jnp.bfloat16), order_map, axis=0)
    points = jnp.einsum("mbqn,cmbnt->cmbqt", tables, moved_low, preferred_element_type=jnp.float32)
    points = points.reshape(2, local_orders, radial, steps_dev).astype(jnp.bfloat16)
    forward, backward = (jnp.asarray(table) for table in angle_matrices(ORDERS))
    back = local_kerr(
        lax.all_to_all(points, "ang", split_axis=2, concat_axis=1, tiled=True), forward, backward
    )
    returned = lax.all_to_all(back, "ang", split_axis=1, concat_axis=2, tiled=True)
    returned = returned.reshape(2, local_orders, nblocks, block, steps_dev)
    increment = jnp.einsum(
        "mbqn,cmbqt->cmbnt", analysis, returned, preferred_element_type=jnp.float32
    )
    increment = increment.reshape(2, local_orders, radial, steps_dev)
    return (moved + increment).astype(jnp.bfloat16)


def per_device(field, radial_tables, weights, order_map, curvature, walk_off):
    parts, orders, radial, steps = field.shape
    nblocks, block = radial_tables.shape[1:3]
    count = lax.axis_size("ang")
    fits = (
        steps == LANES
        and orders % ROWS == 0
        and 2 * orders <= LANES
        and block % (8 * count) == 0
        and radial % LANES == 0
        and LANES % block == 0
        and nblocks >= 2
    )
    plan = pipelined if fits else whole_arrays
    return plan(field, radial_tables, weights, order_map, curvature, walk_off)


def solution(mesh):
    in_specs = (P("groups", "ang", None, "tm"), P(), P(), P("ang"), P("ang", None), P("ang", None))
    out_specs = P("groups", "ang", None, "tm")
    return jax.shard_map(
        per_device, mesh=mesh, in_specs=in_specs, out_specs=out_specs, check_vma=False
    )
```

```python
import functools
import math

import jax
import jax.numpy as jnp
import numpy as np
from jax import lax
from jax.experimental import pallas as pl
from jax.experimental.pallas import tpu as pltpu
from jax.sharding import PartitionSpec as P

ORDERS = 256
LANES = 128
ROWS = 16
STRIDE = ROWS + 1
TEAM = 4

kerr_gamma = 0.00390625


def angle_matrices(count):
    index = np.arange(count, dtype=np.int32)
    phase = (index[:, None] * index[None, :] % count).astype(np.float32) * np.float32(
        2.0 * math.pi / count
    )
    cosine, sine = np.cos(phase), np.sin(phase)
    forward = np.block([[cosine, -sine], [sine, cosine]])
    backward = np.block([[cosine, sine], [-sine, cosine]])
    return forward.astype(jnp.bfloat16), backward.astype(jnp.bfloat16)


def ring(axis, shift):
    count = lax.axis_size(axis)
    return [(i, (i + shift) % count) for i in range(count)]


def lane_index(rows):
    return lax.broadcasted_iota(jnp.int32, (rows, LANES), 1)


def roll(x, shift):
    return pltpu.roll(x, shift, 1)


def params():
    return pltpu.CompilerParams(vmem_limit_bytes=40 * 1024 * 1024)


def cost(flops, size):
    return pl.CostEstimate(flops=flops, bytes_accessed=size, transcendentals=0)


def anywhere(count):
    return [pl.BlockSpec(memory_space=pl.ANY)] * count


def token():
    return jax.ShapeDtypeStruct((8, LANES), jnp.float32)


def edges(field, first, count, block, span, after):
    parts = field.shape[0]
    base, groups = span[0] // ROWS, span[1] // ROWS

    def kernel(x_ref, *refs):
        o_ref, _, acc = refs[-3:]
        g = pl.program_id(1)
        slot = ((lane_index(block) + 1) >> 1) & (LANES // 2 - 1)
        for c in range(parts):
            kept = jnp.zeros((block, LANES), jnp.float32)
            for i in range(ROWS):
                row = roll(x_ref[c, i].astype(jnp.float32), 2 * i)
                kept = jnp.where(slot == i, row, kept)
            kept = roll(kept, 2 * ROWS * (g + base))
            acc[c] = jnp.where(slot // ROWS == g + base, kept, acc[c])

        @pl.when(g == groups - 1)
        def _():
            o_ref[...] = acc[...].astype(o_ref.dtype)

    return pl.pallas_call(
        kernel,
        out_shape=[
            jax.ShapeDtypeStruct((parts, count * block, LANES), field.dtype),
            token(),
        ],
        grid=(count, groups),
        in_specs=[
            pl.BlockSpec((parts, ROWS, block, LANES), lambda j, g: (0, g + base, j + first, 0))
        ]
        + anywhere(len(after)),
        out_specs=[pl.BlockSpec((parts, block, LANES), lambda j, g: (0, j, 0))] + anywhere(1),
        scratch_shapes=[pltpu.VMEM((parts, block, LANES), jnp.float32)],
        compiler_params=params(),
        cost_estimate=cost(0, parts * span[1] * count * block * LANES * 2),
        name="edges",
    )(field, *after)


def join_halo(low, high):
    lane = lane_index(low.shape[0])
    low, high = low.astype(jnp.float32), high.astype(jnp.float32)
    return jnp.where((lane & 1) == 0, roll(low, 1), roll(high, LANES - 1))


def columns(ref, start, block):
    base = start // LANES * LANES
    turned = jnp.transpose(ref[:, base : base + LANES])
    return turned[start - base : start - base + block]


def move(x, halo, beta, delta, m):
    lane = lane_index(beta.shape[0])
    second, first = [], []
    for c in range(2):
        ends = roll(halo[c], (LANES - 2 * m) % LANES)
        left = jnp.where(lane == 0, ends, roll(x[c], 1))
        right = jnp.where(lane == LANES - 1, ends, roll(x[c], LANES - 1))
        second.append(right - 2.0 * x[c] + left)
        first.append(0.5 * (right - left))
    real = x[0] - beta * second[1] + delta * first[0]
    imag = x[1] + beta * second[0] + delta * first[1]
    return real, imag


def team_scratch(block):
    size = TEAM * block
    return [
        pltpu.VMEM((ROWS // TEAM, size, size), jnp.bfloat16),
        pltpu.VMEM((ROWS // TEAM, size, 2 * LANES), jnp.bfloat16),
    ]


def team_product(diagonal, stacked, team, tables, operands):
    block = tables[0].shape[0]
    for k in range(TEAM):
        rows = slice(k * block, (k + 1) * block)
        diagonal[team, rows, rows] = tables[k]
        stacked[team, rows, :] = operands[k]
    product = jnp.dot(diagonal[team], stacked[team], preferred_element_type=jnp.float32)
    return [product[k * block : (k + 1) * block] for k in range(TEAM)]


def radial_specs(parts, kinds, block, radial, b, halo_at, base):
    return [
        pl.BlockSpec((parts, ROWS, block, LANES), lambda g, *_: (0, g + base, b, 0)),
        pl.BlockSpec((parts, block, LANES), lambda g, *_: (0, halo_at, 0)),
        pl.BlockSpec((parts, block, LANES), lambda g, *_: (0, halo_at, 0)),
        pl.BlockSpec((kinds, 1, block, block), lambda g, *_: (0, b, 0, 0)),
        pl.BlockSpec((ROWS, radial), lambda g, *_: (g + base, 0)),
        pl.BlockSpec((ROWS, radial), lambda g, *_: (g + base, 0)),
    ]


def synthesize(field, halo, tables, curvature, walk_off, order_map, me, b, count, span, after):
    low, high, halo_at = halo
    parts, _, radial, _ = field.shape
    kinds, _, block, _ = tables.shape
    share = block // count
    base, groups = span[0] // ROWS, span[1] // ROWS

    def kernel(map_ref, me_ref, x_ref, low_ref, high_ref, tab_ref, beta_ref, delta_ref, *refs):
        outs, (acc, diagonal, stacked) = refs[len(after) : len(after) + count], refs[-3:]
        g = pl.program_id(0)

        @pl.when(g == 0)
        def _():
            diagonal[...] = jnp.zeros_like(diagonal)

        beta = columns(beta_ref, b * block, block)
        delta = columns(delta_ref, b * block, block)
        shift = (LANES - 2 * ROWS * (g + base)) & (LANES - 1)
        ends = [roll(join_halo(low_ref[c], high_ref[c]), shift) for c in range(parts)]
        for team in range(ROWS // TEAM):
            members = range(team * TEAM, (team + 1) * TEAM)
            tables, operands = [], []
            for i in members:
                x = [x_ref[c, i].astype(jnp.float32) for c in range(parts)]
                moved = move(x, ends, beta[:, i : i + 1], delta[:, i : i + 1], i)
                operands.append(jnp.concatenate(moved, 1).astype(jnp.bfloat16))
                tables.append(tab_ref[map_ref[(g + base) * ROWS + i], 0])
            products = team_product(diagonal, stacked, team, tables, operands)
            for i, points in zip(members, products, strict=True):
                for c in range(parts):
                    acc[c, pl.ds(i, block, stride=STRIDE), :] = points[
                        :, c * LANES : (c + 1) * LANES
                    ]
        for s in range(count):
            owner = lax.rem(me_ref[0] + s, count)
            start = pl.multiple_of(owner * share * STRIDE, 8)
            for c in range(parts):
                part = acc.at[c, pl.ds(start, share * STRIDE), :]
                for q in range(share):
                    row = q * STRIDE
                    outs[s][q, c] = part[row : row + ROWS, :].astype(jnp.bfloat16)

    piece = jax.ShapeDtypeStruct((share, parts, span[1], LANES), jnp.bfloat16)
    size = parts * span[1] * block * LANES * 2
    *pieces, done = pl.pallas_call(
        kernel,
        out_shape=[piece] * count + [token()],
        grid_spec=pltpu.PrefetchScalarGridSpec(
            num_scalar_prefetch=2,
            grid=(groups,),
            in_specs=radial_specs(parts, kinds, block, radial, b, halo_at, base)
            + anywhere(len(after)),
            out_specs=[
                pl.BlockSpec((share, parts, ROWS, LANES), lambda g, *_: (0, 0, g, 0))
            ]
            * count
            + anywhere(1),
            scratch_shapes=[pltpu.VMEM((parts, (block + 8) * STRIDE, LANES), jnp.float32)]
            + team_scratch(block),
        ),
        compiler_params=params(),
        cost_estimate=cost(2 * size * block, 2 * size),
        name="synthesize",
    )(order_map, me, field, low, high, tables, curvature, walk_off, *after)
    return pieces, done


def kerr_step(pieces, spans, out_spans, forward, backward, me, after):
    count = len(pieces[0])
    share, parts = pieces[0][0].shape[:2]
    orders = sum(size for _, size in spans)
    every = count * orders
    width = 2
    ins_count, outs_count = count * len(spans), count * len(out_spans)

    def kernel(me_ref, f_ref, b_ref, *refs):
        ins = refs[:ins_count]
        outs = refs[ins_count + len(after) : ins_count + len(after) + outs_count]
        flat, back = refs[-2:]
        for k, (start, size) in enumerate(spans):
            for s in range(count):
                source = lax.rem(me_ref[0] + count - s, count)
                for c in range(parts):
                    row = pl.multiple_of(c * every + source * orders + start, ROWS)
                    for q in range(width):
                        flat[pl.ds(row, size), q * LANES : (q + 1) * LANES] = ins[
                            k * count + s
                        ][q, c]
        angular = jnp.dot(f_ref[...], flat[...], preferred_element_type=jnp.float32)
        real, imag = angular[:every], angular[every:]
        power = kerr_gamma * (real * real + imag * imag)
        kerr = jnp.concatenate([-power * imag, power * real], 0).astype(jnp.bfloat16)
        back[...] = (
            jnp.dot(b_ref[...], kerr, preferred_element_type=jnp.float32) * (1.0 / every)
        ).astype(jnp.bfloat16)
        for k, (start, size) in enumerate(out_spans):
            for s in range(count):
                owner = lax.rem(me_ref[0] + s, count)
                for c in range(parts):
                    row = pl.multiple_of(c * every + owner * orders + start, ROWS)
                    for q in range(width):
                        outs[k * count + s][q, c] = back[
                            pl.ds(row, size), q * LANES : (q + 1) * LANES
                        ]

    def blocks(some):
        return [
            pl.BlockSpec((width, parts, size, LANES), lambda q, *_: (q, 0, 0, 0))
            for _, size in some
            for _ in range(count)
        ]

    whole = pl.BlockSpec((parts * every, parts * every), lambda q, *_: (0, 0))
    lanes = share * LANES
    *back, done = pl.pallas_call(
        kernel,
        out_shape=[
            jax.ShapeDtypeStruct((share, parts, size, LANES), jnp.bfloat16)
            for _, size in out_spans
            for _ in range(count)
        ]
        + [token()],
        grid_spec=pltpu.PrefetchScalarGridSpec(
            num_scalar_prefetch=1,
            grid=(share // width,),
            in_specs=[whole, whole] + blocks(spans) + anywhere(len(after)),
            out_specs=blocks(out_spans) + anywhere(1),
            scratch_shapes=[
                pltpu.VMEM((parts * every, width * LANES), jnp.bfloat16),
                pltpu.VMEM((parts * every, width * LANES), jnp.bfloat16),
            ],
        ),
        compiler_params=params(),
        cost_estimate=cost(4 * (parts * every) ** 2 * lanes, 4 * parts * every * lanes),
        name="kerr",
    )(me, forward, backward, *(piece for group in pieces for piece in group), *after)
    return [back[k * count : (k + 1) * count] for k in range(len(out_spans))], done


def analyze(
    pieces, field, halo, tables, curvature, walk_off, order_map, me, b, span, out, after
):
    low, high, halo_at = halo
    count = len(pieces)
    parts, _, radial, _ = field.shape
    kinds, _, block, _ = tables.shape
    share = block // count
    base, groups = span[0] // ROWS, span[1] // ROWS
    held = () if out is None else (out,)

    def kernel(map_ref, me_ref, *refs):
        ins = refs[:count]
        x_ref, low_ref, high_ref, tab_ref, beta_ref, delta_ref = refs[count : count + 6]
        o_ref, _, acc, diagonal, stacked = refs[-5:]
        g = pl.program_id(0)

        @pl.when(g == 0)
        def _():
            diagonal[...] = jnp.zeros_like(diagonal)

        for s in range(count):
            source = lax.rem(me_ref[0] + count - s, count)
            start = pl.multiple_of(source * share * STRIDE, 8)
            for c in range(parts):
                part = acc.at[c, pl.ds(start, share * STRIDE), :]
                for q in range(share):
                    row = q * STRIDE
                    part[row : row + ROWS, :] = ins[s][q, c].astype(jnp.float32)
        beta = columns(beta_ref, b * block, block)
        delta = columns(delta_ref, b * block, block)
        shift = (LANES - 2 * ROWS * (g + base)) & (LANES - 1)
        ends = [roll(join_halo(low_ref[c], high_ref[c]), shift) for c in range(parts)]
        for team in range(ROWS // TEAM):
            members = range(team * TEAM, (team + 1) * TEAM)
            tables, operands = [], []
            for i in members:
                back = [acc[c, pl.ds(i, block, stride=STRIDE), :] for c in range(parts)]
                operands.append(jnp.concatenate(back, 1).astype(jnp.bfloat16))
                tables.append(tab_ref[map_ref[(g + base) * ROWS + i], 0])
            products = team_product(diagonal, stacked, team, tables, operands)
            for i, increment in zip(members, products, strict=True):
                x = [x_ref[c, i].astype(jnp.float32) for c in range(parts)]
                moved = move(x, ends, beta[:, i : i + 1], delta[:, i : i + 1], i)
                for c in range(parts):
                    total = moved[c] + increment[:, c * LANES : (c + 1) * LANES]
                    o_ref[c, i] = total.astype(jnp.bfloat16)

    size = parts * span[1] * block * LANES * 2
    return pl.pallas_call(
        kernel,
        out_shape=[jax.ShapeDtypeStruct(field.shape, field.dtype), token()],
        grid_spec=pltpu.PrefetchScalarGridSpec(
            num_scalar_prefetch=2,
            grid=(groups,),
            in_specs=[
                pl.BlockSpec((share, parts, ROWS, LANES), lambda g, *_: (0, 0, g, 0))
            ]
            * count
            + radial_specs(parts, kinds, block, radial, b, halo_at, base)
            + anywhere(len(held) + len(after)),
            out_specs=[
                pl.BlockSpec((parts, ROWS, block, LANES), lambda g, *_: (0, g + base, b, 0))
            ]
            + anywhere(1),
            scratch_shapes=[pltpu.VMEM((parts, (block + 8) * STRIDE, LANES), jnp.float32)]
            + team_scratch(block),
        ),
        input_output_aliases={2 + count + 6: 0} if held else {},
        compiler_params=params(),
        cost_estimate=cost(2 * size * block, 3 * size),
        name="analyze",
    )(
        order_map, me, *pieces, field, low, high, tables, curvature, walk_off, *held, *after
    )


def exchange(pieces):
    return [pieces[0]] + [
        lax.ppermute(pieces[s], "ang", ring("ang", s)) for s in range(1, len(pieces))
    ]


def spans_of(sizes):
    starts = [sum(sizes[:k]) for k in range(len(sizes))]
    return list(zip(starts, sizes, strict=True))


def pipelined(field, radial_tables, weights, order_map, curvature, walk_off):
    count = lax.axis_size("ang")
    orders = field.shape[1]
    nblocks, block = radial_tables.shape[1:3]
    me = lax.axis_index("ang").astype(jnp.int32).reshape(1)
    forward, backward = (jnp.asarray(table) for table in angle_matrices(ORDERS))
    scaled = radial_tables.astype(jnp.float32) * weights.reshape(nblocks, block)[None, :, :, None]
    analysis = scaled.astype(jnp.bfloat16).transpose(0, 1, 3, 2)
    whole = spans_of([orders])
    tail = spans_of([orders - ROWS, ROWS]) if orders > ROWS else whole
    spans = {}
    out_spans = {nblocks - 1: tail}
    after = ()
    halos, sent, returned = {}, {}, {}
    out = None

    def halo(first, some, span, after):
        ends, done = edges(field, first, some, block, span, after)
        low = lax.ppermute(ends, "tm", ring("tm", 1))
        high = lax.ppermute(ends, "tm", ring("tm", -1))
        return [(low, high, j) for j in range(some)], (done,)

    def points(b, span, ends, after):
        own, done = synthesize(
            field, ends, radial_tables, curvature, walk_off, order_map, me, b, count, span, after
        )
        sent.setdefault(b, []).append(exchange(own))
        return (done,)

    def turn(b, after):
        back, done = kerr_step(
            sent.pop(b), spans.get(b, whole), out_spans.get(b, whole), forward, backward, me, after
        )
        returned[b] = [exchange(group) for group in back]
        return (done,)

    def finish(b, out, after):
        for span, group in zip(out_spans.get(b, whole), returned.pop(b), strict=True):
            out, done = analyze(
                group, field, halos[b], analysis, curvature, walk_off, order_map, me, b, span,
                out, after,
            )
            after = (done,)
        return out, after

    (halos[0],), after = halo(0, 1, whole[0], after)
    after = points(0, whole[0], halos[0], after)
    (halos[1],), after = halo(1, 1, whole[0], after)
    after = points(1, whole[0], halos[1], after)
    if nblocks > 2:
        rest, after = halo(2, nblocks - 2, whole[0], after)
        halos.update(zip(range(2, nblocks), rest, strict=True))
    for b in range(nblocks):
        if b >= nblocks - 1:
            after = after + tuple(returned[b - 1][0][1:2])
        after = turn(b, after)
        if b >= 1:
            out, after = finish(b - 1, out, after)
        if b + 2 < nblocks:
            after = points(b + 2, whole[0], halos[b + 2], after)
    out, after = finish(nblocks - 1, out, after)
    return out


def with_halo(block, axis, dim):
    low = lax.ppermute(
        lax.slice_in_dim(block, block.shape[dim] - 1, None, axis=dim), axis, ring(axis, 1)
    )
    high = lax.ppermute(lax.slice_in_dim(block, 0, 1, axis=dim), axis, ring(axis, -1))
    return jnp.concatenate([low, block, high], axis=dim)


def local_kerr(pieces, forward, backward):
    orders = pieces.shape[1]
    flat = pieces.reshape(2 * orders, -1)
    angular = jnp.dot(forward, flat, preferred_element_type=jnp.float32)
    power = angular[:orders] ** 2 + angular[orders:] ** 2
    kerr = jnp.concatenate(
        [-kerr_gamma * power * angular[orders:], kerr_gamma * power * angular[:orders]], 0
    )
    kerr = kerr.astype(jnp.bfloat16)
    back = jnp.dot(backward, kerr, preferred_element_type=jnp.float32) * (1.0 / orders)
    return back.astype(jnp.bfloat16).reshape(pieces.shape)


def whole_arrays(field, radial_tables, weights, order_map, curvature, walk_off):
    local_orders, radial, steps_dev = field.shape[1:]
    nblocks, block = radial_tables.shape[1:3]
    padded = with_halo(field, "tm", 3).astype(jnp.float32)
    middle = padded[..., 1:-1]
    right = padded[..., 2:]
    left = padded[..., :-2]
    second = right - 2.0 * middle + left
    first = 0.5 * (right - left)
    beta = curvature[:, :, None]
    delta = walk_off[:, :, None]
    real = middle[0] - beta * second[1] + delta * first[0]
    imag = middle[1] + beta * second[0] + delta * first[1]
    moved = jnp.stack([real, imag])
    moved_low = moved.astype(jnp.bfloat16).reshape(2, local_orders, nblocks, block, steps_dev)
    tables = jnp.take(radial_tables, order_map, axis=0)
    scaled = radial_tables.astype(jnp.float32) * weights.reshape(nblocks, block)[None, :, :, None]
    analysis = jnp.take(scaled.astype(jnp.bfloat16), order_map, axis=0)
    points = jnp.einsum("mbqn,cmbnt->cmbqt", tables, moved_low, preferred_element_type=jnp.float32)
    points = points.reshape(2, local_orders, radial, steps_dev).astype(jnp.bfloat16)
    forward, backward = (jnp.asarray(table) for table in angle_matrices(ORDERS))
    back = local_kerr(
        lax.all_to_all(points, "ang", split_axis=2, concat_axis=1, tiled=True), forward, backward
    )
    returned = lax.all_to_all(back, "ang", split_axis=1, concat_axis=2, tiled=True)
    returned = returned.reshape(2, local_orders, nblocks, block, steps_dev)
    increment = jnp.einsum(
        "mbqn,cmbqt->cmbnt", analysis, returned, preferred_element_type=jnp.float32
    )
    increment = increment.reshape(2, local_orders, radial, steps_dev)
    return (moved + increment).astype(jnp.bfloat16)


def per_device(field, radial_tables, weights, order_map, curvature, walk_off):
    parts, orders, radial, steps = field.shape
    nblocks, block = radial_tables.shape[1:3]
    count = lax.axis_size("ang")
    fits = (
        steps == LANES
        and orders % ROWS == 0
        and 2 * orders <= LANES
        and block % (8 * count) == 0
        and radial % LANES == 0
        and LANES % block == 0
        and nblocks >= 2
    )
    plan = pipelined if fits else whole_arrays
    return plan(field, radial_tables, weights, order_map, curvature, walk_off)


def solution(mesh):
    in_specs = (P("groups", "ang", None, "tm"), P(), P(), P("ang"), P("ang", None), P("ang", None))
    out_specs = P("groups", "ang", None, "tm")
    return jax.shard_map(
        per_device, mesh=mesh, in_specs=in_specs, out_specs=out_specs, check_vma=False
    )
```

```python
import functools
import math

import jax
import jax.numpy as jnp
import numpy as np
from jax import lax
from jax.experimental import pallas as pl
from jax.experimental.pallas import tpu as pltpu
from jax.sharding import PartitionSpec as P

ORDERS = 256
LANES = 128
ROWS = 16
STRIDE = ROWS + 1

kerr_gamma = 0.00390625


def angle_matrices(count):
    index = np.arange(count, dtype=np.int32)
    phase = (index[:, None] * index[None, :] % count).astype(np.float32) * np.float32(
        2.0 * math.pi / count
    )
    cosine, sine = np.cos(phase), np.sin(phase)
    forward = np.block([[cosine, -sine], [sine, cosine]])
    backward = np.block([[cosine, sine], [-sine, cosine]])
    return forward.astype(jnp.bfloat16), backward.astype(jnp.bfloat16)


def ring(axis, shift):
    count = lax.axis_size(axis)
    return [(i, (i + shift) % count) for i in range(count)]


def lane_index(rows):
    return lax.broadcasted_iota(jnp.int32, (rows, LANES), 1)


def roll(x, shift):
    return pltpu.roll(x, shift, 1)


def params():
    return pltpu.CompilerParams(vmem_limit_bytes=40 * 1024 * 1024)


def cost(flops, size):
    return pl.CostEstimate(flops=flops, bytes_accessed=size, transcendentals=0)


def anywhere(count):
    return [pl.BlockSpec(memory_space=pl.ANY)] * count


def token():
    return jax.ShapeDtypeStruct((8, LANES), jnp.float32)


def edges(field, first, count, block, span, after):
    parts = field.shape[0]
    some = 2 * ROWS if span[0] % (2 * ROWS) == 0 and span[1] % (2 * ROWS) == 0 else ROWS
    base, groups = span[0] // some, span[1] // some

    def kernel(x_ref, *refs):
        o_ref, _, acc = refs[-3:]
        g = pl.program_id(1)
        slot = ((lane_index(block) + 1) >> 1) & (LANES // 2 - 1)
        for c in range(parts):
            kept = acc[c]
            for i in range(some):
                m = (g + base) * some + i
                row = roll(x_ref[c, i].astype(jnp.float32), 2 * m)
                kept = jnp.where(slot == m, row, kept)
            acc[c] = kept

        @pl.when(g == groups - 1)
        def _():
            o_ref[...] = acc[...].astype(o_ref.dtype)

    return pl.pallas_call(
        kernel,
        out_shape=[
            jax.ShapeDtypeStruct((parts, count * block, LANES), field.dtype),
            token(),
        ],
        grid=(count, groups),
        in_specs=[
            pl.BlockSpec((parts, some, block, LANES), lambda j, g: (0, g + base, j + first, 0))
        ]
        + anywhere(len(after)),
        out_specs=[pl.BlockSpec((parts, block, LANES), lambda j, g: (0, j, 0))] + anywhere(1),
        scratch_shapes=[pltpu.VMEM((parts, block, LANES), jnp.float32)],
        compiler_params=params(),
        cost_estimate=cost(0, parts * span[1] * count * block * LANES * 2),
        name="edges",
    )(field, *after)


def join_halo(low, high):
    lane = lane_index(low.shape[0])
    low, high = low.astype(jnp.float32), high.astype(jnp.float32)
    return jnp.where((lane & 1) == 0, roll(low, 1), roll(high, LANES - 1))


def columns(ref, start, block):
    base = start // LANES * LANES
    turned = jnp.transpose(ref[:, base : base + LANES])
    return turned[start - base : start - base + block]


def move(x, halo, beta, delta, m):
    lane = lane_index(beta.shape[0])
    second, first = [], []
    for c in range(2):
        ends = roll(halo[c], (LANES - 2 * m) & (LANES - 1))
        left = jnp.where(lane == 0, ends, roll(x[c], 1))
        right = jnp.where(lane == LANES - 1, ends, roll(x[c], LANES - 1))
        second.append(right - 2.0 * x[c] + left)
        first.append(0.5 * (right - left))
    real = x[0] - beta * second[1] + delta * first[0]
    imag = x[1] + beta * second[0] + delta * first[1]
    return real, imag


def radial_specs(parts, kinds, block, radial, b, halo_at, base):
    return [
        pl.BlockSpec((parts, ROWS, block, LANES), lambda g, *_: (0, g + base, b, 0)),
        pl.BlockSpec((parts, block, LANES), lambda g, *_: (0, halo_at, 0)),
        pl.BlockSpec((parts, block, LANES), lambda g, *_: (0, halo_at, 0)),
        pl.BlockSpec((kinds, 1, block, block), lambda g, *_: (0, b, 0, 0)),
        pl.BlockSpec((ROWS, radial), lambda g, *_: (g + base, 0)),
        pl.BlockSpec((ROWS, radial), lambda g, *_: (g + base, 0)),
    ]


def synthesize(field, halo, tables, curvature, walk_off, order_map, me, b, count, span, after):
    low, high, halo_at = halo
    parts, _, radial, _ = field.shape
    kinds, _, block, _ = tables.shape
    share = block // count
    base, groups = span[0] // ROWS, span[1] // ROWS

    def kernel(map_ref, me_ref, x_ref, low_ref, high_ref, tab_ref, beta_ref, delta_ref, *refs):
        outs, acc = refs[len(after) : len(after) + count], refs[-1]
        g = pl.program_id(0)
        beta = columns(beta_ref, b * block, block)
        delta = columns(delta_ref, b * block, block)
        ends = [join_halo(low_ref[c], high_ref[c]) for c in range(parts)]
        for i in range(ROWS):
            m = (g + base) * ROWS + i
            x = [x_ref[c, i].astype(jnp.float32) for c in range(parts)]
            moved = move(x, ends, beta[:, i : i + 1], delta[:, i : i + 1], m)
            moved = jnp.concatenate(moved, 1).astype(jnp.bfloat16)
            points = jnp.dot(
                tab_ref[map_ref[m], 0], moved, preferred_element_type=jnp.float32
            )
            for c in range(parts):
                acc[c, pl.ds(i, block, stride=STRIDE), :] = points[:, c * LANES : (c + 1) * LANES]
        for s in range(count):
            owner = lax.rem(me_ref[0] + s, count)
            start = pl.multiple_of(owner * share * STRIDE, 8)
            for c in range(parts):
                part = acc.at[c, pl.ds(start, share * STRIDE), :]
                for q in range(share):
                    row = q * STRIDE
                    outs[s][q, c] = part[row : row + ROWS, :].astype(jnp.bfloat16)

    piece = jax.ShapeDtypeStruct((share, parts, span[1], LANES), jnp.bfloat16)
    size = parts * span[1] * block * LANES * 2
    *pieces, done = pl.pallas_call(
        kernel,
        out_shape=[piece] * count + [token()],
        grid_spec=pltpu.PrefetchScalarGridSpec(
            num_scalar_prefetch=2,
            grid=(groups,),
            in_specs=radial_specs(parts, kinds, block, radial, b, halo_at, base)
            + anywhere(len(after)),
            out_specs=[
                pl.BlockSpec((share, parts, ROWS, LANES), lambda g, *_: (0, 0, g, 0))
            ]
            * count
            + anywhere(1),
            scratch_shapes=[pltpu.VMEM((parts, (block + 8) * STRIDE, LANES), jnp.float32)],
        ),
        compiler_params=params(),
        cost_estimate=cost(2 * size * block, 2 * size),
        name="synthesize",
    )(order_map, me, field, low, high, tables, curvature, walk_off, *after)
    return pieces, done


def kerr_step(pieces, spans, out_spans, forward, backward, me, after):
    count = len(pieces[0])
    share, parts = pieces[0][0].shape[:2]
    orders = sum(size for _, size in spans)
    every = count * orders
    width = 2
    ins_count, outs_count = count * len(spans), count * len(out_spans)

    def kernel(me_ref, f_ref, b_ref, *refs):
        ins = refs[:ins_count]
        outs = refs[ins_count + len(after) : ins_count + len(after) + outs_count]
        flat, back = refs[-2:]
        for k, (start, size) in enumerate(spans):
            for s in range(count):
                source = lax.rem(me_ref[0] + count - s, count)
                for c in range(parts):
                    row = pl.multiple_of(c * every + source * orders + start, ROWS)
                    for q in range(width):
                        flat[pl.ds(row, size), q * LANES : (q + 1) * LANES] = ins[
                            k * count + s
                        ][q, c]
        angular = jnp.dot(f_ref[...], flat[...], preferred_element_type=jnp.float32)
        real, imag = angular[:every], angular[every:]
        power = kerr_gamma * (real * real + imag * imag)
        kerr = jnp.concatenate([-power * imag, power * real], 0).astype(jnp.bfloat16)
        back[...] = (
            jnp.dot(b_ref[...], kerr, preferred_element_type=jnp.float32) * (1.0 / every)
        ).astype(jnp.bfloat16)
        for k, (start, size) in enumerate(out_spans):
            for s in range(count):
                owner = lax.rem(me_ref[0] + s, count)
                for c in range(parts):
                    row = pl.multiple_of(c * every + owner * orders + start, ROWS)
                    for q in range(width):
                        outs[k * count + s][q, c] = back[
                            pl.ds(row, size), q * LANES : (q + 1) * LANES
                        ]

    def blocks(some):
        return [
            pl.BlockSpec((width, parts, size, LANES), lambda q, *_: (q, 0, 0, 0))
            for _, size in some
            for _ in range(count)
        ]

    whole = pl.BlockSpec((parts * every, parts * every), lambda q, *_: (0, 0))
    lanes = share * LANES
    *back, done = pl.pallas_call(
        kernel,
        out_shape=[
            jax.ShapeDtypeStruct((share, parts, size, LANES), jnp.bfloat16)
            for _, size in out_spans
            for _ in range(count)
        ]
        + [token()],
        grid_spec=pltpu.PrefetchScalarGridSpec(
            num_scalar_prefetch=1,
            grid=(share // width,),
            in_specs=[whole, whole] + blocks(spans) + anywhere(len(after)),
            out_specs=blocks(out_spans) + anywhere(1),
            scratch_shapes=[
                pltpu.VMEM((parts * every, width * LANES), jnp.bfloat16),
                pltpu.VMEM((parts * every, width * LANES), jnp.bfloat16),
            ],
        ),
        compiler_params=params(),
        cost_estimate=cost(4 * (parts * every) ** 2 * lanes, 4 * parts * every * lanes),
        name="kerr",
    )(me, forward, backward, *(piece for group in pieces for piece in group), *after)
    return [back[k * count : (k + 1) * count] for k in range(len(out_spans))], done


def analyze(
    pieces, field, halo, tables, curvature, walk_off, order_map, me, b, span, out, after
):
    low, high, halo_at = halo
    count = len(pieces)
    parts, _, radial, _ = field.shape
    kinds, _, block, _ = tables.shape
    share = block // count
    base, groups = span[0] // ROWS, span[1] // ROWS
    held = () if out is None else (out,)

    def kernel(map_ref, me_ref, *refs):
        ins = refs[:count]
        x_ref, low_ref, high_ref, tab_ref, beta_ref, delta_ref = refs[count : count + 6]
        o_ref, _, acc = refs[-3:]
        g = pl.program_id(0)
        for s in range(count):
            source = lax.rem(me_ref[0] + count - s, count)
            start = pl.multiple_of(source * share * STRIDE, 8)
            for c in range(parts):
                part = acc.at[c, pl.ds(start, share * STRIDE), :]
                for q in range(share):
                    row = q * STRIDE
                    part[row : row + ROWS, :] = ins[s][q, c].astype(jnp.float32)
        beta = columns(beta_ref, b * block, block)
        delta = columns(delta_ref, b * block, block)
        ends = [join_halo(low_ref[c], high_ref[c]) for c in range(parts)]
        for i in range(ROWS):
            m = (g + base) * ROWS + i
            x = [x_ref[c, i].astype(jnp.float32) for c in range(parts)]
            moved = move(x, ends, beta[:, i : i + 1], delta[:, i : i + 1], m)
            back = [acc[c, pl.ds(i, block, stride=STRIDE), :] for c in range(parts)]
            back = jnp.concatenate(back, 1).astype(jnp.bfloat16)
            increment = jnp.dot(
                tab_ref[map_ref[m], 0], back, preferred_element_type=jnp.float32
            )
            for c in range(parts):
                total = moved[c] + increment[:, c * LANES : (c + 1) * LANES]
                o_ref[c, i] = total.astype(jnp.bfloat16)

    size = parts * span[1] * block * LANES * 2
    return pl.pallas_call(
        kernel,
        out_shape=[jax.ShapeDtypeStruct(field.shape, field.dtype), token()],
        grid_spec=pltpu.PrefetchScalarGridSpec(
            num_scalar_prefetch=2,
            grid=(groups,),
            in_specs=[
                pl.BlockSpec((share, parts, ROWS, LANES), lambda g, *_: (0, 0, g, 0))
            ]
            * count
            + radial_specs(parts, kinds, block, radial, b, halo_at, base)
            + anywhere(len(held) + len(after)),
            out_specs=[
                pl.BlockSpec((parts, ROWS, block, LANES), lambda g, *_: (0, g + base, b, 0))
            ]
            + anywhere(1),
            scratch_shapes=[pltpu.VMEM((parts, (block + 8) * STRIDE, LANES), jnp.float32)],
        ),
        input_output_aliases={2 + count + 6: 0} if held else {},
        compiler_params=params(),
        cost_estimate=cost(2 * size * block, 3 * size),
        name="analyze",
    )(
        order_map, me, *pieces, field, low, high, tables, curvature, walk_off, *held, *after
    )


def exchange(pieces):
    return [pieces[0]] + [
        lax.ppermute(pieces[s], "ang", ring("ang", s)) for s in range(1, len(pieces))
    ]


def spans_of(sizes):
    starts = [sum(sizes[:k]) for k in range(len(sizes))]
    return list(zip(starts, sizes, strict=True))


def pipelined(field, radial_tables, weights, order_map, curvature, walk_off):
    count = lax.axis_size("ang")
    orders = field.shape[1]
    nblocks, block = radial_tables.shape[1:3]
    me = lax.axis_index("ang").astype(jnp.int32).reshape(1)
    forward, backward = (jnp.asarray(table) for table in angle_matrices(ORDERS))
    scaled = radial_tables.astype(jnp.float32) * weights.reshape(nblocks, block)[None, :, :, None]
    analysis = scaled.astype(jnp.bfloat16).transpose(0, 1, 3, 2)
    whole = spans_of([orders])
    tail = spans_of([orders - ROWS, ROWS]) if orders > ROWS else whole
    spans = {}
    out_spans = {nblocks - 1: tail}
    after = ()
    halos, sent, returned = {}, {}, {}
    out = None

    def halo(first, some, span, after):
        ends, done = edges(field, first, some, block, span, after)
        low = lax.ppermute(ends, "tm", ring("tm", 1))
        high = lax.ppermute(ends, "tm", ring("tm", -1))
        return [(low, high, j) for j in range(some)], (done,)

    def points(b, span, ends, after):
        own, done = synthesize(
            field, ends, radial_tables, curvature, walk_off, order_map, me, b, count, span, after
        )
        sent.setdefault(b, []).append(exchange(own))
        return (done,)

    def turn(b, after):
        back, done = kerr_step(
            sent.pop(b), spans.get(b, whole), out_spans.get(b, whole), forward, backward, me, after
        )
        returned[b] = [exchange(group) for group in back]
        return (done,)

    def finish(b, out, after):
        for span, group in zip(out_spans.get(b, whole), returned.pop(b), strict=True):
            out, done = analyze(
                group, field, halos[b], analysis, curvature, walk_off, order_map, me, b, span,
                out, after,
            )
            after = (done,)
        return out, after

    (halos[0],), after = halo(0, 1, whole[0], after)
    after = points(0, whole[0], halos[0], after)
    (halos[1],), after = halo(1, 1, whole[0], after)
    after = points(1, whole[0], halos[1], after)
    if nblocks > 2:
        rest, after = halo(2, nblocks - 2, whole[0], after)
        halos.update(zip(range(2, nblocks), rest, strict=True))
    for b in range(nblocks):
        if b >= nblocks - 1:
            after = after + tuple(returned[b - 1][0][1:2])
        after = turn(b, after)
        if b >= 1:
            out, after = finish(b - 1, out, after)
        if b + 2 < nblocks:
            after = points(b + 2, whole[0], halos[b + 2], after)
    out, after = finish(nblocks - 1, out, after)
    return out


def with_halo(block, axis, dim):
    low = lax.ppermute(
        lax.slice_in_dim(block, block.shape[dim] - 1, None, axis=dim), axis, ring(axis, 1)
    )
    high = lax.ppermute(lax.slice_in_dim(block, 0, 1, axis=dim), axis, ring(axis, -1))
    return jnp.concatenate([low, block, high], axis=dim)


def local_kerr(pieces, forward, backward):
    orders = pieces.shape[1]
    flat = pieces.reshape(2 * orders, -1)
    angular = jnp.dot(forward, flat, preferred_element_type=jnp.float32)
    power = angular[:orders] ** 2 + angular[orders:] ** 2
    kerr = jnp.concatenate(
        [-kerr_gamma * power * angular[orders:], kerr_gamma * power * angular[:orders]], 0
    )
    kerr = kerr.astype(jnp.bfloat16)
    back = jnp.dot(backward, kerr, preferred_element_type=jnp.float32) * (1.0 / orders)
    return back.astype(jnp.bfloat16).reshape(pieces.shape)


def whole_arrays(field, radial_tables, weights, order_map, curvature, walk_off):
    local_orders, radial, steps_dev = field.shape[1:]
    nblocks, block = radial_tables.shape[1:3]
    padded = with_halo(field, "tm", 3).astype(jnp.float32)
    middle = padded[..., 1:-1]
    right = padded[..., 2:]
    left = padded[..., :-2]
    second = right - 2.0 * middle + left
    first = 0.5 * (right - left)
    beta = curvature[:, :, None]
    delta = walk_off[:, :, None]
    real = middle[0] - beta * second[1] + delta * first[0]
    imag = middle[1] + beta * second[0] + delta * first[1]
    moved = jnp.stack([real, imag])
    moved_low = moved.astype(jnp.bfloat16).reshape(2, local_orders, nblocks, block, steps_dev)
    tables = jnp.take(radial_tables, order_map, axis=0)
    scaled = radial_tables.astype(jnp.float32) * weights.reshape(nblocks, block)[None, :, :, None]
    analysis = jnp.take(scaled.astype(jnp.bfloat16), order_map, axis=0)
    points = jnp.einsum("mbqn,cmbnt->cmbqt", tables, moved_low, preferred_element_type=jnp.float32)
    points = points.reshape(2, local_orders, radial, steps_dev).astype(jnp.bfloat16)
    forward, backward = (jnp.asarray(table) for table in angle_matrices(ORDERS))
    back = local_kerr(
        lax.all_to_all(points, "ang", split_axis=2, concat_axis=1, tiled=True), forward, backward
    )
    returned = lax.all_to_all(back, "ang", split_axis=1, concat_axis=2, tiled=True)
    returned = returned.reshape(2, local_orders, nblocks, block, steps_dev)
    increment = jnp.einsum(
        "mbqn,cmbqt->cmbnt", analysis, returned, preferred_element_type=jnp.float32
    )
    increment = increment.reshape(2, local_orders, radial, steps_dev)
    return (moved + increment).astype(jnp.bfloat16)


def per_device(field, radial_tables, weights, order_map, curvature, walk_off):
    parts, orders, radial, steps = field.shape
    nblocks, block = radial_tables.shape[1:3]
    count = lax.axis_size("ang")
    fits = (
        steps == LANES
        and orders % ROWS == 0
        and 2 * orders <= LANES
        and block % (8 * count) == 0
        and radial % LANES == 0
        and LANES % block == 0
        and nblocks >= 2
    )
    plan = pipelined if fits else whole_arrays
    return plan(field, radial_tables, weights, order_map, curvature, walk_off)


def solution(mesh):
    in_specs = (P("groups", "ang", None, "tm"), P(), P(), P("ang"), P("ang", None), P("ang", None))
    out_specs = P("groups", "ang", None, "tm")
    return jax.shard_map(
        per_device, mesh=mesh, in_specs=in_specs, out_specs=out_specs, check_vma=False
    )
```
